128 devices in a mesh: tower: 4 (over x_lo, core), dp: 32 (over z, x_hi, y).
Axes of the slice: x: 4 (x_hi: 2, x_lo: 2; x = x_hi * 2 + x_lo), y: 4, z: 4, core: 2. Of those that a mesh axis runs over, the one named last changes fastest.
Arguments:
- image_feats: bfloat16 [12288, 1664], P('dp'), may hold values from -80 to 80
- text_feats: bfloat16 [12288, 1024], P('dp'), may hold values from -80 to 80
- image_weight: bfloat16 [1664, 1024], replicated, may hold values from -0.15625 to 0.15625
- text_weight: bfloat16 [1024, 1024], replicated, may hold values from -0.1875 to 0.1875
- partner: int32 [12288], P('dp'), may hold values from 0 to 12287, each once
- log_scale: float32 [1], replicated, may hold values from 2.1 to 2.5
- logit_bias: float32 [1], replicated, may hold values from -10 to -8
Outputs:
- proj_grads: float32 [2688, 1024], P(('tower', 'dp'))
The draws below stay inside these ranges and needn't reach their ends.
All inputs are finite; a program needn't handle non-finite values.
Results may differ from the reference program's by a relative error of at most 0.00055.
The reference program's roundings to bfloat16 on the way count: a program that leaves them out, or rounds other values in their place, can miss the bound.
Values may be sent and summed in bfloat16 or wider, within the bound.
No kernel may reach another device: no remote copies, remote signals or barrier semaphores. Data moves between devices by JAX's collectives and lax.ppermute only.
A program may use at most 128 MiB of HBM per device.

```python
import math
import jax
import jax.numpy as jnp
from jax import lax

E = 1024
DI = 1664
DT = 1024
PAIRS = 12288
N_DP = 32


def spread_scales(key, count, columns):
    key_rows, key_cols = jax.random.split(key)
    row_scale = jnp.exp(jax.random.uniform(key_rows, (count, 1), jnp.float32) * math.log(10.0))
    col_scale = jnp.exp(jax.random.uniform(key_cols, (1, columns), jnp.float32) * math.log(10.0))
    return row_scale * col_scale / 5.0


def draw_image_feats(key, part):
    key = jax.random.fold_in(key, 11)
    key_scale, key_noise = jax.random.split(key, 2)
    scales = spread_scales(key_scale, PAIRS, DI)
    values = jnp.clip(jax.random.normal(key_noise, (PAIRS, DI), jnp.float32), -4.0, 4.0)
    return (values * scales).astype(jnp.bfloat16)


def draw_text_feats(key, part):
    key = jax.random.fold_in(key, 12)
    key_scale, key_noise = jax.random.split(key, 2)
    scales = spread_scales(key_scale, PAIRS, DT)
    values = jnp.clip(jax.random.normal(key_noise, (PAIRS, DT), jnp.float32), -4.0, 4.0)
    return (values * scales).astype(jnp.bfloat16)


def bell_draw(stream_key, shape, spread, limit, held_as=jnp.bfloat16):
    return jnp.clip(spread * jax.random.normal(stream_key, shape, jnp.float32), -limit, limit).astype(held_as)


def setup_inputs(seed: int = 0) -> dict:
    splits = jax.random.split(jax.random.key(seed), 8)
    return {
        "image_feats": draw_image_feats(jax.random.fold_in(splits[7], 71), 0),
        "text_feats": draw_text_feats(jax.random.fold_in(splits[7], 71), 0),
        "image_weight": bell_draw(splits[2], (DI, E), DI ** -0.5, 0.15625),
        "text_weight": bell_draw(splits[3], (DT, E), DT ** -0.5, 0.1875),
        "partner": jax.random.permutation(splits[4], PAIRS).astype(jnp.int32),
        "log_scale": jnp.clip(jax.random.uniform(splits[5], (1,), jnp.float32, 2.1, 2.5), 2.1, 2.5),
        "logit_bias": jnp.clip(jax.random.uniform(splits[6], (1,), jnp.float32, -10.0, -8.0), -10.0, -8.0),
    }


def embed_rows(features, weight):
    projected = jnp.dot(features, weight, preferred_element_type=jnp.float32)
    inverse = lax.rsqrt(lax.optimization_barrier(jnp.sum(projected * projected, axis=1)) + 1e-06).astype(jnp.bfloat16)
    widened = lax.optimization_barrier(inverse).astype(jnp.float32)
    return ((projected * widened[:, None]).astype(jnp.bfloat16), inverse)

def back_rows(embedded, inverse, gradients):
    widened = embedded.astype(jnp.float32)
    inner_sum = lax.optimization_barrier(jnp.sum(widened * gradients, axis=1, keepdims=True))
    return (inverse.astype(jnp.float32)[:, None] * (gradients - widened * inner_sum)).astype(jnp.bfloat16)

def weight_term(features, back_pre):
    return lax.dot_general(features, back_pre, (((0,), (0,)), ((), ())), preferred_element_type=jnp.float32)

def reference(image_feats, text_feats, image_weight, text_weight, partner, log_scale, logit_bias):
    images, image_inverse = embed_rows(image_feats, image_weight)
    texts, text_inverse = embed_rows(text_feats, text_weight)
    logit_scale = jnp.exp(log_scale[0])
    logit_shift = logit_bias[0]
    block_rows = PAIRS // N_DP
    columns = lax.iota(jnp.int32, PAIRS)

    def pair_block(text_sum, block_index):
        start_row = (block_index * block_rows).astype(jnp.int32)
        rows_here = lax.dynamic_slice_in_dim(images, start_row, block_rows, 0)
        partners_here = lax.dynamic_slice_in_dim(partner, start_row, block_rows, 0)
        logits = logit_scale * lax.dot_general(rows_here, texts, (((1,), (1,)), ((), ())), preferred_element_type=jnp.float32) + logit_shift
        labels = jnp.where(partners_here[:, None] == columns[None, :], 1.0, -1.0).astype(jnp.float32)
        slopes = -labels * jax.nn.sigmoid(-labels * logits)
        coefficient = (logit_scale * slopes).astype(jnp.bfloat16)
        image_grad = jnp.dot(coefficient, texts, preferred_element_type=jnp.float32)
        text_sum = text_sum + lax.dot_general(coefficient, rows_here, (((0,), (0,)), ((), ())), preferred_element_type=jnp.float32)
        return (text_sum, image_grad)
    text_grad, image_blocks = lax.scan(pair_block, jnp.zeros((PAIRS, E), jnp.float32), jnp.arange(N_DP, dtype=jnp.int32))
    image_grad = image_blocks.reshape(PAIRS, E)
    image_back = back_rows(images, image_inverse, image_grad)
    text_back = back_rows(texts, text_inverse, text_grad)
    return jnp.concatenate([weight_term(image_feats, image_back), weight_term(text_feats, text_back)], 0)
```

```python
import jax
import jax.numpy as jnp
from jax import lax
from jax.sharding import Mesh, PartitionSpec as P

AXES = ("xl", "core", "z", "xh", "y")
SIZES = {"xl": 2, "core": 2, "z": 4, "xh": 2, "y": 4}
DP = ("z", "xh", "y")
TOWER = ("xl", "core")
GROUP = 24


def shifted(array, axis, by):
    if axis == "x":
        number = [0, 2, 1, 3]
        return lax.ppermute(
            array, ("xl", "xh"), [(number[i], number[(i + by) % 4]) for i in range(4)]
        )
    return lax.ppermute(array, axis, [(i, (i + by) % 4) for i in range(4)])


def ring_gather(block, axis):
    half = block.shape[0] // 2
    before = shifted(block, axis, 1)
    after = shifted(block, axis, -1)
    far = jnp.concatenate(
        [shifted(before[:half], axis, 1), shifted(after[half:], axis, -1)], 0
    )
    return [block, after, before, far]


def ring_scatter(chunks, axis):
    mine, after, before, far = chunks
    half = mine.shape[0] // 2
    via_right = shifted(far[:half], axis, 1)
    via_left = shifted(far[half:], axis, -1)
    got_low = shifted(before[:half], axis, -1)
    got_high = shifted(after[half:], axis, 1)
    low = shifted(after[:half] + via_right, axis, 1)
    high = shifted(before[half:] + via_left, axis, -1)
    return jnp.concatenate(
        [mine[:half] + got_low + low, mine[half:] + got_high + high], 0
    )


def embed_rows(features, weight):
    projected = jnp.dot(features, weight, preferred_element_type=jnp.float32)
    inverse = lax.rsqrt(jnp.sum(projected * projected, axis=1) + 1e-06).astype(jnp.bfloat16)
    inverse = lax.optimization_barrier(inverse)
    embedded = (projected * inverse.astype(jnp.float32)[:, None]).astype(jnp.bfloat16)
    return (lax.optimization_barrier(embedded), inverse)


def back_rows(embedded, inverse, gradients):
    widened = embedded.astype(jnp.float32)
    inner_sum = jnp.sum(widened * gradients, axis=1, keepdims=True)
    return (inverse.astype(jnp.float32)[:, None] * (gradients - widened * inner_sum)).astype(
        jnp.bfloat16
    )


def body(image_feats, text_feats, image_weight, text_weight, partner, log_scale, logit_bias):
    rows, width = text_feats.shape[0], image_weight.shape[1]
    quarter_rows = rows // 4
    out_rows = (image_feats.shape[1] + text_feats.shape[1]) // 4
    own_rows = out_rows // 32
    xl, core = lax.axis_index("xl"), lax.axis_index("core")
    z, xh, y = lax.axis_index("z"), lax.axis_index("xh"), lax.axis_index("y")
    quarter = (core * 2 + xl) * quarter_rows
    logit_scale = jnp.exp(log_scale[0])
    logit_shift = logit_bias[0]

    def quarter_of(array):
        return lax.dynamic_slice_in_dim(array, quarter, quarter_rows, 0)

    own_images, image_inverse = embed_rows(quarter_of(image_feats), image_weight)
    own_texts, text_inverse = embed_rows(text_feats, text_weight)
    flip = [(i, 3 - i) for i in range(4)]
    other_texts = lax.ppermute(own_texts, ("xl", "xh"), flip)
    texts = jnp.concatenate([own_texts, other_texts], 0)

    half = quarter_rows // 2
    part_a = jnp.concatenate(ring_gather(own_images[:half], "z"), 0)
    part_b = jnp.concatenate(ring_gather(own_images[half:], "y"), 0)
    images = jnp.concatenate(ring_gather(part_a, "y") + ring_gather(part_b, "z"), 0)

    sent = jnp.broadcast_to(quarter_of(partner)[None], (16, quarter_rows))
    got = lax.all_to_all(sent, ("z", "y"), split_axis=0, concat_axis=0, tiled=True)
    got = got.reshape(4, 4, quarter_rows)
    steps = jnp.array([0, 1, 3, 2], jnp.int32)
    got = jnp.take(jnp.take(got, (z + steps) % 4, axis=0), (y + steps) % 4, axis=1)
    partners = jnp.concatenate(
        [got[:, :, :half].transpose(1, 0, 2).reshape(-1), got[:, :, half:].reshape(-1)]
    )

    logits = (
        logit_scale
        * lax.dot_general(
            images, texts, (((1,), (1,)), ((), ())), preferred_element_type=jnp.float32
        )
        + logit_shift
    )
    local = lax.iota(jnp.int32, rows)
    block_of = lambda which: ((z * 2 + which) * 4 + y) * rows
    columns = jnp.concatenate([block_of(xh) + local, block_of(1 - xh) + local])
    labels = jnp.where(partners[:, None] == columns[None, :], 1.0, -1.0).astype(jnp.float32)
    slopes = -labels * jax.nn.sigmoid(-labels * logits)
    coefficient = (logit_scale * slopes).astype(jnp.bfloat16)
    image_part = jnp.dot(coefficient, texts, preferred_element_type=jnp.float32)
    text_part = lax.dot_general(
        coefficient, images, (((0,), (0,)), ((), ())), preferred_element_type=jnp.float32
    )

    by_core = text_part.reshape(2, 2, rows // 2, width)
    kept = lax.dynamic_index_in_dim(by_core, core, 1, keepdims=False)
    given = lax.dynamic_index_in_dim(by_core, 1 - core, 1, keepdims=False)
    summed = kept + lax.ppermute(given, "core", [(0, 1), (1, 0)])
    summed = summed.reshape(4, quarter_rows, width)
    pick = lambda first, second: lax.dynamic_index_in_dim(
        summed, jnp.where(xl == 0, first, second), 0, keepdims=False
    )
    text_grad = ring_scatter([pick(0, 1), pick(1, 2), pick(3, 0), pick(2, 3)], "x")

    rows_a = image_part[: 2 * rows].reshape(4, 8 * half // 2, width)
    rows_b = image_part[2 * rows :].reshape(4, 8 * half // 2, width)
    sum_a = ring_scatter([rows_a[i] for i in range(4)], "y")
    sum_b = ring_scatter([rows_b[i] for i in range(4)], "z")
    sum_a = sum_a.reshape(4, half, width)
    sum_b = sum_b.reshape(4, half, width)
    image_grad = jnp.concatenate(
        [
            ring_scatter([sum_a[i] for i in range(4)], "z"),
            ring_scatter([sum_b[i] for i in range(4)], "y"),
        ],
        0,
    )

    image_back = back_rows(own_images, image_inverse, image_grad)
    text_back = back_rows(quarter_of(own_texts), quarter_of(text_inverse), text_grad)

    def tower_gather(back):
        pair = jnp.concatenate([back, lax.ppermute(back, "xl", [(0, 1), (1, 0)])], 0)
        return jnp.concatenate([pair, lax.ppermute(pair, "core", [(0, 1), (1, 0)])], 0)

    def tower_order(feats):
        pick = lambda c, x: lax.dynamic_slice_in_dim(
            feats, (c * 2 + x) * quarter_rows, quarter_rows, 0
        )
        return jnp.concatenate(
            [pick(core, xl), pick(core, 1 - xl), pick(1 - core, xl), pick(1 - core, 1 - xl)], 0
        )

    tower = xl * 2 + core
    place = lax.iota(jnp.int32, 32 * GROUP)
    wanted = tower * out_rows + (place // GROUP) * own_rows + place % GROUP
    wanted = jnp.where(place % GROUP < own_rows, wanted, -1)

    def chosen(feats, first):
        index = first + lax.iota(jnp.int32, feats.shape[1])
        select = (wanted[:, None] == index[None, :]).astype(jnp.bfloat16)
        return lax.dot_general(
            select, tower_order(feats), (((1,), (1,)), ((), ())),
            preferred_element_type=jnp.float32,
        ).astype(jnp.bfloat16)

    image_columns = chosen(image_feats, 0)
    text_columns = chosen(text_feats, image_feats.shape[1])
    terms = jnp.dot(
        image_columns, tower_gather(image_back), preferred_element_type=jnp.float32
    ) + jnp.dot(text_columns, tower_gather(text_back), preferred_element_type=jnp.float32)
    spread = lax.all_to_all(
        terms.reshape(32, GROUP, width), DP, split_axis=0, concat_axis=0, tiled=True
    )
    return jnp.sum(spread, axis=0)[:own_rows]


def solution(mesh):
    fine = Mesh(mesh.devices.reshape([SIZES[a] for a in AXES]), AXES)
    placed = (P(DP, None), P(DP, None), P(), P(), P(DP), P(), P())
    return jax.shard_map(
        body, mesh=fine, in_specs=placed, out_specs=P(TOWER + DP, None), check_vma=False
    )
```

```python
import jax
import jax.numpy as jnp
from jax import lax
from jax.sharding import Mesh, PartitionSpec as P

AXES = ("xl", "core", "z", "xh", "y")
SIZES = {"xl": 2, "core": 2, "z": 4, "xh": 2, "y": 4}
DP = ("z", "xh", "y")
TOWER = ("xl", "core")
GROUP = 24
SWAP = [(0, 1), (1, 0)]
FLIP = [(0, 3), (1, 2), (2, 1), (3, 0)]


def embed_rows(features, weight):
    projected = jnp.dot(features, weight, preferred_element_type=jnp.float32)
    inverse = lax.rsqrt(jnp.sum(projected * projected, axis=1) + 1e-06).astype(jnp.bfloat16)
    inverse = lax.optimization_barrier(inverse)
    embedded = (projected * inverse.astype(jnp.float32)[:, None]).astype(jnp.bfloat16)
    return (lax.optimization_barrier(embedded), inverse)


def back_rows(embedded, inverse, gradients):
    widened = embedded.astype(jnp.float32)
    inner_sum = jnp.sum(widened * gradients, axis=1, keepdims=True)
    return (inverse.astype(jnp.float32)[:, None] * (gradients - widened * inner_sum)).astype(
        jnp.bfloat16
    )


def body(image_feats, text_feats, image_weight, text_weight, partner, log_scale, logit_bias):
    rows, width = text_feats.shape[0], image_weight.shape[1]
    half, quarter = rows // 2, rows // 4
    out_rows = (image_feats.shape[1] + text_feats.shape[1]) // 4
    own_rows = out_rows // 32
    xl, core = lax.axis_index("xl"), lax.axis_index("core")
    z, xh, y = lax.axis_index("z"), lax.axis_index("xh"), lax.axis_index("y")
    text_half = jnp.where(xl == xh, 0, 1)
    text_quarter = text_half * 2 + core
    logit_scale = jnp.exp(log_scale[0])
    logit_shift = logit_bias[0]

    def rows_at(array, start, count):
        return lax.dynamic_slice_in_dim(array, start, count, 0)

    half_images, image_inverse = embed_rows(rows_at(image_feats, core * half, half), image_weight)
    own_texts, text_inverse = embed_rows(
        rows_at(text_feats, text_quarter * quarter, quarter), text_weight
    )
    other_texts = lax.ppermute(own_texts, ("xl", "xh"), FLIP)
    pair_texts = jnp.concatenate([own_texts, other_texts], 0)
    sent = jnp.broadcast_to(pair_texts[None], (4, half, width))
    texts = lax.all_to_all(sent, "y", split_axis=0, concat_axis=0, tiled=True)
    texts = texts.reshape(4 * half, width)
    mine = lax.all_gather(half_images, "z", axis=0, tiled=True)
    theirs = lax.ppermute(mine, "core", SWAP)
    images = jnp.concatenate([mine, theirs], 0)

    sent = jnp.broadcast_to(partner[None], (4, rows))
    partners = lax.all_to_all(sent, "z", split_axis=0, concat_axis=0, tiled=True)
    partners = partners.reshape(4, 2, half)
    partners = jnp.concatenate(
        [
            lax.dynamic_index_in_dim(partners, core, 1, keepdims=False).reshape(-1),
            lax.dynamic_index_in_dim(partners, 1 - core, 1, keepdims=False).reshape(-1),
        ]
    )

    logits = (
        logit_scale
        * lax.dot_general(
            images, texts, (((1,), (1,)), ((), ())), preferred_element_type=jnp.float32
        )
        + logit_shift
    )
    place = lax.iota(jnp.int32, 4 * half)
    text_xh = jnp.where(place % half < quarter, xh, 1 - xh)
    columns = ((z * 2 + text_xh) * 4 + place // half) * rows
    columns = columns + text_quarter * quarter + place % quarter
    labels = jnp.where(partners[:, None] == columns[None, :], 1.0, -1.0).astype(jnp.float32)
    slopes = -labels * jax.nn.sigmoid(-labels * logits)
    coefficient = (logit_scale * slopes).astype(jnp.bfloat16)
    given = jnp.dot(coefficient[4 * half :], texts, preferred_element_type=jnp.float32)
    taken = lax.ppermute(given, "core", SWAP)
    text_part = lax.dot_general(
        coefficient, images, (((0,), (0,)), ((), ())), preferred_element_type=jnp.float32
    )
    kept = jnp.dot(coefficient[: 4 * half], texts, preferred_element_type=jnp.float32)

    image_sum = lax.psum_scatter(kept + taken, "z", scatter_dimension=0, tiled=True)
    image_got = lax.ppermute(rows_at(image_sum, (1 - xl) * quarter, quarter), "xl", SWAP)
    image_grad = rows_at(image_sum, xl * quarter, quarter) + image_got

    text_terms = lax.all_to_all(
        text_part.reshape(4, half, width), "y", split_axis=0, concat_axis=0, tiled=True
    )
    text_sum = jnp.sum(text_terms, axis=0)
    text_grad = text_sum[:quarter] + lax.ppermute(text_sum[quarter:], ("xl", "xh"), FLIP)

    image_back = back_rows(
        rows_at(half_images, xl * quarter, quarter),
        rows_at(image_inverse, xl * quarter, quarter),
        image_grad,
    )
    text_back = back_rows(own_texts, text_inverse, text_grad)
    image_backs = lax.all_gather(image_back, TOWER, axis=0, tiled=True)
    text_backs = lax.all_gather(text_back, TOWER, axis=0, tiled=True)

    image_order = jnp.concatenate(
        [image_feats[i * quarter : (i + 1) * quarter] for i in (0, 2, 1, 3)], 0
    )
    text_order = jnp.concatenate(
        [rows_at(text_feats, xh * half, half), rows_at(text_feats, (1 - xh) * half, half)], 0
    )
    tower = xl * 2 + core
    place = lax.iota(jnp.int32, 32 * GROUP)
    wanted = tower * out_rows + (place // GROUP) * own_rows + place % GROUP
    wanted = jnp.where(place % GROUP < own_rows, wanted, -1)

    def chosen(feats, first):
        index = first + lax.iota(jnp.int32, feats.shape[1])
        select = (wanted[:, None] == index[None, :]).astype(jnp.bfloat16)
        return lax.dot_general(
            select, feats, (((1,), (1,)), ((), ())), preferred_element_type=jnp.float32
        ).astype(jnp.bfloat16)

    image_columns = chosen(image_order, 0)
    text_columns = chosen(text_order, image_feats.shape[1])
    terms = jnp.dot(image_columns, image_backs, preferred_element_type=jnp.float32) + jnp.dot(
        text_columns, text_backs, preferred_element_type=jnp.float32
    )
    spread = lax.all_to_all(
        terms.reshape(32, GROUP, width), DP, split_axis=0, concat_axis=0, tiled=True
    )
    return jnp.sum(spread, axis=0)[:own_rows]


def solution(mesh):
    fine = Mesh(mesh.devices.reshape([SIZES[a] for a in AXES]), AXES)
    placed = (P(DP, None), P(DP, None), P(), P(), P(DP), P(), P())
    return jax.shard_map(
        body, mesh=fine, in_specs=placed, out_specs=P(TOWER + DP, None), check_vma=False
    )
```

```python
import jax
import jax.numpy as jnp
from jax import lax
from jax.sharding import Mesh, PartitionSpec as P

AXES = ("xl", "core", "z", "xh", "y")
SIZES = {"xl": 2, "core": 2, "z": 4, "xh": 2, "y": 4}
DP = ("z", "xh", "y")
TOWER = ("xl", "core")
GROUP = 24
SWAP = [(0, 1), (1, 0)]
FLIP = [(0, 3), (1, 2), (2, 1), (3, 0)]


def embed_rows(features, weight):
    projected = jnp.dot(features, weight, preferred_element_type=jnp.float32)
    inverse = lax.rsqrt(jnp.sum(projected * projected, axis=1) + 1e-06).astype(jnp.bfloat16)
    inverse = lax.optimization_barrier(inverse)
    embedded = (projected * inverse.astype(jnp.float32)[:, None]).astype(jnp.bfloat16)
    return (lax.optimization_barrier(embedded), inverse)


def back_rows(embedded, inverse, gradients):
    widened = embedded.astype(jnp.float32)
    inner_sum = jnp.sum(widened * gradients, axis=1, keepdims=True)
    return (inverse.astype(jnp.float32)[:, None] * (gradients - widened * inner_sum)).astype(
        jnp.bfloat16
    )


def to_all(block, axis):
    sent = jnp.broadcast_to(block[None], (4,) + block.shape)
    got = lax.all_to_all(sent, axis, split_axis=0, concat_axis=0, tiled=True)
    return got.reshape((-1,) + block.shape[1:])


def reduce_blocks(terms, own_rows):
    largest = jnp.maximum(jnp.max(jnp.abs(terms), axis=(1, 2), keepdims=True), 1e-30)
    exponent = jnp.ceil(jnp.log2(largest) * 16.0 + 0.01)
    coded = jnp.round(terms * (32767.0 * jnp.exp2(exponent * -0.0625)))
    row = lax.broadcasted_iota(jnp.int32, terms.shape, 1)
    coded = jnp.where(row == own_rows, exponent, coded).astype(jnp.int16)
    got = lax.all_to_all(coded, DP, split_axis=0, concat_axis=0, tiled=True)
    scale = jnp.exp2(got[:, own_rows, :1].astype(jnp.float32) * 0.0625) * (1.0 / 32767.0)
    return jnp.sum(got[:, :own_rows].astype(jnp.float32) * scale[:, :, None], axis=0)


def body(image_feats, text_feats, image_weight, text_weight, partner, log_scale, logit_bias):
    rows, width = text_feats.shape[0], image_weight.shape[1]
    half, quarter = rows // 2, rows // 4
    out_rows = (image_feats.shape[1] + text_feats.shape[1]) // 4
    own_rows = out_rows // 32
    xl, core = lax.axis_index("xl"), lax.axis_index("core")
    z, xh, y = lax.axis_index("z"), lax.axis_index("xh"), lax.axis_index("y")
    text_half = jnp.where(xl == xh, 0, 1)
    text_quarter = text_half * 2 + core
    logit_scale = jnp.exp(log_scale[0])
    logit_shift = logit_bias[0]

    def rows_at(array, start, count):
        return lax.dynamic_slice_in_dim(array, start, count, 0)

    own_texts, text_inverse = embed_rows(
        rows_at(text_feats, text_quarter * quarter, quarter), text_weight
    )
    other_texts = lax.ppermute(own_texts, ("xl", "xh"), FLIP)
    half_images, image_inverse = embed_rows(rows_at(image_feats, core * half, half), image_weight)
    mine = to_all(half_images, "z")
    texts = to_all(jnp.concatenate([own_texts, other_texts], 0), "y")
    theirs = lax.ppermute(mine, "core", SWAP)
    images = jnp.concatenate([mine, theirs], 0)

    partners = to_all(partner, "z").reshape(4, 2, half)
    partners = jnp.concatenate(
        [
            lax.dynamic_index_in_dim(partners, core, 1, keepdims=False).reshape(-1),
            lax.dynamic_index_in_dim(partners, 1 - core, 1, keepdims=False).reshape(-1),
        ]
    )

    logits = (
        logit_scale
        * lax.dot_general(
            images, texts, (((1,), (1,)), ((), ())), preferred_element_type=jnp.float32
        )
        + logit_shift
    )
    place = lax.iota(jnp.int32, 4 * half)
    text_xh = jnp.where(place % half < quarter, xh, 1 - xh)
    columns = ((z * 2 + text_xh) * 4 + place // half) * rows
    columns = columns + text_quarter * quarter + place % quarter
    labels = jnp.where(partners[:, None] == columns[None, :], 1.0, -1.0).astype(jnp.float32)
    slopes = -labels * jax.nn.sigmoid(-labels * logits)
    coefficient = (logit_scale * slopes).astype(jnp.bfloat16)
    text_part = lax.dot_general(
        coefficient, images, (((0,), (0,)), ((), ())), preferred_element_type=jnp.float32
    )
    given = jnp.dot(coefficient[4 * half :], texts, preferred_element_type=jnp.float32)
    taken = lax.ppermute(given, "core", SWAP)
    kept = jnp.dot(coefficient[: 4 * half], texts, preferred_element_type=jnp.float32)

    text_terms = lax.all_to_all(
        text_part.reshape(4, half, width), "y", split_axis=0, concat_axis=0, tiled=True
    )
    image_terms = lax.all_to_all(
        (kept + taken).reshape(4, half, width), "z", split_axis=0, concat_axis=0, tiled=True
    )
    text_got = lax.ppermute(jnp.sum(text_terms[:, quarter:], axis=0), ("xl", "xh"), FLIP)
    text_grad = jnp.sum(text_terms[:, :quarter], axis=0) + text_got
    image_got = lax.ppermute(
        jnp.sum(lax.dynamic_slice_in_dim(image_terms, (1 - xl) * quarter, quarter, 1), axis=0),
        "xl",
        SWAP,
    )
    image_grad = image_got + jnp.sum(
        lax.dynamic_slice_in_dim(image_terms, xl * quarter, quarter, 1), axis=0
    )

    image_back = back_rows(
        rows_at(half_images, xl * quarter, quarter),
        rows_at(image_inverse, xl * quarter, quarter),
        image_grad,
    )
    text_back = back_rows(own_texts, text_inverse, text_grad)
    image_backs = lax.all_gather(image_back, TOWER, axis=0, tiled=True)
    text_backs = lax.all_gather(text_back, TOWER, axis=0, tiled=True)

    image_order = jnp.concatenate(
        [image_feats[i * quarter : (i + 1) * quarter] for i in (0, 2, 1, 3)], 0
    )
    text_order = jnp.concatenate(
        [rows_at(text_feats, xh * half, half), rows_at(text_feats, (1 - xh) * half, half)], 0
    )
    tower = xl * 2 + core
    place = lax.iota(jnp.int32, 32 * GROUP)
    wanted = tower * out_rows + (place // GROUP) * own_rows + place % GROUP
    wanted = jnp.where(place % GROUP < own_rows, wanted, -1)

    def chosen(feats, first):
        index = first + lax.iota(jnp.int32, feats.shape[1])
        select = (wanted[:, None] == index[None, :]).astype(jnp.bfloat16)
        return lax.dot_general(
            select, feats, (((1,), (1,)), ((), ())), preferred_element_type=jnp.float32
        ).astype(jnp.bfloat16)

    image_columns = chosen(image_order, 0)
    text_columns = chosen(text_order, image_feats.shape[1])
    terms = jnp.dot(image_columns, image_backs, preferred_element_type=jnp.float32) + jnp.dot(
        text_columns, text_backs, preferred_element_type=jnp.float32
    )
    return reduce_blocks(terms.reshape(32, GROUP, width), own_rows)


def solution(mesh):
    fine = Mesh(mesh.devices.reshape([SIZES[a] for a in AXES]), AXES)
    placed = (P(DP, None), P(DP, None), P(), P(), P(DP), P(), P())
    return jax.shard_map(
        body, mesh=fine, in_specs=placed, out_specs=P(TOWER + DP, None), check_vma=False
    )
```

```python
import math

import jax
import jax.numpy as jnp
from jax import lax
from jax.experimental import pallas as pl
from jax.experimental.pallas import tpu as pltpu
from jax.sharding import Mesh, PartitionSpec as P

AXES = ("xl", "core", "z", "xh", "y")
SIZES = {"xl": 2, "core": 2, "z": 4, "xh": 2, "y": 4}
DP = ("z", "xh", "y")
TOWER = ("xl", "core")
SWAP = [(0, 1), (1, 0)]
FLIP = [(0, 3), (1, 2), (2, 1), (3, 0)]
ROWS = 384
HALF, QUARTER = 192, 96
EXTRA = 16
E = 1024
TILE = 4 * HALF
OWN = 21
GROUP = 24
SLICE = E // 4
STEP = 8
NT = (((1,), (1,)), ((), ()))
TN = (((0,), (0,)), ((), ()))
OCTAVE = math.log(2.0) / 16.0
F32, BF16 = jnp.float32, jnp.bfloat16


def shifted(array, axis, by):
    return lax.ppermute(array, axis, [(i, (i + by) % 4) for i in range(4)])


def call(kernel, outs, flops, moved, limit=16, **options):
    return pl.pallas_call(
        kernel,
        out_shape=outs,
        cost_estimate=pl.CostEstimate(flops=flops, bytes_accessed=moved, transcendentals=0),
        compiler_params=pltpu.CompilerParams(vmem_limit_bytes=limit << 20),
        **options,
    )


def shape(*dims, dtype=F32):
    return jax.ShapeDtypeStruct(dims, dtype)


VMEM = pl.BlockSpec(memory_space=pltpu.VMEM)
SMEM = pl.BlockSpec(memory_space=pltpu.SMEM)
ANY = pl.BlockSpec(memory_space=pl.ANY)


def position(where_ref):
    index = where_ref[0]
    xl, core, z, xh, y = index // 64, index // 32 % 2, index // 8 % 4, index // 4 % 2, index % 4
    return xl, core, z, xh, y, (xl + xh) % 2 * 2 + core


def normalised(pre_ref, inverse_ref):
    pre = pre_ref[...]
    total = jnp.sum(pre * pre, axis=1, keepdims=True)
    inverse = lax.rsqrt(total + 1e-06).astype(BF16).astype(F32)
    inverse_ref[...] = jnp.broadcast_to(inverse[:QUARTER], (QUARTER, 128))
    return (pre * inverse).astype(BF16)


def embed_kernel(
    where_ref, partner_ref, text_feats, image_feats, text_weight, image_weight,
    text_ref, text_inverse, load_ref, image_inverse,
    text_rows, image_rows, text_held, image_held, text_pre, image_pre, sems,
):
    count = 0

    def begin(source, target):
        nonlocal count
        copy = pltpu.make_async_copy(source, target, sems.at[count])
        copy.start()
        count += 1
        return copy

    xl, core, _, _, _, text_quarter = position(where_ref)
    places = core * 2 + xl, core * 2 + 1 - xl

    def rows(place):
        return pl.ds(pl.multiple_of(place * QUARTER, QUARTER), QUARTER)

    def begin_weight(weight, held, ends):
        spans = [slice(a, b) for a, b in zip((0,) + ends, ends)]
        return [(span, begin(weight.at[span], held.at[span])) for span in spans]

    def project(rows_ref, held, waits, pre_ref):
        for i, (span, copy) in enumerate(waits):
            copy.wait()
            got = jnp.dot(rows_ref[:, span], held[span, :], preferred_element_type=F32)
            pre_ref[...] = got if i == 0 else pre_ref[...] + got

    text_copy = begin(text_feats.at[rows(text_quarter)], text_rows)
    text_waits = begin_weight(text_weight, text_held, (256, 512, 768, 1024))
    image_copies = [
        begin(image_feats.at[rows(place)], image_rows.at[i * QUARTER : (i + 1) * QUARTER])
        for i, place in enumerate(places)
    ]
    image_waits = begin_weight(image_weight, image_held, (384, 768, 1152, 1664))

    text_copy.wait()
    project(text_rows, text_held, text_waits, text_pre)
    text_ref[...] = normalised(text_pre, text_inverse)
    for copy in image_copies:
        copy.wait()
    project(image_rows, image_held, image_waits, image_pre)
    load_ref[:HALF, :] = normalised(image_pre, image_inverse)

    partner = jnp.concatenate([partner_ref[i : i + 1, :] for i in range(3)], 1).astype(F32)
    partner = jnp.broadcast_to(partner, (EXTRA, ROWS))
    lane = lax.broadcasted_iota(jnp.int32, (EXTRA, ROWS), 1)
    row = lax.broadcasted_iota(jnp.int32, (EXTRA, ROWS), 0)
    chosen = jnp.zeros((EXTRA, ROWS), F32)
    for i, place in enumerate(places):
        moved = pltpu.roll(partner, (i + 4 - place) % 4 * QUARTER, 1)
        chosen = jnp.where(lane // QUARTER == i, moved, chosen)
    high = jnp.floor(chosen * (1.0 / 128.0))
    parts = jnp.where(row == 0, high, jnp.where(row == 1, chosen - 128.0 * high, 0.0))
    load_ref[HALF:, :] = jnp.zeros((EXTRA, E), BF16)
    load_ref[HALF:, :ROWS] = parts.astype(BF16)


def ring_gather(block, axis):
    before, after = shifted(block, axis, 1), shifted(block, axis, -1)
    far_low = shifted(before[:QUARTER], axis, 1)
    far_high = shifted(after[QUARTER:], axis, -1)
    return block, after, before, far_low, far_high


def ring_scatter(far_low, far_high, after, before, mine, axis, crossed):
    far = shifted(far_low + crossed(far_high), axis, 2)
    got_right, got_left = shifted(after, axis, 1), shifted(before, axis, -1)
    high = mine[QUARTER:] + got_right[QUARTER:] + got_left[QUARTER:]
    return mine, got_right, got_left, far, crossed(high)


ORDER = ((2, 0), (2, 1), (1, 0), (1, 1), (3, 0), (3, 1), (0, 0), (0, 1))


def in_order(refs, out_ref):
    me, after, before, far_low, far_high = refs
    for place, (step, half) in enumerate(ORDER):
        ref = (me, after, far_high if half else far_low, before)[step]
        start = 0 if step == 2 else half * QUARTER
        out_ref[place * QUARTER : (place + 1) * QUARTER, :] = ref[start : start + QUARTER, :]


def images_kernel(me, after, before, far_low, far_high, out_ref):
    in_order((me, after, before, far_low, far_high), out_ref)
    lane = lax.broadcasted_iota(jnp.int32, (EXTRA, E), 1)
    carried = [ref[start:, :].astype(F32) for ref, start in (
        (me, HALF), (after, HALF), (far_high, QUARTER), (before, HALF)
    )]
    total = jnp.zeros((EXTRA, E), F32)
    for place, (step, half) in enumerate(ORDER):
        inside = (lane >= half * QUARTER) & (lane < (half + 1) * QUARTER)
        piece = jnp.where(inside, carried[step], 0.0)
        total += pltpu.roll(piece, (place - half) * QUARTER % E, 1)
    out_ref[TILE:, :] = total.astype(BF16)


def coefficients(where_ref, scalar_ref, images_ref, texts_ref, coef_ref):
    _, _, z, xh, y, text_quarter = position(where_ref)
    parts = images_ref[TILE:, :TILE].astype(F32)
    partner = (parts[0:1] * 128.0 + parts[1:2]).astype(jnp.int32)
    scale, shift = scalar_ref[0], scalar_ref[1]
    row = lax.broadcasted_iota(jnp.int32, (HALF, 1), 0)
    for block in range(4):
        rows = slice(block * HALF, (block + 1) * HALF)
        low, high = (
            ((z * 2 + (1 - xh if half else xh)) * 4 + lax.rem(y + step, 4)) * ROWS
            + text_quarter * QUARTER
            for step, half in ORDER[2 * block : 2 * block + 2]
        )
        index = row + jnp.where(row < QUARTER, low, high - QUARTER)
        logits = scale * lax.dot_general(
            texts_ref[rows, :], images_ref[:TILE, :], NT, preferred_element_type=F32
        ) + shift
        own = index == partner
        slopes = jnp.where(own, -scale, scale) / (1.0 + jnp.exp(jnp.where(own, logits, -logits)))
        coef_ref[rows, :] = slopes.astype(BF16)


def image_terms(coef_ref, texts_ref, part):
    return lax.dot_general(
        coef_ref[:, part * ROWS : (part + 1) * ROWS], texts_ref[...], TN,
        preferred_element_type=F32,
    )


def share_out(got, outs):
    start = 0
    for out in outs:
        out[...] = got[start : start + out.shape[0]]
        start += out.shape[0]


def own_kernel(
    where_ref, scalar_ref, me, after, before, far_low, far_high, images_ref, early_a, early_b,
    texts_ref, coef_ref,
):
    in_order((me, after, before, far_low, far_high), texts_ref)
    coefficients(where_ref, scalar_ref, images_ref, texts_ref, coef_ref)


def given_kernel(where_ref, scalar_ref, texts_ref, images_ref, coef_ref, given_ref):
    coefficients(where_ref, scalar_ref, images_ref, texts_ref, coef_ref)
    given_ref[...] = image_terms(coef_ref, texts_ref, 0)


def given_rest_kernel(texts_ref, coef_ref, given_ref):
    given_ref[...] = image_terms(coef_ref, texts_ref, 1)


def text_kernel(part, own_coef, images_ref, others_coef, others_ref, *outs):
    rows = slice(part * ROWS, (part + 1) * ROWS)
    got = jnp.dot(own_coef[rows, :], images_ref[:TILE, :], preferred_element_type=F32)
    got += jnp.dot(others_coef[rows, :], others_ref[:TILE, :], preferred_element_type=F32)
    share_out(got, outs)


def kept_kernel(part, texts_ref, coef_ref, taken_ref, *outs):
    share_out(image_terms(coef_ref, texts_ref, part) + taken_ref[...], outs)


def back_kernel(*refs):
    *inputs, out_ref = refs
    for tower in range(2):
        mine, right, left, far, got, emb, inverse = inputs[tower * 7 : tower * 7 + 7]
        gradients = mine[:QUARTER, :] + right[:QUARTER, :] + left[:QUARTER, :]
        gradients += far[...] + got[...]
        widened = emb[:QUARTER, :].astype(F32)
        inner_sum = jnp.sum(widened * gradients, axis=1, keepdims=True)
        value = (inverse[:, :1] * (gradients - widened * inner_sum)).astype(BF16)
        for i in range(4):
            out_ref[i, tower * QUARTER : (tower + 1) * QUARTER, :] = value[
                :, i * SLICE : (i + 1) * SLICE
            ]


def terms_kernel(images_ref, texts_ref, backs_ref, out_ref, both_ref):
    for i in range(4):
        for part in range(2):
            both_ref[part, i * QUARTER : (i + 1) * QUARTER, :] = backs_ref[
                i, part * QUARTER : (part + 1) * QUARTER, :
            ]
    rows = STEP * GROUP
    steps = 128 // STEP
    last = images_ref.shape[0] // rows - 1
    first = steps - texts_ref.shape[0] // rows
    for step in range(steps):
        terms = jnp.zeros((rows, SLICE), F32)
        if step <= last:
            terms += jnp.dot(
                images_ref[step * rows : (step + 1) * rows, :], both_ref[0],
                preferred_element_type=F32,
            )
        if step >= first:
            terms += jnp.dot(
                texts_ref[(step - first) * rows : (step - first + 1) * rows, :], both_ref[1],
                preferred_element_type=F32,
            )
        terms = terms.reshape(STEP, GROUP, SLICE)
        largest = jnp.max(jnp.max(jnp.abs(terms), axis=1), axis=1, keepdims=True)
        exponent = jnp.ceil(jnp.log(jnp.maximum(largest, 1e-30)) * (1.0 / OCTAVE) + 0.01)
        factor = 32767.0 * jnp.exp(exponent * -OCTAVE)
        row = lax.broadcasted_iota(jnp.int32, terms.shape, 1)
        coded = jnp.where(row == OWN, exponent[:, :, None], jnp.round(terms * factor[:, :, None]))
        out_ref[step * STEP : (step + 1) * STEP] = coded.astype(jnp.int32).astype(jnp.int16)


def total_kernel(coded_ref, out_ref):
    for part in range(4):
        total = jnp.zeros((GROUP, SLICE), F32)
        for i in range(32):
            terms = coded_ref[part * 32 + i].astype(jnp.int32).astype(F32)
            total += terms * (jnp.exp(terms[OWN : OWN + 1, :] * OCTAVE) * (1.0 / 32767.0))
        out_ref[:, part * SLICE : (part + 1) * SLICE] = total[:OWN]


def groups_kernel(where_ref, image_feats, text_feats, early, image_out, text_out, held_ref):
    def fill(feats_ref, out_ref, starts, start, first):
        depth = feats_ref.shape[1]
        for i, at in enumerate(starts):
            held_ref[i * QUARTER : (i + 1) * QUARTER, :depth] = feats_ref[at, :]
        for i in range(out_ref.shape[0] // (STEP * GROUP)):
            begin = (first + i) * STEP * OWN - start
            low = min(max(begin // 128 * 128, 0), depth - ROWS)
            row = lax.broadcasted_iota(jnp.int32, (STEP * GROUP, ROWS), 0)
            lane = lax.broadcasted_iota(jnp.int32, (STEP * GROUP, ROWS), 1)
            inside = lax.rem(row, GROUP)
            wanted = lax.div(row, GROUP) * OWN + inside + (begin - low)
            select = jnp.where((inside < OWN) & (wanted == lane), 1.0, 0.0).astype(BF16)
            out_ref[i * STEP * GROUP : (i + 1) * STEP * GROUP, :] = lax.dot_general(
                select, held_ref[:, low : low + ROWS], NT, preferred_element_type=F32
            ).astype(BF16)

    width = image_feats.shape[1]
    quarters = [pl.ds(i * QUARTER, QUARTER) for i in (0, 2, 1, 3)]
    fill(image_feats, image_out, quarters, 0, 0)
    _, _, _, xh, _, _ = position(where_ref)
    half = [xh, xh, 1 - xh, 1 - xh]
    quarters = [
        pl.ds(pl.multiple_of(half[i] * HALF + i % 2 * QUARTER, QUARTER), QUARTER) for i in range(4)
    ]
    fill(text_feats, text_out, quarters, width, width // OWN // STEP)


def body(image_feats, text_feats, image_weight, text_weight, partner, log_scale, logit_bias):
    where = lax.axis_index(AXES).astype(jnp.int32).reshape(1)
    scalars = jnp.concatenate([jnp.exp(log_scale), logit_bias])

    depth = image_feats.shape[1]
    own_texts, text_inverse, load, image_inverse = call(
        embed_kernel,
        [
            shape(QUARTER, E, dtype=BF16), shape(QUARTER, 128),
            shape(HALF + EXTRA, E, dtype=BF16), shape(QUARTER, 128),
        ],
        2 * (QUARTER * E + HALF * depth) * E, 8 << 20, 60,
        in_specs=[SMEM, VMEM] + [ANY] * 4, out_specs=[VMEM] * 4,
        scratch_shapes=[
            pltpu.VMEM((QUARTER, E), BF16), pltpu.VMEM((HALF, depth), BF16),
            pltpu.VMEM((E, E), BF16), pltpu.VMEM((depth, E), BF16),
            pltpu.VMEM((QUARTER, E), F32), pltpu.VMEM((HALF, E), F32),
            pltpu.SemaphoreType.DMA((11,)),
        ],
    )(where, partner.reshape(3, 128), text_feats, image_feats, text_weight, image_weight)
    other_texts = lax.ppermute(own_texts, ("xl", "xh"), FLIP)
    pair = jnp.concatenate([own_texts, other_texts], 0)
    image_pieces, text_pieces = ring_gather(load, "z"), ring_gather(pair, "y")
    images = call(
        images_kernel, shape(TILE + EXTRA, E, dtype=BF16), 0, 4 << 20,
        in_specs=[VMEM] * 5, out_specs=VMEM,
    )(*image_pieces)
    others = lax.ppermute(images, "core", SWAP)

    last, first = (depth - 1) // OWN // STEP, depth // OWN // STEP
    image_groups, text_groups = call(
        groups_kernel,
        [
            shape((last + 1) * STEP * GROUP, ROWS, dtype=BF16),
            shape((128 // STEP - first) * STEP * GROUP, ROWS, dtype=BF16),
        ],
        2 * 17 * STEP * GROUP * ROWS * ROWS, 5 << 20,
        in_specs=[SMEM, VMEM, VMEM, ANY], out_specs=[VMEM] * 2,
        scratch_shapes=[pltpu.VMEM((ROWS, depth), BF16)],
    )(where, image_feats, text_feats, image_pieces[2])

    flops = 2 * TILE * TILE * E
    coef, texts = shape(TILE, TILE, dtype=BF16), shape(TILE, E, dtype=BF16)
    ways = [shape(QUARTER, E)] * 2 + [shape(HALF, E)]
    rest = [shape(HALF, E)] * 2

    def run(kernel, outs, share, count, *options):
        return call(
            lambda *refs: kernel(*options, *refs), outs, int(share * flops), 6 << 20, 24,
            in_specs=[VMEM] * count, out_specs=[VMEM] * len(outs),
        )

    texts, own_coef = call(
        own_kernel, [texts, coef], 16 * flops, 6 << 20, 24,
        in_specs=[SMEM] * 2 + [VMEM] * 6 + [ANY] * 2, out_specs=[VMEM] * 2,
    )(where, scalars, *text_pieces, images, image_groups, text_groups)
    others_coef, given = call(
        given_kernel, [coef, shape(ROWS, E)], 2 * flops, 8 << 20, 24,
        in_specs=[SMEM] * 2 + [VMEM] * 2, out_specs=[VMEM] * 2,
    )(where, scalars, texts, others)
    taken = lax.ppermute(given, "core", SWAP)
    sides = own_coef, images, others_coef, others
    text_ways = run(text_kernel, ways, 1, 4, 0)(*sides)
    given_rest, = run(given_rest_kernel, [shape(ROWS, E)], 0.5, 2)(texts, others_coef)
    taken_rest = lax.ppermute(given_rest, "core", SWAP)
    image_ways = run(kept_kernel, ways, 0.5, 3, 0)(texts, own_coef, taken)
    text_rest = run(text_kernel, rest, 8, 4, 1)(*sides)
    image_rest = run(kept_kernel, rest, 0.5, 3, 1)(texts, own_coef, taken_rest)
    text_sums = ring_scatter(
        *text_ways, *text_rest, "y", lambda a: lax.ppermute(a, ("xl", "xh"), FLIP)
    )
    image_sums = ring_scatter(
        *image_ways, *image_rest, "z", lambda a: lax.ppermute(a, "xl", SWAP)
    )

    backs = call(
        back_kernel, shape(4, HALF, SLICE, dtype=BF16), 0, 6 << 20,
        in_specs=[VMEM] * 14, out_specs=VMEM,
    )(*image_sums, load, image_inverse, *text_sums, own_texts, text_inverse)
    backs = lax.all_to_all(backs, TOWER, split_axis=0, concat_axis=0, tiled=True)

    coded = call(
        terms_kernel, shape(128, GROUP, SLICE, dtype=jnp.int16),
        4 * 128 * GROUP * ROWS * SLICE, 6 << 20, 24,
        in_specs=[VMEM] * 3, out_specs=VMEM,
        scratch_shapes=[pltpu.VMEM((2, ROWS, SLICE), BF16)],
    )(image_groups, text_groups, backs)
    coded = lax.all_to_all(coded, AXES, split_axis=0, concat_axis=0, tiled=True)
    return call(total_kernel, shape(OWN, E), 0, 2 << 20, in_specs=[VMEM], out_specs=VMEM)(coded)


def solution(mesh):
    fine = Mesh(mesh.devices.reshape([SIZES[a] for a in AXES]), AXES)
    placed = (P(DP, None), P(DP, None), P(), P(), P(DP), P(), P())
    return jax.shard_map(
        body, mesh=fine, in_specs=placed, out_specs=P(TOWER + DP, None), check_vma=False
    )
```

```python
import math

import jax
import jax.numpy as jnp
from jax import lax
from jax.experimental import pallas as pl
from jax.experimental.pallas import tpu as pltpu
from jax.sharding import Mesh, PartitionSpec as P

AXES = ("xl", "core", "z", "xh", "y")
SIZES = {"xl": 2, "core": 2, "z": 4, "xh": 2, "y": 4}
DP = ("z", "xh", "y")
TOWER = ("xl", "core")
SWAP = [(0, 1), (1, 0)]
FLIP = [(0, 3), (1, 2), (2, 1), (3, 0)]
ROWS = 384
HALF, QUARTER = 192, 96
EXTRA = 16
E = 1024
TILE = 4 * HALF
OWN = 21
GROUP = 24
SLICE = E // 4
STEP = 8
NT = (((1,), (1,)), ((), ()))
TN = (((0,), (0,)), ((), ()))
OCTAVE = math.log(2.0) / 16.0
F32, BF16 = jnp.float32, jnp.bfloat16


def shifted(array, axis, by):
    return lax.ppermute(array, axis, [(i, (i + by) % 4) for i in range(4)])


def call(kernel, outs, flops, moved, limit=16, **options):
    return pl.pallas_call(
        kernel,
        out_shape=outs,
        cost_estimate=pl.CostEstimate(flops=flops, bytes_accessed=moved, transcendentals=0),
        compiler_params=pltpu.CompilerParams(vmem_limit_bytes=limit << 20),
        **options,
    )


def shape(*dims, dtype=F32):
    return jax.ShapeDtypeStruct(dims, dtype)


VMEM = pl.BlockSpec(memory_space=pltpu.VMEM)
SMEM = pl.BlockSpec(memory_space=pltpu.SMEM)
ANY = pl.BlockSpec(memory_space=pl.ANY)


def position(where_ref):
    index = where_ref[0]
    xl, core, z, xh, y = index // 64, index // 32 % 2, index // 8 % 4, index // 4 % 2, index % 4
    return xl, core, z, xh, y, (xl + xh) % 2 * 2 + core


def normalised(pre_ref, inverse_ref):
    pre = pre_ref[...]
    total = jnp.sum(pre * pre, axis=1, keepdims=True)
    inverse = lax.rsqrt(total + 1e-06).astype(BF16).astype(F32)
    inverse_ref[...] = jnp.broadcast_to(inverse[:QUARTER], (QUARTER, 128))
    return (pre * inverse).astype(BF16)


def embed_kernel(
    where_ref, partner_ref, text_feats, image_feats, text_weight, image_weight,
    text_ref, text_inverse, load_ref, image_inverse,
    text_rows, image_rows, text_held, image_held, text_pre, image_pre, sems,
):
    count = 0

    def begin(source, target):
        nonlocal count
        copy = pltpu.make_async_copy(source, target, sems.at[count])
        copy.start()
        count += 1
        return copy

    xl, core, _, _, _, text_quarter = position(where_ref)
    places = core * 2 + xl, core * 2 + 1 - xl

    def rows(place):
        return pl.ds(pl.multiple_of(place * QUARTER, QUARTER), QUARTER)

    def begin_weight(weight, held, ends):
        spans = [slice(a, b) for a, b in zip((0,) + ends, ends)]
        return [(span, begin(weight.at[span], held.at[span])) for span in spans]

    def project(rows_ref, held, waits, pre_ref):
        for i, (span, copy) in enumerate(waits):
            copy.wait()
            got = jnp.dot(rows_ref[:, span], held[span, :], preferred_element_type=F32)
            pre_ref[...] = got if i == 0 else pre_ref[...] + got

    text_copy = begin(text_feats.at[rows(text_quarter)], text_rows)
    text_waits = begin_weight(text_weight, text_held, (256, 512, 768, 1024))
    image_copies = [
        begin(image_feats.at[rows(place)], image_rows.at[i * QUARTER : (i + 1) * QUARTER])
        for i, place in enumerate(places)
    ]
    image_waits = begin_weight(image_weight, image_held, (384, 768, 1152, 1664))

    text_copy.wait()
    project(text_rows, text_held, text_waits, text_pre)
    text_ref[...] = normalised(text_pre, text_inverse)
    for copy in image_copies:
        copy.wait()
    project(image_rows, image_held, image_waits, image_pre)
    load_ref[:HALF, :] = normalised(image_pre, image_inverse)

    partner = jnp.concatenate([partner_ref[i : i + 1, :] for i in range(3)], 1).astype(F32)
    partner = jnp.broadcast_to(partner, (EXTRA, ROWS))
    lane = lax.broadcasted_iota(jnp.int32, (EXTRA, ROWS), 1)
    row = lax.broadcasted_iota(jnp.int32, (EXTRA, ROWS), 0)
    chosen = jnp.zeros((EXTRA, ROWS), F32)
    for i, place in enumerate(places):
        moved = pltpu.roll(partner, (i + 4 - place) % 4 * QUARTER, 1)
        chosen = jnp.where(lane // QUARTER == i, moved, chosen)
    high = jnp.floor(chosen * (1.0 / 128.0))
    parts = jnp.where(row == 0, high, jnp.where(row == 1, chosen - 128.0 * high, 0.0))
    load_ref[HALF:, :] = jnp.zeros((EXTRA, E), BF16)
    load_ref[HALF:, :ROWS] = parts.astype(BF16)


def ring_gather(block, axis):
    before, after = shifted(block, axis, 1), shifted(block, axis, -1)
    far_low = shifted(before[:QUARTER], axis, 1)
    far_high = shifted(after[QUARTER:], axis, -1)
    return block, after, before, far_low, far_high


def far_kernel(low_ref, high_ref, early_ref, out_ref):
    out_ref[...] = low_ref[...] + high_ref[...]


def ring_scatter(far_low, far_high, after, before, mine, axis, crossed):
    far = crossed(far_high)
    got_right, got_left = shifted(after, axis, 1), shifted(before, axis, -1)
    far = call(
        far_kernel, shape(QUARTER, E), 0, 1 << 20, in_specs=[VMEM, VMEM, ANY], out_specs=VMEM
    )(far_low, far, got_left)
    high = mine[QUARTER:] + got_right[QUARTER:] + got_left[QUARTER:]
    return mine, got_right, got_left, shifted(far, axis, 2), crossed(high)


ORDER = ((2, 0), (2, 1), (1, 0), (1, 1), (3, 0), (3, 1), (0, 0), (0, 1))


def in_order(refs, out_ref):
    me, after, before, far_low, far_high = refs
    for place, (step, half) in enumerate(ORDER):
        ref = (me, after, far_high if half else far_low, before)[step]
        start = 0 if step == 2 else half * QUARTER
        out_ref[place * QUARTER : (place + 1) * QUARTER, :] = ref[start : start + QUARTER, :]


def images_kernel(me, after, before, far_low, far_high, out_ref):
    in_order((me, after, before, far_low, far_high), out_ref)
    lane = lax.broadcasted_iota(jnp.int32, (EXTRA, E), 1)
    carried = [ref[start:, :].astype(F32) for ref, start in (
        (me, HALF), (after, HALF), (far_high, QUARTER), (before, HALF)
    )]
    total = jnp.zeros((EXTRA, E), F32)
    for place, (step, half) in enumerate(ORDER):
        inside = (lane >= half * QUARTER) & (lane < (half + 1) * QUARTER)
        piece = jnp.where(inside, carried[step], 0.0)
        total += pltpu.roll(piece, (place - half) * QUARTER % E, 1)
    out_ref[TILE:, :] = total.astype(BF16)


def coefficients(where_ref, scale_ref, shift_ref, images_ref, texts_ref, coef_ref):
    _, _, z, xh, y, text_quarter = position(where_ref)
    parts = images_ref[TILE:, :TILE].astype(F32)
    partner = (parts[0:1] * 128.0 + parts[1:2]).astype(jnp.int32)
    scale, shift = jnp.exp(jnp.full((1, 1), scale_ref[0], F32)), shift_ref[0]
    row = lax.broadcasted_iota(jnp.int32, (TILE, 1), 0)
    index = row
    for place, (step, half) in enumerate(ORDER):
        block = (z * 2 + (1 - xh if half else xh)) * 4 + lax.rem(y + step, 4)
        start = block * ROWS + text_quarter * QUARTER
        index = jnp.where(row // QUARTER == place, row + (start - place * QUARTER), index)
    logits = scale * lax.dot_general(
        texts_ref[...], images_ref[:TILE, :], NT, preferred_element_type=F32
    ) + shift
    own = index == partner
    slopes = jnp.where(own, -scale, scale) / (1.0 + jnp.exp(jnp.where(own, logits, -logits)))
    coef_ref[...] = slopes.astype(BF16)


def image_terms(coef_ref, texts_ref, part):
    return lax.dot_general(
        coef_ref[:, part * ROWS : (part + 1) * ROWS], texts_ref[...], TN,
        preferred_element_type=F32,
    )


def share_out(got, outs):
    start = 0
    for out in outs:
        out[...] = got[start : start + out.shape[0]]
        start += out.shape[0]


def own_kernel(
    where_ref, scale_ref, shift_ref, me, after, before, far_low, far_high, images_ref, early_a, early_b,
    texts_ref, coef_ref,
):
    in_order((me, after, before, far_low, far_high), texts_ref)
    coefficients(where_ref, scale_ref, shift_ref, images_ref, texts_ref, coef_ref)


def given_kernel(where_ref, scale_ref, shift_ref, texts_ref, images_ref, coef_ref, given_ref):
    coefficients(where_ref, scale_ref, shift_ref, images_ref, texts_ref, coef_ref)
    given_ref[...] = image_terms(coef_ref, texts_ref, 0)


def given_rest_kernel(texts_ref, coef_ref, given_ref):
    given_ref[...] = image_terms(coef_ref, texts_ref, 1)


def text_kernel(part, own_coef, images_ref, others_coef, others_ref, *outs):
    rows = slice(part * ROWS, (part + 1) * ROWS)
    got = jnp.dot(own_coef[rows, :], images_ref[:TILE, :], preferred_element_type=F32)
    got += jnp.dot(others_coef[rows, :], others_ref[:TILE, :], preferred_element_type=F32)
    share_out(got, outs)


def kept_kernel(part, texts_ref, coef_ref, taken_ref, *outs):
    share_out(image_terms(coef_ref, texts_ref, part) + taken_ref[...], outs)


def back_kernel(*refs):
    *inputs, out_ref = refs
    for tower in range(2):
        mine, right, left, far, got, emb, inverse = inputs[tower * 7 : tower * 7 + 7]
        gradients = mine[:QUARTER, :] + right[:QUARTER, :] + left[:QUARTER, :]
        gradients += far[...] + got[...]
        widened = emb[:QUARTER, :].astype(F32)
        inner_sum = jnp.sum(widened * gradients, axis=1, keepdims=True)
        value = (inverse[:, :1] * (gradients - widened * inner_sum)).astype(BF16)
        for i in range(4):
            out_ref[i, tower * QUARTER : (tower + 1) * QUARTER, :] = value[
                :, i * SLICE : (i + 1) * SLICE
            ]


def terms_kernel(images_ref, texts_ref, backs_ref, out_ref, both_ref):
    for i in range(4):
        for part in range(2):
            both_ref[part, i * QUARTER : (i + 1) * QUARTER, :] = backs_ref[
                i, part * QUARTER : (part + 1) * QUARTER, :
            ]
    rows = STEP * GROUP
    steps = 128 // STEP
    last = images_ref.shape[0] // rows - 1
    first = steps - texts_ref.shape[0] // rows
    for step in range(steps):
        terms = jnp.zeros((rows, SLICE), F32)
        if step <= last:
            terms += jnp.dot(
                images_ref[step * rows : (step + 1) * rows, :], both_ref[0],
                preferred_element_type=F32,
            )
        if step >= first:
            terms += jnp.dot(
                texts_ref[(step - first) * rows : (step - first + 1) * rows, :], both_ref[1],
                preferred_element_type=F32,
            )
        terms = terms.reshape(STEP, GROUP, SLICE)
        largest = jnp.max(jnp.max(jnp.abs(terms), axis=1), axis=1, keepdims=True)
        exponent = jnp.ceil(jnp.log(jnp.maximum(largest, 1e-30)) * (1.0 / OCTAVE) + 0.01)
        factor = 32767.0 * jnp.exp(exponent * -OCTAVE)
        row = lax.broadcasted_iota(jnp.int32, terms.shape, 1)
        coded = jnp.where(row == OWN, exponent[:, :, None], jnp.round(terms * factor[:, :, None]))
        out_ref[step * STEP : (step + 1) * STEP] = coded.astype(jnp.int32).astype(jnp.int16)


def total_kernel(coded_ref, out_ref):
    for part in range(4):
        total = jnp.zeros((GROUP, SLICE), F32)
        for i in range(32):
            terms = coded_ref[part * 32 + i].astype(jnp.int32).astype(F32)
            total += terms * (jnp.exp(terms[OWN : OWN + 1, :] * OCTAVE) * (1.0 / 32767.0))
        out_ref[:, part * SLICE : (part + 1) * SLICE] = total[:OWN]


def groups_kernel(where_ref, image_feats, text_feats, early, image_out, text_out, held_ref):
    def fill(feats_ref, out_ref, starts, start, first):
        depth = feats_ref.shape[1]
        for i, at in enumerate(starts):
            held_ref[i * QUARTER : (i + 1) * QUARTER, :depth] = feats_ref[at, :]
        for i in range(out_ref.shape[0] // (STEP * GROUP)):
            begin = (first + i) * STEP * OWN - start
            low = min(max(begin // 128 * 128, 0), depth - ROWS)
            row = lax.broadcasted_iota(jnp.int32, (STEP * GROUP, ROWS), 0)
            lane = lax.broadcasted_iota(jnp.int32, (STEP * GROUP, ROWS), 1)
            inside = lax.rem(row, GROUP)
            wanted = lax.div(row, GROUP) * OWN + inside + (begin - low)
            select = jnp.where((inside < OWN) & (wanted == lane), 1.0, 0.0).astype(BF16)
            out_ref[i * STEP * GROUP : (i + 1) * STEP * GROUP, :] = lax.dot_general(
                select, held_ref[:, low : low + ROWS], NT, preferred_element_type=F32
            ).astype(BF16)

    width = image_feats.shape[1]
    quarters = [pl.ds(i * QUARTER, QUARTER) for i in (0, 2, 1, 3)]
    fill(image_feats, image_out, quarters, 0, 0)
    _, _, _, xh, _, _ = position(where_ref)
    half = [xh, xh, 1 - xh, 1 - xh]
    quarters = [
        pl.ds(pl.multiple_of(half[i] * HALF + i % 2 * QUARTER, QUARTER), QUARTER) for i in range(4)
    ]
    fill(text_feats, text_out, quarters, width, width // OWN // STEP)


def body(image_feats, text_feats, image_weight, text_weight, partner, log_scale, logit_bias):
    where = lax.axis_index(AXES).astype(jnp.int32).reshape(1)
    depth = image_feats.shape[1]
    own_texts, text_inverse, load, image_inverse = call(
        embed_kernel,
        [
            shape(QUARTER, E, dtype=BF16), shape(QUARTER, 128),
            shape(HALF + EXTRA, E, dtype=BF16), shape(QUARTER, 128),
        ],
        2 * (QUARTER * E + HALF * depth) * E, 8 << 20, 60,
        in_specs=[SMEM, VMEM] + [ANY] * 4, out_specs=[VMEM] * 4,
        scratch_shapes=[
            pltpu.VMEM((QUARTER, E), BF16), pltpu.VMEM((HALF, depth), BF16),
            pltpu.VMEM((E, E), BF16), pltpu.VMEM((depth, E), BF16),
            pltpu.VMEM((QUARTER, E), F32), pltpu.VMEM((HALF, E), F32),
            pltpu.SemaphoreType.DMA((11,)),
        ],
    )(where, partner.reshape(3, 128), text_feats, image_feats, text_weight, image_weight)
    other_texts = lax.ppermute(own_texts, ("xl", "xh"), FLIP)
    pair = jnp.concatenate([own_texts, other_texts], 0)
    image_pieces, text_pieces = ring_gather(load, "z"), ring_gather(pair, "y")
    images = call(
        images_kernel, shape(TILE + EXTRA, E, dtype=BF16), 0, 4 << 20,
        in_specs=[VMEM] * 5, out_specs=VMEM,
    )(*image_pieces)
    others = lax.ppermute(images, "core", SWAP)

    last, first = (depth - 1) // OWN // STEP, depth // OWN // STEP
    image_groups, text_groups = call(
        groups_kernel,
        [
            shape((last + 1) * STEP * GROUP, ROWS, dtype=BF16),
            shape((128 // STEP - first) * STEP * GROUP, ROWS, dtype=BF16),
        ],
        2 * 17 * STEP * GROUP * ROWS * ROWS, 5 << 20,
        in_specs=[SMEM, VMEM, VMEM, ANY], out_specs=[VMEM] * 2,
        scratch_shapes=[pltpu.VMEM((ROWS, depth), BF16)],
    )(where, image_feats, text_feats, image_pieces[2])

    flops = 2 * TILE * TILE * E
    coef, texts = shape(TILE, TILE, dtype=BF16), shape(TILE, E, dtype=BF16)
    ways = [shape(QUARTER, E)] * 2 + [shape(HALF, E)]
    rest = [shape(HALF, E)] * 2

    def run(kernel, outs, share, count, *options):
        return call(
            lambda *refs: kernel(*options, *refs), outs, int(share * flops), 6 << 20, 24,
            in_specs=[VMEM] * count, out_specs=[VMEM] * len(outs),
        )

    texts, own_coef = call(
        own_kernel, [texts, coef], 16 * flops, 6 << 20, 24,
        in_specs=[SMEM] * 3 + [VMEM] * 6 + [ANY] * 2, out_specs=[VMEM] * 2,
    )(where, log_scale, logit_bias, *text_pieces, images, image_groups, text_groups)
    others_coef, given = call(
        given_kernel, [coef, shape(ROWS, E)], 2 * flops, 8 << 20, 24,
        in_specs=[SMEM] * 3 + [VMEM] * 2, out_specs=[VMEM] * 2,
    )(where, log_scale, logit_bias, texts, others)
    taken = lax.ppermute(given, "core", SWAP)
    sides = own_coef, images, others_coef, others
    text_ways = run(text_kernel, ways, 1, 4, 0)(*sides)
    given_rest, = run(given_rest_kernel, [shape(ROWS, E)], 0.5, 2)(texts, others_coef)
    taken_rest = lax.ppermute(given_rest, "core", SWAP)
    image_ways = run(kept_kernel, ways, 0.5, 3, 0)(texts, own_coef, taken)
    text_rest = run(text_kernel, rest, 8, 4, 1)(*sides)
    image_rest = run(kept_kernel, rest, 0.5, 3, 1)(texts, own_coef, taken_rest)
    text_sums = ring_scatter(
        *text_ways, *text_rest, "y", lambda a: lax.ppermute(a, ("xl", "xh"), FLIP)
    )
    image_sums = ring_scatter(
        *image_ways, *image_rest, "z", lambda a: lax.ppermute(a, "xl", SWAP)
    )

    backs = call(
        back_kernel, shape(4, HALF, SLICE, dtype=BF16), 0, 6 << 20,
        in_specs=[VMEM] * 14, out_specs=VMEM,
    )(*image_sums, load, image_inverse, *text_sums, own_texts, text_inverse)
    backs = lax.all_to_all(backs, TOWER, split_axis=0, concat_axis=0, tiled=True)

    coded = call(
        terms_kernel, shape(128, GROUP, SLICE, dtype=jnp.int16),
        4 * 128 * GROUP * ROWS * SLICE, 6 << 20, 24,
        in_specs=[VMEM] * 3, out_specs=VMEM,
        scratch_shapes=[pltpu.VMEM((2, ROWS, SLICE), BF16)],
    )(image_groups, text_groups, backs)
    coded = lax.all_to_all(coded, AXES, split_axis=0, concat_axis=0, tiled=True)
    return call(total_kernel, shape(OWN, E), 0, 2 << 20, in_specs=[VMEM], out_specs=VMEM)(coded)


def solution(mesh):
    fine = Mesh(mesh.devices.reshape([SIZES[a] for a in AXES]), AXES)
    placed = (P(DP, None), P(DP, None), P(), P(), P(DP), P(), P())
    return jax.shard_map(
        body, mesh=fine, in_specs=placed, out_specs=P(TOWER + DP, None), check_vma=False
    )
```

```python
import math

import jax
import jax.numpy as jnp
from jax import lax
from jax.experimental import pallas as pl
from jax.experimental.pallas import tpu as pltpu
from jax.sharding import Mesh, PartitionSpec as P

AXES = ("xl", "core", "z", "xh", "y")
SIZES = {"xl": 2, "core": 2, "z": 4, "xh": 2, "y": 4}
DP = ("z", "xh", "y")
TOWER = ("xl", "core")
SWAP = [(0, 1), (1, 0)]
FLIP = [(0, 3), (1, 2), (2, 1), (3, 0)]
ROWS = 384
HALF, QUARTER = 192, 96
EXTRA = 16
E = 1024
TILE = 4 * HALF
OWN = 21
GROUP = 24
SLICE = E // 4
STEP = 8
NT = (((1,), (1,)), ((), ()))
TN = (((0,), (0,)), ((), ()))
OCTAVE = math.log(2.0) / 16.0
F32, BF16 = jnp.float32, jnp.bfloat16


def shifted(array, axis, by):
    return lax.ppermute(array, axis, [(i, (i + by) % 4) for i in range(4)])


def call(kernel, outs, flops, moved, limit=16, **options):
    return pl.pallas_call(
        kernel,
        out_shape=outs,
        cost_estimate=pl.CostEstimate(flops=flops, bytes_accessed=moved, transcendentals=0),
        compiler_params=pltpu.CompilerParams(vmem_limit_bytes=limit << 20),
        **options,
    )


def shape(*dims, dtype=F32):
    return jax.ShapeDtypeStruct(dims, dtype)


VMEM = pl.BlockSpec(memory_space=pltpu.VMEM)
SMEM = pl.BlockSpec(memory_space=pltpu.SMEM)
ANY = pl.BlockSpec(memory_space=pl.ANY)


def position(where_ref):
    index = where_ref[0]
    xl, core, z, xh, y = index // 64, index // 32 % 2, index // 8 % 4, index // 4 % 2, index % 4
    return xl, core, z, xh, y, (xl + xh) % 2 * 2 + core


def normalised(pre_ref, inverse_ref):
    pre = pre_ref[...]
    total = jnp.sum(pre * pre, axis=1, keepdims=True)
    inverse = lax.rsqrt(total + 1e-06).astype(BF16).astype(F32)
    inverse_ref[...] = jnp.broadcast_to(inverse[:QUARTER], (QUARTER, 128))
    return (pre * inverse).astype(BF16)


def embed_kernel(
    where_ref, partner_ref, text_feats, image_feats, text_weight, image_weight,
    text_ref, text_inverse, load_ref, image_inverse,
    text_rows, image_rows, text_held, image_held, text_pre, image_pre, sems,
):
    count = 0

    def begin(source, target):
        nonlocal count
        copy = pltpu.make_async_copy(source, target, sems.at[count])
        copy.start()
        count += 1
        return copy

    xl, core, _, _, _, text_quarter = position(where_ref)
    places = core * 2 + xl, core * 2 + 1 - xl

    def rows(place):
        return pl.ds(pl.multiple_of(place * QUARTER, QUARTER), QUARTER)

    def begin_weight(weight, held, ends):
        spans = [slice(a, b) for a, b in zip((0,) + ends, ends)]
        return [(span, begin(weight.at[span], held.at[span])) for span in spans]

    def project(rows_ref, held, waits, pre_ref):
        for i, (span, copy) in enumerate(waits):
            copy.wait()
            got = jnp.dot(rows_ref[:, span], held[span, :], preferred_element_type=F32)
            pre_ref[...] = got if i == 0 else pre_ref[...] + got

    text_copy = begin(text_feats.at[rows(text_quarter)], text_rows)
    text_waits = begin_weight(text_weight, text_held, (256, 512, 768, 1024))
    image_copies = [
        begin(image_feats.at[rows(place)], image_rows.at[i * QUARTER : (i + 1) * QUARTER])
        for i, place in enumerate(places)
    ]
    image_waits = begin_weight(image_weight, image_held, (384, 768, 1152, 1664))

    text_copy.wait()
    project(text_rows, text_held, text_waits, text_pre)
    text_ref[...] = normalised(text_pre, text_inverse)
    for copy in image_copies:
        copy.wait()
    project(image_rows, image_held, image_waits, image_pre)
    load_ref[:HALF, :] = normalised(image_pre, image_inverse)

    partner = jnp.concatenate([partner_ref[i : i + 1, :] for i in range(3)], 1).astype(F32)
    partner = jnp.broadcast_to(partner, (EXTRA, ROWS))
    lane = lax.broadcasted_iota(jnp.int32, (EXTRA, ROWS), 1)
    row = lax.broadcasted_iota(jnp.int32, (EXTRA, ROWS), 0)
    chosen = jnp.zeros((EXTRA, ROWS), F32)
    for i, place in enumerate(places):
        moved = pltpu.roll(partner, (i + 4 - place) % 4 * QUARTER, 1)
        chosen = jnp.where(lane // QUARTER == i, moved, chosen)
    high = jnp.floor(chosen * (1.0 / 128.0))
    parts = jnp.where(row == 0, high, jnp.where(row == 1, chosen - 128.0 * high, 0.0))
    load_ref[HALF:, :] = jnp.zeros((EXTRA, E), BF16)
    load_ref[HALF:, :ROWS] = parts.astype(BF16)


def ring_gather(block, axis):
    before, after = shifted(block, axis, 1), shifted(block, axis, -1)
    far_low = shifted(before[:QUARTER], axis, 1)
    far_high = shifted(after[QUARTER:], axis, -1)
    return block, after, before, far_low, far_high


def far_kernel(low_ref, high_ref, early_ref, out_ref):
    out_ref[...] = low_ref[...] + high_ref[...]


def add_kernel(low_ref, high_ref, out_ref):
    out_ref[...] = low_ref[...] + high_ref[...]


def behind_kernel(far_ref, early_ref, out_ref):
    out_ref[...] = far_ref[...]


def ring_scatter(far_low, far_high, after, before, mine, axis, crossed):
    far = crossed(far_high)
    got_right, got_left = shifted(after, axis, 1), shifted(before, axis, -1)
    if axis == "z":
        far = call(
            far_kernel, shape(QUARTER, E), 0, 1 << 20, in_specs=[VMEM, VMEM, ANY], out_specs=VMEM
        )(far_low, far, got_left)
    else:
        far = call(
            add_kernel, shape(QUARTER, E), 4 << 30, 1 << 20, in_specs=[VMEM] * 2, out_specs=VMEM
        )(far_low, far)
        far = call(
            behind_kernel, shape(QUARTER, E), 0, 1 << 20, in_specs=[VMEM, ANY], out_specs=VMEM
        )(far, got_left)
    high = mine[QUARTER:] + got_right[QUARTER:] + got_left[QUARTER:]
    return mine, got_right, got_left, shifted(far, axis, 2), crossed(high)


ORDER = ((2, 0), (2, 1), (1, 0), (1, 1), (3, 0), (3, 1), (0, 0), (0, 1))


def in_order(refs, out_ref):
    me, after, before, far_low, far_high = refs
    for place, (step, half) in enumerate(ORDER):
        ref = (me, after, far_high if half else far_low, before)[step]
        start = 0 if step == 2 else half * QUARTER
        out_ref[place * QUARTER : (place + 1) * QUARTER, :] = ref[start : start + QUARTER, :]


def images_kernel(me, after, before, far_low, far_high, out_ref):
    in_order((me, after, before, far_low, far_high), out_ref)
    lane = lax.broadcasted_iota(jnp.int32, (EXTRA, E), 1)
    carried = [ref[start:, :].astype(F32) for ref, start in (
        (me, HALF), (after, HALF), (far_high, QUARTER), (before, HALF)
    )]
    total = jnp.zeros((EXTRA, E), F32)
    for place, (step, half) in enumerate(ORDER):
        inside = (lane >= half * QUARTER) & (lane < (half + 1) * QUARTER)
        piece = jnp.where(inside, carried[step], 0.0)
        total += pltpu.roll(piece, (place - half) * QUARTER % E, 1)
    out_ref[TILE:, :] = total.astype(BF16)


def coefficients(where_ref, scale_ref, shift_ref, images_ref, texts_ref, coef_ref):
    _, _, z, xh, y, text_quarter = position(where_ref)
    parts = images_ref[TILE:, :TILE].astype(F32)
    partner = (parts[0:1] * 128.0 + parts[1:2]).astype(jnp.int32)
    scale, shift = jnp.exp(jnp.full((1, 1), scale_ref[0], F32)), shift_ref[0]
    row = lax.broadcasted_iota(jnp.int32, (TILE, 1), 0)
    index = row
    for place, (step, half) in enumerate(ORDER):
        block = (z * 2 + (1 - xh if half else xh)) * 4 + lax.rem(y + step, 4)
        start = block * ROWS + text_quarter * QUARTER
        index = jnp.where(row // QUARTER == place, row + (start - place * QUARTER), index)
    logits = scale * lax.dot_general(
        texts_ref[...], images_ref[:TILE, :], NT, preferred_element_type=F32
    ) + shift
    own = index == partner
    slopes = jnp.where(own, -scale, scale) / (1.0 + jnp.exp(jnp.where(own, logits, -logits)))
    coef_ref[...] = slopes.astype(BF16)


def image_terms(coef_ref, texts_ref, part):
    return lax.dot_general(
        coef_ref[:, part * ROWS : (part + 1) * ROWS], texts_ref[...], TN,
        preferred_element_type=F32,
    )


def share_out(got, outs):
    start = 0
    for out in outs:
        out[...] = got[start : start + out.shape[0]]
        start += out.shape[0]


def own_kernel(
    where_ref, scale_ref, shift_ref, me, after, before, far_low, far_high, images_ref, early_a, early_b,
    texts_ref, coef_ref,
):
    in_order((me, after, before, far_low, far_high), texts_ref)
    coefficients(where_ref, scale_ref, shift_ref, images_ref, texts_ref, coef_ref)


def given_kernel(where_ref, scale_ref, shift_ref, texts_ref, images_ref, coef_ref, given_ref):
    coefficients(where_ref, scale_ref, shift_ref, images_ref, texts_ref, coef_ref)
    given_ref[...] = image_terms(coef_ref, texts_ref, 0)


def given_rest_kernel(texts_ref, coef_ref, given_ref):
    given_ref[...] = image_terms(coef_ref, texts_ref, 1)


def text_kernel(part, own_coef, images_ref, others_coef, others_ref, *outs):
    rows = slice(part * ROWS, (part + 1) * ROWS)
    got = jnp.dot(own_coef[rows, :], images_ref[:TILE, :], preferred_element_type=F32)
    got += jnp.dot(others_coef[rows, :], others_ref[:TILE, :], preferred_element_type=F32)
    share_out(got, outs)


def kept_kernel(part, texts_ref, coef_ref, taken_ref, *outs):
    share_out(image_terms(coef_ref, texts_ref, part) + taken_ref[...], outs)


def back_kernel(*refs):
    *inputs, out_ref = refs
    for tower in range(2):
        mine, right, left, far, got, emb, inverse = inputs[tower * 7 : tower * 7 + 7]
        gradients = mine[:QUARTER, :] + right[:QUARTER, :] + left[:QUARTER, :]
        gradients += far[...] + got[...]
        widened = emb[:QUARTER, :].astype(F32)
        inner_sum = jnp.sum(widened * gradients, axis=1, keepdims=True)
        value = (inverse[:, :1] * (gradients - widened * inner_sum)).astype(BF16)
        for i in range(4):
            out_ref[i, tower * QUARTER : (tower + 1) * QUARTER, :] = value[
                :, i * SLICE : (i + 1) * SLICE
            ]


def terms_kernel(images_ref, texts_ref, backs_ref, out_ref, both_ref):
    for i in range(4):
        for part in range(2):
            both_ref[part, i * QUARTER : (i + 1) * QUARTER, :] = backs_ref[
                i, part * QUARTER : (part + 1) * QUARTER, :
            ]
    rows = STEP * GROUP
    steps = 128 // STEP
    last = images_ref.shape[0] // rows - 1
    first = steps - texts_ref.shape[0] // rows
    for step in range(steps):
        terms = jnp.zeros((rows, SLICE), F32)
        if step <= last:
            terms += jnp.dot(
                images_ref[step * rows : (step + 1) * rows, :], both_ref[0],
                preferred_element_type=F32,
            )
        if step >= first:
            terms += jnp.dot(
                texts_ref[(step - first) * rows : (step - first + 1) * rows, :], both_ref[1],
                preferred_element_type=F32,
            )
        terms = terms.reshape(STEP, GROUP, SLICE)
        largest = jnp.max(jnp.max(jnp.abs(terms), axis=1), axis=1, keepdims=True)
        exponent = jnp.ceil(jnp.log(jnp.maximum(largest, 1e-30)) * (1.0 / OCTAVE) + 0.01)
        factor = 32767.0 * jnp.exp(exponent * -OCTAVE)
        row = lax.broadcasted_iota(jnp.int32, terms.shape, 1)
        coded = jnp.where(row == OWN, exponent[:, :, None], jnp.round(terms * factor[:, :, None]))
        out_ref[step * STEP : (step + 1) * STEP] = coded.astype(jnp.int32).astype(jnp.int16)


def total_kernel(coded_ref, out_ref):
    for part in range(4):
        total = jnp.zeros((GROUP, SLICE), F32)
        for i in range(32):
            terms = coded_ref[part * 32 + i].astype(jnp.int32).astype(F32)
            total += terms * (jnp.exp(terms[OWN : OWN + 1, :] * OCTAVE) * (1.0 / 32767.0))
        out_ref[:, part * SLICE : (part + 1) * SLICE] = total[:OWN]


def groups_kernel(where_ref, image_feats, text_feats, early, image_out, text_out, held_ref):
    def fill(feats_ref, out_ref, starts, start, first):
        depth = feats_ref.shape[1]
        for i, at in enumerate(starts):
            held_ref[i * QUARTER : (i + 1) * QUARTER, :depth] = feats_ref[at, :]
        for i in range(out_ref.shape[0] // (STEP * GROUP)):
            begin = (first + i) * STEP * OWN - start
            low = min(max(begin // 128 * 128, 0), depth - ROWS)
            row = lax.broadcasted_iota(jnp.int32, (STEP * GROUP, ROWS), 0)
            lane = lax.broadcasted_iota(jnp.int32, (STEP * GROUP, ROWS), 1)
            inside = lax.rem(row, GROUP)
            wanted = lax.div(row, GROUP) * OWN + inside + (begin - low)
            select = jnp.where((inside < OWN) & (wanted == lane), 1.0, 0.0).astype(BF16)
            out_ref[i * STEP * GROUP : (i + 1) * STEP * GROUP, :] = lax.dot_general(
                select, held_ref[:, low : low + ROWS], NT, preferred_element_type=F32
            ).astype(BF16)

    width = image_feats.shape[1]
    quarters = [pl.ds(i * QUARTER, QUARTER) for i in (0, 2, 1, 3)]
    fill(image_feats, image_out, quarters, 0, 0)
    _, _, _, xh, _, _ = position(where_ref)
    half = [xh, xh, 1 - xh, 1 - xh]
    quarters = [
        pl.ds(pl.multiple_of(half[i] * HALF + i % 2 * QUARTER, QUARTER), QUARTER) for i in range(4)
    ]
    fill(text_feats, text_out, quarters, width, width // OWN // STEP)


def body(image_feats, text_feats, image_weight, text_weight, partner, log_scale, logit_bias):
    where = lax.axis_index(AXES).astype(jnp.int32).reshape(1)
    depth = image_feats.shape[1]
    own_texts, text_inverse, load, image_inverse = call(
        embed_kernel,
        [
            shape(QUARTER, E, dtype=BF16), shape(QUARTER, 128),
            shape(HALF + EXTRA, E, dtype=BF16), shape(QUARTER, 128),
        ],
        2 * (QUARTER * E + HALF * depth) * E, 8 << 20, 60,
        in_specs=[SMEM, VMEM] + [ANY] * 4, out_specs=[VMEM] * 4,
        scratch_shapes=[
            pltpu.VMEM((QUARTER, E), BF16), pltpu.VMEM((HALF, depth), BF16),
            pltpu.VMEM((E, E), BF16), pltpu.VMEM((depth, E), BF16),
            pltpu.VMEM((QUARTER, E), F32), pltpu.VMEM((HALF, E), F32),
            pltpu.SemaphoreType.DMA((11,)),
        ],
    )(where, partner.reshape(3, 128), text_feats, image_feats, text_weight, image_weight)
    other_texts = lax.ppermute(own_texts, ("xl", "xh"), FLIP)
    pair = jnp.concatenate([own_texts, other_texts], 0)
    image_pieces, text_pieces = ring_gather(load, "z"), ring_gather(pair, "y")
    images = call(
        images_kernel, shape(TILE + EXTRA, E, dtype=BF16), 0, 4 << 20,
        in_specs=[VMEM] * 5, out_specs=VMEM,
    )(*image_pieces)
    others = lax.ppermute(images, "core", SWAP)

    last, first = (depth - 1) // OWN // STEP, depth // OWN // STEP
    image_groups, text_groups = call(
        groups_kernel,
        [
            shape((last + 1) * STEP * GROUP, ROWS, dtype=BF16),
            shape((128 // STEP - first) * STEP * GROUP, ROWS, dtype=BF16),
        ],
        2 * 17 * STEP * GROUP * ROWS * ROWS, 5 << 20,
        in_specs=[SMEM, VMEM, VMEM, ANY], out_specs=[VMEM] * 2,
        scratch_shapes=[pltpu.VMEM((ROWS, depth), BF16)],
    )(where, image_feats, text_feats, image_pieces[2])

    flops = 2 * TILE * TILE * E
    coef, texts = shape(TILE, TILE, dtype=BF16), shape(TILE, E, dtype=BF16)
    ways = [shape(QUARTER, E)] * 2 + [shape(HALF, E)]
    rest = [shape(HALF, E)] * 2

    def run(kernel, outs, share, count, *options):
        return call(
            lambda *refs: kernel(*options, *refs), outs, int(share * flops), 6 << 20, 24,
            in_specs=[VMEM] * count, out_specs=[VMEM] * len(outs),
        )

    texts, own_coef = call(
        own_kernel, [texts, coef], 16 * flops, 6 << 20, 24,
        in_specs=[SMEM] * 3 + [VMEM] * 6 + [ANY] * 2, out_specs=[VMEM] * 2,
    )(where, log_scale, logit_bias, *text_pieces, images, image_groups, text_groups)
    others_coef, given = call(
        given_kernel, [coef, shape(ROWS, E)], 2 * flops, 8 << 20, 24,
        in_specs=[SMEM] * 3 + [VMEM] * 2, out_specs=[VMEM] * 2,
    )(where, log_scale, logit_bias, texts, others)
    taken = lax.ppermute(given, "core", SWAP)
    sides = own_coef, images, others_coef, others
    text_ways = run(text_kernel, ways, 1, 4, 0)(*sides)
    given_rest, = run(given_rest_kernel, [shape(ROWS, E)], 0.5, 2)(texts, others_coef)
    taken_rest = lax.ppermute(given_rest, "core", SWAP)
    image_ways = run(kept_kernel, ways, 0.5, 3, 0)(texts, own_coef, taken)
    text_rest = run(text_kernel, rest, 8, 4, 1)(*sides)
    image_rest = run(kept_kernel, rest, 0.5, 3, 1)(texts, own_coef, taken_rest)
    text_sums = ring_scatter(
        *text_ways, *text_rest, "y", lambda a: lax.ppermute(a, ("xl", "xh"), FLIP)
    )
    image_sums = ring_scatter(
        *image_ways, *image_rest, "z", lambda a: lax.ppermute(a, "xl", SWAP)
    )

    backs = call(
        back_kernel, shape(4, HALF, SLICE, dtype=BF16), 0, 6 << 20,
        in_specs=[VMEM] * 14, out_specs=VMEM,
    )(*image_sums, load, image_inverse, *text_sums, own_texts, text_inverse)
    backs = lax.all_to_all(backs, TOWER, split_axis=0, concat_axis=0, tiled=True)

    coded = call(
        terms_kernel, shape(128, GROUP, SLICE, dtype=jnp.int16),
        4 * 128 * GROUP * ROWS * SLICE, 6 << 20, 24,
        in_specs=[VMEM] * 3, out_specs=VMEM,
        scratch_shapes=[pltpu.VMEM((2, ROWS, SLICE), BF16)],
    )(image_groups, text_groups, backs)
    coded = lax.all_to_all(coded, AXES, split_axis=0, concat_axis=0, tiled=True)
    return call(total_kernel, shape(OWN, E), 0, 2 << 20, in_specs=[VMEM], out_specs=VMEM)(coded)


def solution(mesh):
    fine = Mesh(mesh.devices.reshape([SIZES[a] for a in AXES]), AXES)
    placed = (P(DP, None), P(DP, None), P(), P(), P(DP), P(), P())
    return jax.shard_map(
        body, mesh=fine, in_specs=placed, out_specs=P(TOWER + DP, None), check_vma=False
    )
```

```python
import math

import jax
import jax.numpy as jnp
from jax import lax
from jax.experimental import pallas as pl
from jax.experimental.pallas import tpu as pltpu
from jax.sharding import Mesh, PartitionSpec as P

AXES = ("xl", "core", "z", "xh", "y")
SIZES = {"xl": 2, "core": 2, "z": 4, "xh": 2, "y": 4}
DP = ("z", "xh", "y")
TOWER = ("xl", "core")
SWAP = [(0, 1), (1, 0)]
FLIP = [(0, 3), (1, 2), (2, 1), (3, 0)]
ROWS = 384
HALF, QUARTER = 192, 96
EXTRA = 16
E = 1024
TILE = 4 * HALF
OWN = 21
GROUP = 24
SLICE = E // 4
STEP = 8
NT = (((1,), (1,)), ((), ()))
TN = (((0,), (0,)), ((), ()))
OCTAVE = math.log(2.0) / 16.0
F32, BF16 = jnp.float32, jnp.bfloat16


def shifted(array, axis, by):
    return lax.ppermute(array, axis, [(i, (i + by) % 4) for i in range(4)])


def call(kernel, outs, flops, moved, limit=16, **options):
    return pl.pallas_call(
        kernel,
        out_shape=outs,
        cost_estimate=pl.CostEstimate(flops=flops, bytes_accessed=moved, transcendentals=0),
        compiler_params=pltpu.CompilerParams(vmem_limit_bytes=limit << 20),
        **options,
    )


def shape(*dims, dtype=F32):
    return jax.ShapeDtypeStruct(dims, dtype)


VMEM = pl.BlockSpec(memory_space=pltpu.VMEM)
SMEM = pl.BlockSpec(memory_space=pltpu.SMEM)
ANY = pl.BlockSpec(memory_space=pl.ANY)


def position(where_ref):
    index = where_ref[0]
    xl, core, z, xh, y = index // 64, index // 32 % 2, index // 8 % 4, index // 4 % 2, index % 4
    return xl, core, z, xh, y, (xl + xh) % 2 * 2 + core


def normalised(pre_ref, inverse_ref):
    pre = pre_ref[...]
    total = jnp.sum(pre * pre, axis=1, keepdims=True)
    inverse = lax.rsqrt(total + 1e-06).astype(BF16).astype(F32)
    inverse_ref[...] = jnp.broadcast_to(inverse[:QUARTER], (QUARTER, 128))
    return (pre * inverse).astype(BF16)


def embed_kernel(
    where_ref, partner_ref, text_feats, image_feats, text_weight, image_weight,
    text_ref, text_inverse, load_ref, image_inverse,
    text_rows, image_rows, text_held, image_held, text_pre, image_pre, sems,
):
    count = 0

    def begin(source, target):
        nonlocal count
        copy = pltpu.make_async_copy(source, target, sems.at[count])
        copy.start()
        count += 1
        return copy

    xl, core, _, _, _, text_quarter = position(where_ref)
    places = core * 2 + xl, core * 2 + 1 - xl

    def rows(place):
        return pl.ds(pl.multiple_of(place * QUARTER, QUARTER), QUARTER)

    def begin_weight(weight, held, ends):
        spans = [slice(a, b) for a, b in zip((0,) + ends, ends)]
        return [(span, begin(weight.at[span], held.at[span])) for span in spans]

    def project(rows_ref, held, waits, pre_ref):
        for i, (span, copy) in enumerate(waits):
            copy.wait()
            got = jnp.dot(rows_ref[:, span], held[span, :], preferred_element_type=F32)
            pre_ref[...] = got if i == 0 else pre_ref[...] + got

    text_copy = begin(text_feats.at[rows(text_quarter)], text_rows)
    text_waits = begin_weight(text_weight, text_held, (256, 512, 768, 1024))
    image_copies = [
        begin(image_feats.at[rows(place)], image_rows.at[i * QUARTER : (i + 1) * QUARTER])
        for i, place in enumerate(places)
    ]
    image_waits = begin_weight(image_weight, image_held, (384, 768, 1152, 1664))

    text_copy.wait()
    project(text_rows, text_held, text_waits, text_pre)
    text_ref[...] = normalised(text_pre, text_inverse)
    for copy in image_copies:
        copy.wait()
    project(image_rows, image_held, image_waits, image_pre)
    load_ref[:HALF, :] = normalised(image_pre, image_inverse)

    partner = jnp.concatenate([partner_ref[i : i + 1, :] for i in range(3)], 1).astype(F32)
    partner = jnp.broadcast_to(partner, (EXTRA, ROWS))
    lane = lax.broadcasted_iota(jnp.int32, (EXTRA, ROWS), 1)
    row = lax.broadcasted_iota(jnp.int32, (EXTRA, ROWS), 0)
    chosen = jnp.zeros((EXTRA, ROWS), F32)
    for i, place in enumerate(places):
        moved = pltpu.roll(partner, (i + 4 - place) % 4 * QUARTER, 1)
        chosen = jnp.where(lane // QUARTER == i, moved, chosen)
    high = jnp.floor(chosen * (1.0 / 128.0))
    parts = jnp.where(row == 0, high, jnp.where(row == 1, chosen - 128.0 * high, 0.0))
    load_ref[HALF:, :] = jnp.zeros((EXTRA, E), BF16)
    load_ref[HALF:, :ROWS] = parts.astype(BF16)


def ring_gather(block, axis):
    before, after = shifted(block, axis, 1), shifted(block, axis, -1)
    far_low = shifted(before[:QUARTER], axis, 1)
    far_high = shifted(after[QUARTER:], axis, -1)
    return block, after, before, far_low, far_high


def far_kernel(low_ref, high_ref, early_ref, out_ref):
    out_ref[...] = low_ref[...] + high_ref[...]


def add_kernel(low_ref, high_ref, out_ref):
    out_ref[...] = low_ref[...] + high_ref[...]


def behind_kernel(far_ref, early_ref, out_ref):
    out_ref[...] = far_ref[...]


def ring_scatter(far_low, far_high, after, before, mine, axis, crossed):
    far = crossed(far_high)
    got_right, got_left = shifted(after, axis, 1), shifted(before, axis, -1)
    if axis == "z":
        far = call(
            far_kernel, shape(QUARTER, E), 0, 1 << 20, in_specs=[VMEM, VMEM, ANY], out_specs=VMEM
        )(far_low, far, got_left)
    else:
        far = call(
            add_kernel, shape(QUARTER, E), 4 << 30, 1 << 20, in_specs=[VMEM] * 2, out_specs=VMEM
        )(far_low, far)
        far = call(
            behind_kernel, shape(QUARTER, E), 0, 1 << 20, in_specs=[VMEM, ANY], out_specs=VMEM
        )(far, got_left)
    high = mine[QUARTER:] + got_right[QUARTER:] + got_left[QUARTER:]
    return mine, got_right, got_left, shifted(far, axis, 2), crossed(high)


ORDER = ((2, 0), (2, 1), (1, 0), (1, 1), (3, 0), (3, 1), (0, 0), (0, 1))


def in_order(refs, out_ref):
    me, after, before, far_low, far_high = refs
    for place, (step, half) in enumerate(ORDER):
        ref = (me, after, far_high if half else far_low, before)[step]
        start = 0 if step == 2 else half * QUARTER
        out_ref[place * QUARTER : (place + 1) * QUARTER, :] = ref[start : start + QUARTER, :]


def images_kernel(me, after, before, far_low, far_high, out_ref):
    in_order((me, after, before, far_low, far_high), out_ref)
    lane = lax.broadcasted_iota(jnp.int32, (EXTRA, E), 1)
    carried = [ref[start:, :].astype(F32) for ref, start in (
        (me, HALF), (after, HALF), (far_high, QUARTER), (before, HALF)
    )]
    total = jnp.zeros((EXTRA, E), F32)
    for place, (step, half) in enumerate(ORDER):
        inside = (lane >= half * QUARTER) & (lane < (half + 1) * QUARTER)
        piece = jnp.where(inside, carried[step], 0.0)
        total += pltpu.roll(piece, (place - half) * QUARTER % E, 1)
    out_ref[TILE:, :] = total.astype(BF16)


def coefficients(where_ref, scale_ref, shift_ref, images_ref, texts_ref, coef_ref):
    _, _, z, xh, y, text_quarter = position(where_ref)
    parts = images_ref[TILE:, :TILE].astype(F32)
    partner = (parts[0:1] * 128.0 + parts[1:2]).astype(jnp.int32)
    scale, shift = jnp.exp(jnp.full((1, 1), scale_ref[0], F32)), shift_ref[0]
    row = lax.broadcasted_iota(jnp.int32, (TILE, 1), 0)
    index = row
    for place, (step, half) in enumerate(ORDER):
        block = (z * 2 + (1 - xh if half else xh)) * 4 + lax.rem(y + step, 4)
        start = block * ROWS + text_quarter * QUARTER
        index = jnp.where(row // QUARTER == place, row + (start - place * QUARTER), index)
    logits = scale * lax.dot_general(
        texts_ref[...], images_ref[:TILE, :], NT, preferred_element_type=F32
    ) + shift
    own = index == partner
    slopes = jnp.where(own, -scale, scale) / (1.0 + jnp.exp(jnp.where(own, logits, -logits)))
    coef_ref[...] = slopes.astype(BF16)


def image_terms(coef_ref, texts_ref, part):
    return lax.dot_general(
        coef_ref[:, part * ROWS : (part + 1) * ROWS], texts_ref[...], TN,
        preferred_element_type=F32,
    )


def share_out(got, outs):
    start = 0
    for out in outs:
        out[...] = got[start : start + out.shape[0]]
        start += out.shape[0]


def own_kernel(
    where_ref, scale_ref, shift_ref, me, after, before, far_low, far_high, images_ref, early_a, early_b,
    texts_ref, coef_ref,
):
    in_order((me, after, before, far_low, far_high), texts_ref)
    coefficients(where_ref, scale_ref, shift_ref, images_ref, texts_ref, coef_ref)


def given_kernel(where_ref, scale_ref, shift_ref, texts_ref, images_ref, coef_ref, given_ref):
    coefficients(where_ref, scale_ref, shift_ref, images_ref, texts_ref, coef_ref)
    given_ref[...] = image_terms(coef_ref, texts_ref, 0)


def given_rest_kernel(texts_ref, coef_ref, given_ref):
    given_ref[...] = image_terms(coef_ref, texts_ref, 1)


def text_kernel(part, own_coef, images_ref, others_coef, others_ref, *outs):
    rows = slice(part * ROWS, (part + 1) * ROWS)
    got = jnp.dot(own_coef[rows, :], images_ref[:TILE, :], preferred_element_type=F32)
    got += jnp.dot(others_coef[rows, :], others_ref[:TILE, :], preferred_element_type=F32)
    share_out(got, outs)


def kept_kernel(part, texts_ref, coef_ref, taken_ref, *outs):
    share_out(image_terms(coef_ref, texts_ref, part) + taken_ref[...], outs)


def back_kernel(where_ref, *refs):
    *inputs, own_ref, core_ref, xl_ref, both_ref, held_ref = refs
    for tower in range(2):
        mine, right, left, far, got, emb, inverse = inputs[tower * 7 : tower * 7 + 7]
        gradients = mine[:QUARTER, :] + right[:QUARTER, :] + left[:QUARTER, :]
        gradients += far[...] + got[...]
        widened = emb[:QUARTER, :].astype(F32)
        inner_sum = jnp.sum(widened * gradients, axis=1, keepdims=True)
        value = (inverse[:, :1] * (gradients - widened * inner_sum)).astype(BF16)
        for i in range(4):
            held_ref[i, tower * QUARTER : (tower + 1) * QUARTER, :] = value[
                :, i * SLICE : (i + 1) * SLICE
            ]
    xl, core, _, _, _, _ = position(where_ref)
    own_ref[...] = held_ref[xl * 2 + core]
    core_ref[...] = held_ref[xl * 2 + 1 - core]
    xl_ref[...] = held_ref[2 - xl * 2 + core]
    both_ref[...] = held_ref[3 - xl * 2 - core]


def terms_kernel(images_ref, texts_ref, own, core, xl, both, out_ref, both_ref):
    for i, ref in enumerate((own, core, xl, both)):
        for part in range(2):
            both_ref[part, i * QUARTER : (i + 1) * QUARTER, :] = ref[
                part * QUARTER : (part + 1) * QUARTER, :
            ]
    rows = STEP * GROUP
    steps = 128 // STEP
    last = images_ref.shape[0] // rows - 1
    first = steps - texts_ref.shape[0] // rows
    for step in range(steps):
        terms = jnp.zeros((rows, SLICE), F32)
        if step <= last:
            terms += jnp.dot(
                images_ref[step * rows : (step + 1) * rows, :], both_ref[0],
                preferred_element_type=F32,
            )
        if step >= first:
            terms += jnp.dot(
                texts_ref[(step - first) * rows : (step - first + 1) * rows, :], both_ref[1],
                preferred_element_type=F32,
            )
        terms = terms.reshape(STEP, GROUP, SLICE)
        largest = jnp.max(jnp.max(jnp.abs(terms), axis=1), axis=1, keepdims=True)
        exponent = jnp.ceil(jnp.log(jnp.maximum(largest, 1e-30)) * (1.0 / OCTAVE) + 0.01)
        factor = 32767.0 * jnp.exp(exponent * -OCTAVE)
        row = lax.broadcasted_iota(jnp.int32, terms.shape, 1)
        coded = jnp.where(row == OWN, exponent[:, :, None], jnp.round(terms * factor[:, :, None]))
        out_ref[step * STEP : (step + 1) * STEP] = coded.astype(jnp.int32).astype(jnp.int16)


def total_kernel(coded_ref, out_ref):
    for part in range(4):
        total = jnp.zeros((GROUP, SLICE), F32)
        for i in range(32):
            terms = coded_ref[part * 32 + i].astype(jnp.int32).astype(F32)
            total += terms * (jnp.exp(terms[OWN : OWN + 1, :] * OCTAVE) * (1.0 / 32767.0))
        out_ref[:, part * SLICE : (part + 1) * SLICE] = total[:OWN]


def groups_kernel(where_ref, image_feats, text_feats, early, image_out, text_out, held_ref):
    def fill(feats_ref, out_ref, starts, start, first):
        depth = feats_ref.shape[1]
        for i, at in enumerate(starts):
            held_ref[i * QUARTER : (i + 1) * QUARTER, :depth] = feats_ref[at, :]
        for i in range(out_ref.shape[0] // (STEP * GROUP)):
            begin = (first + i) * STEP * OWN - start
            low = min(max(begin // 128 * 128, 0), depth - ROWS)
            row = lax.broadcasted_iota(jnp.int32, (STEP * GROUP, ROWS), 0)
            lane = lax.broadcasted_iota(jnp.int32, (STEP * GROUP, ROWS), 1)
            inside = lax.rem(row, GROUP)
            wanted = lax.div(row, GROUP) * OWN + inside + (begin - low)
            select = jnp.where((inside < OWN) & (wanted == lane), 1.0, 0.0).astype(BF16)
            out_ref[i * STEP * GROUP : (i + 1) * STEP * GROUP, :] = lax.dot_general(
                select, held_ref[:, low : low + ROWS], NT, preferred_element_type=F32
            ).astype(BF16)

    def quarters(places):
        return [pl.ds(pl.multiple_of(place * QUARTER, QUARTER), QUARTER) for place in places]

    width = image_feats.shape[1]
    xl, core, _, _, _, text_quarter = position(where_ref)
    half = text_quarter // 2
    fill(
        image_feats, image_out,
        quarters([c * 2 + x for x in (xl, 1 - xl) for c in (core, 1 - core)]), 0, 0,
    )
    fill(
        text_feats, text_out,
        quarters([h * 2 + c for h in (half, 1 - half) for c in (core, 1 - core)]),
        width, width // OWN // STEP,
    )


def body(image_feats, text_feats, image_weight, text_weight, partner, log_scale, logit_bias):
    where = lax.axis_index(AXES).astype(jnp.int32).reshape(1)
    depth = image_feats.shape[1]
    own_texts, text_inverse, load, image_inverse = call(
        embed_kernel,
        [
            shape(QUARTER, E, dtype=BF16), shape(QUARTER, 128),
            shape(HALF + EXTRA, E, dtype=BF16), shape(QUARTER, 128),
        ],
        2 * (QUARTER * E + HALF * depth) * E, 8 << 20, 60,
        in_specs=[SMEM, VMEM] + [ANY] * 4, out_specs=[VMEM] * 4,
        scratch_shapes=[
            pltpu.VMEM((QUARTER, E), BF16), pltpu.VMEM((HALF, depth), BF16),
            pltpu.VMEM((E, E), BF16), pltpu.VMEM((depth, E), BF16),
            pltpu.VMEM((QUARTER, E), F32), pltpu.VMEM((HALF, E), F32),
            pltpu.SemaphoreType.DMA((11,)),
        ],
    )(where, partner.reshape(3, 128), text_feats, image_feats, text_weight, image_weight)
    other_texts = lax.ppermute(own_texts, ("xl", "xh"), FLIP)
    pair = jnp.concatenate([own_texts, other_texts], 0)
    image_pieces, text_pieces = ring_gather(load, "z"), ring_gather(pair, "y")
    images = call(
        images_kernel, shape(TILE + EXTRA, E, dtype=BF16), 0, 4 << 20,
        in_specs=[VMEM] * 5, out_specs=VMEM,
    )(*image_pieces)
    others = lax.ppermute(images, "core", SWAP)

    last, first = (depth - 1) // OWN // STEP, depth // OWN // STEP
    image_groups, text_groups = call(
        groups_kernel,
        [
            shape((last + 1) * STEP * GROUP, ROWS, dtype=BF16),
            shape((128 // STEP - first) * STEP * GROUP, ROWS, dtype=BF16),
        ],
        2 * 17 * STEP * GROUP * ROWS * ROWS, 5 << 20,
        in_specs=[SMEM, VMEM, VMEM, ANY], out_specs=[VMEM] * 2,
        scratch_shapes=[pltpu.VMEM((ROWS, depth), BF16)],
    )(where, image_feats, text_feats, image_pieces[2])

    flops = 2 * TILE * TILE * E
    coef, texts = shape(TILE, TILE, dtype=BF16), shape(TILE, E, dtype=BF16)
    ways = [shape(QUARTER, E)] * 2 + [shape(HALF, E)]
    rest = [shape(HALF, E)] * 2

    def run(kernel, outs, share, count, *options):
        return call(
            lambda *refs: kernel(*options, *refs), outs, int(share * flops), 6 << 20, 24,
            in_specs=[VMEM] * count, out_specs=[VMEM] * len(outs),
        )

    texts, own_coef = call(
        own_kernel, [texts, coef], 16 * flops, 6 << 20, 24,
        in_specs=[SMEM] * 3 + [VMEM] * 6 + [ANY] * 2, out_specs=[VMEM] * 2,
    )(where, log_scale, logit_bias, *text_pieces, images, image_groups, text_groups)
    others_coef, given = call(
        given_kernel, [coef, shape(ROWS, E)], 2 * flops, 8 << 20, 24,
        in_specs=[SMEM] * 3 + [VMEM] * 2, out_specs=[VMEM] * 2,
    )(where, log_scale, logit_bias, texts, others)
    taken = lax.ppermute(given, "core", SWAP)
    sides = own_coef, images, others_coef, others
    text_ways = run(text_kernel, ways, 1, 4, 0)(*sides)
    given_rest, = run(given_rest_kernel, [shape(ROWS, E)], 0.5, 2)(texts, others_coef)
    taken_rest = lax.ppermute(given_rest, "core", SWAP)
    image_ways = run(kept_kernel, ways, 0.5, 3, 0)(texts, own_coef, taken)
    text_rest = run(text_kernel, rest, 8, 4, 1)(*sides)
    image_rest = run(kept_kernel, rest, 0.5, 3, 1)(texts, own_coef, taken_rest)
    text_sums = ring_scatter(
        *text_ways, *text_rest, "y", lambda a: lax.ppermute(a, ("xl", "xh"), FLIP)
    )
    image_sums = ring_scatter(
        *image_ways, *image_rest, "z", lambda a: lax.ppermute(a, "xl", SWAP)
    )

    piece = shape(HALF, SLICE, dtype=BF16)
    own, other_core, other_xl, other_both = call(
        back_kernel, [piece] * 4, 0, 6 << 20,
        in_specs=[SMEM] + [VMEM] * 14, out_specs=[VMEM] * 4,
        scratch_shapes=[pltpu.VMEM((4, HALF, SLICE), BF16)],
    )(where, *image_sums, load, image_inverse, *text_sums, own_texts, text_inverse)
    backs = (
        own,
        lax.ppermute(other_core, "core", SWAP),
        lax.ppermute(other_xl, "xl", SWAP),
        lax.ppermute(other_both, TOWER, [(i, 3 - i) for i in range(4)]),
    )

    coded = call(
        terms_kernel, shape(128, GROUP, SLICE, dtype=jnp.int16),
        4 * 128 * GROUP * ROWS * SLICE, 6 << 20, 24,
        in_specs=[VMEM] * 6, out_specs=VMEM,
        scratch_shapes=[pltpu.VMEM((2, ROWS, SLICE), BF16)],
    )(image_groups, text_groups, *backs)
    coded = lax.all_to_all(coded, AXES, split_axis=0, concat_axis=0, tiled=True)
    return call(total_kernel, shape(OWN, E), 0, 2 << 20, in_specs=[VMEM], out_specs=VMEM)(coded)


def solution(mesh):
    fine = Mesh(mesh.devices.reshape([SIZES[a] for a in AXES]), AXES)
    placed = (P(DP, None), P(DP, None), P(), P(), P(DP), P(), P())
    return jax.shard_map(
        body, mesh=fine, in_specs=placed, out_specs=P(TOWER + DP, None), check_vma=False
    )
```

```python
import math

import jax
import jax.numpy as jnp
from jax import lax
from jax.experimental import pallas as pl
from jax.experimental.pallas import tpu as pltpu
from jax.sharding import Mesh, PartitionSpec as P

AXES = ("xl", "core", "z", "xh", "y")
SIZES = {"xl": 2, "core": 2, "z": 4, "xh": 2, "y": 4}
DP = ("z", "xh", "y")
TOWER = ("xl", "core")
SWAP = [(0, 1), (1, 0)]
FLIP = [(0, 3), (1, 2), (2, 1), (3, 0)]
ROWS = 384
HALF, QUARTER = 192, 96
EXTRA = 16
E = 1024
TILE = 4 * HALF
OWN = 21
GROUP = 24
SLICE = E // 4
STEP = 8
NT = (((1,), (1,)), ((), ()))
TN = (((0,), (0,)), ((), ()))
OCTAVE = math.log(2.0) / 16.0
F32, BF16 = jnp.float32, jnp.bfloat16


def shifted(array, axis, by):
    return lax.ppermute(array, axis, [(i, (i + by) % 4) for i in range(4)])


def call(kernel, outs, flops, moved, limit=16, **options):
    return pl.pallas_call(
        kernel,
        out_shape=outs,
        cost_estimate=pl.CostEstimate(flops=flops, bytes_accessed=moved, transcendentals=0),
        compiler_params=pltpu.CompilerParams(vmem_limit_bytes=limit << 20),
        **options,
    )


def shape(*dims, dtype=F32):
    return jax.ShapeDtypeStruct(dims, dtype)


VMEM = pl.BlockSpec(memory_space=pltpu.VMEM)
SMEM = pl.BlockSpec(memory_space=pltpu.SMEM)
ANY = pl.BlockSpec(memory_space=pl.ANY)


def position(where_ref):
    index = where_ref[0]
    xl, core, z, xh, y = index // 64, index // 32 % 2, index // 8 % 4, index // 4 % 2, index % 4
    return xl, core, z, xh, y, (xl + xh) % 2 * 2 + core


def normalised(pre_ref, inverse_ref):
    pre = pre_ref[...]
    total = jnp.sum(pre * pre, axis=1, keepdims=True)
    inverse = lax.rsqrt(total + 1e-06).astype(BF16).astype(F32)
    inverse_ref[...] = jnp.broadcast_to(inverse[:QUARTER], (QUARTER, 128))
    return (pre * inverse).astype(BF16)


def embed_kernel(
    where_ref, partner_ref, text_feats, image_feats, text_weight, image_weight,
    text_ref, text_inverse, load_ref, image_inverse,
    text_rows, image_rows, text_held, image_held, text_pre, image_pre, sems,
):
    count = 0

    def begin(source, target):
        nonlocal count
        copy = pltpu.make_async_copy(source, target, sems.at[count])
        copy.start()
        count += 1
        return copy

    xl, core, _, _, _, text_quarter = position(where_ref)
    places = core * 2 + xl, core * 2 + 1 - xl

    def rows(place):
        return pl.ds(pl.multiple_of(place * QUARTER, QUARTER), QUARTER)

    def begin_weight(weight, held, ends):
        spans = [slice(a, b) for a, b in zip((0,) + ends, ends)]
        return [(span, begin(weight.at[span], held.at[span])) for span in spans]

    def project(rows_ref, held, waits, pre_ref):
        for i, (span, copy) in enumerate(waits):
            copy.wait()
            got = jnp.dot(rows_ref[:, span], held[span, :], preferred_element_type=F32)
            pre_ref[...] = got if i == 0 else pre_ref[...] + got

    text_copy = begin(text_feats.at[rows(text_quarter)], text_rows)
    text_waits = begin_weight(text_weight, text_held, (256, 512, 768, 1024))
    image_copies = [
        begin(image_feats.at[rows(place)], image_rows.at[i * QUARTER : (i + 1) * QUARTER])
        for i, place in enumerate(places)
    ]
    image_waits = begin_weight(image_weight, image_held, (384, 768, 1152, 1664))

    text_copy.wait()
    project(text_rows, text_held, text_waits, text_pre)
    text_ref[...] = normalised(text_pre, text_inverse)
    for copy in image_copies:
        copy.wait()
    project(image_rows, image_held, image_waits, image_pre)
    load_ref[:HALF, :] = normalised(image_pre, image_inverse)

    partner = jnp.concatenate([partner_ref[i : i + 1, :] for i in range(3)], 1).astype(F32)
    partner = jnp.broadcast_to(partner, (EXTRA, ROWS))
    lane = lax.broadcasted_iota(jnp.int32, (EXTRA, ROWS), 1)
    row = lax.broadcasted_iota(jnp.int32, (EXTRA, ROWS), 0)
    chosen = jnp.zeros((EXTRA, ROWS), F32)
    for i, place in enumerate(places):
        moved = pltpu.roll(partner, (i + 4 - place) % 4 * QUARTER, 1)
        chosen = jnp.where(lane // QUARTER == i, moved, chosen)
    high = jnp.floor(chosen * (1.0 / 128.0))
    parts = jnp.where(row == 0, high, jnp.where(row == 1, chosen - 128.0 * high, 0.0))
    load_ref[HALF:, :] = jnp.zeros((EXTRA, E), BF16)
    load_ref[HALF:, :ROWS] = parts.astype(BF16)


def ring_gather(block, axis):
    before, after = shifted(block, axis, 1), shifted(block, axis, -1)
    far_low = shifted(before[:QUARTER], axis, 1)
    far_high = shifted(after[QUARTER:], axis, -1)
    return block, after, before, far_low, far_high


def far_kernel(low_ref, high_ref, early_ref, out_ref):
    out_ref[...] = low_ref[...] + high_ref[...]


def add_kernel(low_ref, high_ref, out_ref):
    out_ref[...] = low_ref[...] + high_ref[...]


def behind_kernel(far_ref, early_ref, out_ref):
    out_ref[...] = far_ref[...]


def ring_scatter(far_low, far_high, after, before, mine, axis, crossed, marker=None):
    far = crossed(far_high)
    got_right, got_left = shifted(after, axis, 1), shifted(before, axis, -1)
    if axis == "z":
        far = call(
            far_kernel, shape(QUARTER, E), 0, 1 << 20, in_specs=[VMEM, VMEM, ANY], out_specs=VMEM
        )(far_low, far, marker)
    else:
        far = call(
            add_kernel, shape(QUARTER, E), 4 << 30, 1 << 20, in_specs=[VMEM] * 2, out_specs=VMEM
        )(far_low, far)
        far = call(
            behind_kernel, shape(QUARTER, E), 0, 1 << 20, in_specs=[VMEM, ANY], out_specs=VMEM
        )(far, got_left)
    high = mine[QUARTER:] + got_right[QUARTER:] + got_left[QUARTER:]
    return mine, got_right, got_left, shifted(far, axis, 2), crossed(high)


ORDER = ((2, 0), (2, 1), (1, 0), (1, 1), (3, 0), (3, 1), (0, 0), (0, 1))


def in_order(refs, out_ref):
    me, after, before, far_low, far_high = refs
    for place, (step, half) in enumerate(ORDER):
        ref = (me, after, far_high if half else far_low, before)[step]
        start = 0 if step == 2 else half * QUARTER
        out_ref[place * QUARTER : (place + 1) * QUARTER, :] = ref[start : start + QUARTER, :]


def images_kernel(me, after, before, far_low, far_high, out_ref):
    in_order((me, after, before, far_low, far_high), out_ref)
    lane = lax.broadcasted_iota(jnp.int32, (EXTRA, E), 1)
    carried = [ref[start:, :].astype(F32) for ref, start in (
        (me, HALF), (after, HALF), (far_high, QUARTER), (before, HALF)
    )]
    total = jnp.zeros((EXTRA, E), F32)
    for place, (step, half) in enumerate(ORDER):
        inside = (lane >= half * QUARTER) & (lane < (half + 1) * QUARTER)
        piece = jnp.where(inside, carried[step], 0.0)
        total += pltpu.roll(piece, (place - half) * QUARTER % E, 1)
    out_ref[TILE:, :] = total.astype(BF16)


def coefficients(where_ref, scale_ref, shift_ref, images_ref, texts_ref, coef_ref):
    _, _, z, xh, y, text_quarter = position(where_ref)
    parts = images_ref[TILE:, :TILE].astype(F32)
    partner = (parts[0:1] * 128.0 + parts[1:2]).astype(jnp.int32)
    scale, shift = jnp.exp(jnp.full((1, 1), scale_ref[0], F32)), shift_ref[0]
    row = lax.broadcasted_iota(jnp.int32, (TILE, 1), 0)
    index = row
    for place, (step, half) in enumerate(ORDER):
        block = (z * 2 + (1 - xh if half else xh)) * 4 + lax.rem(y + step, 4)
        start = block * ROWS + text_quarter * QUARTER
        index = jnp.where(row // QUARTER == place, row + (start - place * QUARTER), index)
    logits = scale * lax.dot_general(
        texts_ref[...], images_ref[:TILE, :], NT, preferred_element_type=F32
    ) + shift
    own = index == partner
    slopes = jnp.where(own, -scale, scale) / (1.0 + jnp.exp(jnp.where(own, logits, -logits)))
    coef_ref[...] = slopes.astype(BF16)


def image_terms(coef_ref, texts_ref, part):
    return lax.dot_general(
        coef_ref[:, part * ROWS : (part + 1) * ROWS], texts_ref[...], TN,
        preferred_element_type=F32,
    )


def share_out(got, outs):
    start = 0
    for out in outs:
        out[...] = got[start : start + out.shape[0]]
        start += out.shape[0]


def own_kernel(
    where_ref, scale_ref, shift_ref, me, after, before, far_low, far_high, images_ref, early_a, early_b,
    texts_ref, coef_ref,
):
    in_order((me, after, before, far_low, far_high), texts_ref)
    coefficients(where_ref, scale_ref, shift_ref, images_ref, texts_ref, coef_ref)


def given_kernel(where_ref, scale_ref, shift_ref, texts_ref, images_ref, coef_ref, given_ref):
    coefficients(where_ref, scale_ref, shift_ref, images_ref, texts_ref, coef_ref)
    given_ref[...] = image_terms(coef_ref, texts_ref, 0)


def given_rest_kernel(texts_ref, coef_ref, given_ref):
    given_ref[...] = image_terms(coef_ref, texts_ref, 1)


def text_kernel(part, own_coef, images_ref, others_coef, others_ref, *outs):
    rows = slice(part * ROWS, (part + 1) * ROWS)
    got = jnp.dot(own_coef[rows, :], images_ref[:TILE, :], preferred_element_type=F32)
    got += jnp.dot(others_coef[rows, :], others_ref[:TILE, :], preferred_element_type=F32)
    share_out(got, outs)


def kept_kernel(part, texts_ref, coef_ref, taken_ref, *outs):
    share_out(image_terms(coef_ref, texts_ref, part) + taken_ref[...], outs)


def back_kernel(
    where_ref, mine, right, left, far, got, emb, inverse, own_ref, core_ref, xl_ref, both_ref, held_ref
):
    gradients = mine[:QUARTER, :] + right[:QUARTER, :] + left[:QUARTER, :]
    gradients += far[...] + got[...]
    widened = emb[:QUARTER, :].astype(F32)
    inner_sum = jnp.sum(widened * gradients, axis=1, keepdims=True)
    value = (inverse[:, :1] * (gradients - widened * inner_sum)).astype(BF16)
    for i in range(4):
        held_ref[i] = value[:, i * SLICE : (i + 1) * SLICE]
    xl, core, _, _, _, _ = position(where_ref)
    own_ref[...] = held_ref[xl * 2 + core]
    core_ref[...] = held_ref[xl * 2 + 1 - core]
    xl_ref[...] = held_ref[2 - xl * 2 + core]
    both_ref[...] = held_ref[3 - xl * 2 - core]


def terms_kernel(images_ref, texts_ref, *refs):
    *backs, out_ref, both_ref = refs
    for i, ref in enumerate(backs):
        both_ref[i // 4, i % 4 * QUARTER : (i % 4 + 1) * QUARTER, :] = ref[...]
    rows = STEP * GROUP
    steps = 128 // STEP
    last = images_ref.shape[0] // rows - 1
    first = steps - texts_ref.shape[0] // rows
    for step in range(steps):
        terms = jnp.zeros((rows, SLICE), F32)
        if step <= last:
            terms += jnp.dot(
                images_ref[step * rows : (step + 1) * rows, :], both_ref[0],
                preferred_element_type=F32,
            )
        if step >= first:
            terms += jnp.dot(
                texts_ref[(step - first) * rows : (step - first + 1) * rows, :], both_ref[1],
                preferred_element_type=F32,
            )
        terms = terms.reshape(STEP, GROUP, SLICE)
        largest = jnp.max(jnp.max(jnp.abs(terms), axis=1), axis=1, keepdims=True)
        exponent = jnp.ceil(jnp.log(jnp.maximum(largest, 1e-30)) * (1.0 / OCTAVE) + 0.01)
        factor = 32767.0 * jnp.exp(exponent * -OCTAVE)
        row = lax.broadcasted_iota(jnp.int32, terms.shape, 1)
        coded = jnp.where(row == OWN, exponent[:, :, None], jnp.round(terms * factor[:, :, None]))
        out_ref[step * STEP : (step + 1) * STEP] = coded.astype(jnp.int32).astype(jnp.int16)


def total_kernel(coded_ref, out_ref):
    for part in range(4):
        total = jnp.zeros((GROUP, SLICE), F32)
        for i in range(32):
            terms = coded_ref[part * 32 + i].astype(jnp.int32).astype(F32)
            total += terms * (jnp.exp(terms[OWN : OWN + 1, :] * OCTAVE) * (1.0 / 32767.0))
        out_ref[:, part * SLICE : (part + 1) * SLICE] = total[:OWN]


def groups_kernel(where_ref, image_feats, text_feats, early, image_out, text_out, held_ref):
    def fill(feats_ref, out_ref, starts, start, first):
        depth = feats_ref.shape[1]
        for i, at in enumerate(starts):
            held_ref[i * QUARTER : (i + 1) * QUARTER, :depth] = feats_ref[at, :]
        for i in range(out_ref.shape[0] // (STEP * GROUP)):
            begin = (first + i) * STEP * OWN - start
            low = min(max(begin // 128 * 128, 0), depth - ROWS)
            row = lax.broadcasted_iota(jnp.int32, (STEP * GROUP, ROWS), 0)
            lane = lax.broadcasted_iota(jnp.int32, (STEP * GROUP, ROWS), 1)
            inside = lax.rem(row, GROUP)
            wanted = lax.div(row, GROUP) * OWN + inside + (begin - low)
            select = jnp.where((inside < OWN) & (wanted == lane), 1.0, 0.0).astype(BF16)
            out_ref[i * STEP * GROUP : (i + 1) * STEP * GROUP, :] = lax.dot_general(
                select, held_ref[:, low : low + ROWS], NT, preferred_element_type=F32
            ).astype(BF16)

    def quarters(places):
        return [pl.ds(pl.multiple_of(place * QUARTER, QUARTER), QUARTER) for place in places]

    width = image_feats.shape[1]
    xl, core, _, _, _, text_quarter = position(where_ref)
    half = text_quarter // 2
    fill(
        image_feats, image_out,
        quarters([c * 2 + x for x in (xl, 1 - xl) for c in (core, 1 - core)]), 0, 0,
    )
    fill(
        text_feats, text_out,
        quarters([h * 2 + c for h in (half, 1 - half) for c in (core, 1 - core)]),
        width, width // OWN // STEP,
    )


def body(image_feats, text_feats, image_weight, text_weight, partner, log_scale, logit_bias):
    where = lax.axis_index(AXES).astype(jnp.int32).reshape(1)
    depth = image_feats.shape[1]
    own_texts, text_inverse, load, image_inverse = call(
        embed_kernel,
        [
            shape(QUARTER, E, dtype=BF16), shape(QUARTER, 128),
            shape(HALF + EXTRA, E, dtype=BF16), shape(QUARTER, 128),
        ],
        2 * (QUARTER * E + HALF * depth) * E, 8 << 20, 60,
        in_specs=[SMEM, VMEM] + [ANY] * 4, out_specs=[VMEM] * 4,
        scratch_shapes=[
            pltpu.VMEM((QUARTER, E), BF16), pltpu.VMEM((HALF, depth), BF16),
            pltpu.VMEM((E, E), BF16), pltpu.VMEM((depth, E), BF16),
            pltpu.VMEM((QUARTER, E), F32), pltpu.VMEM((HALF, E), F32),
            pltpu.SemaphoreType.DMA((11,)),
        ],
    )(where, partner.reshape(3, 128), text_feats, image_feats, text_weight, image_weight)
    other_texts = lax.ppermute(own_texts, ("xl", "xh"), FLIP)
    pair = jnp.concatenate([own_texts, other_texts], 0)
    image_pieces, text_pieces = ring_gather(load, "z"), ring_gather(pair, "y")
    images = call(
        images_kernel, shape(TILE + EXTRA, E, dtype=BF16), 0, 4 << 20,
        in_specs=[VMEM] * 5, out_specs=VMEM,
    )(*image_pieces)
    others = lax.ppermute(images, "core", SWAP)

    last, first = (depth - 1) // OWN // STEP, depth // OWN // STEP
    image_groups, text_groups = call(
        groups_kernel,
        [
            shape((last + 1) * STEP * GROUP, ROWS, dtype=BF16),
            shape((128 // STEP - first) * STEP * GROUP, ROWS, dtype=BF16),
        ],
        2 * 17 * STEP * GROUP * ROWS * ROWS, 5 << 20,
        in_specs=[SMEM, VMEM, VMEM, ANY], out_specs=[VMEM] * 2,
        scratch_shapes=[pltpu.VMEM((ROWS, depth), BF16)],
    )(where, image_feats, text_feats, image_pieces[2])

    flops = 2 * TILE * TILE * E
    coef, texts = shape(TILE, TILE, dtype=BF16), shape(TILE, E, dtype=BF16)
    ways = [shape(QUARTER, E)] * 2 + [shape(HALF, E)]
    rest = [shape(HALF, E)] * 2

    def run(kernel, outs, share, count, *options):
        return call(
            lambda *refs: kernel(*options, *refs), outs, int(share * flops), 6 << 20, 24,
            in_specs=[VMEM] * count, out_specs=[VMEM] * len(outs),
        )

    texts, own_coef = call(
        own_kernel, [texts, coef], 16 * flops, 6 << 20, 24,
        in_specs=[SMEM] * 3 + [VMEM] * 6 + [ANY] * 2, out_specs=[VMEM] * 2,
    )(where, log_scale, logit_bias, *text_pieces, images, image_groups, text_groups)
    others_coef, given = call(
        given_kernel, [coef, shape(ROWS, E)], 2 * flops, 8 << 20, 24,
        in_specs=[SMEM] * 3 + [VMEM] * 2, out_specs=[VMEM] * 2,
    )(where, log_scale, logit_bias, texts, others)
    taken = lax.ppermute(given, "core", SWAP)
    sides = own_coef, images, others_coef, others
    text_ways = run(text_kernel, ways, 1, 4, 0)(*sides)
    given_rest, = run(given_rest_kernel, [shape(ROWS, E)], 0.5, 2)(texts, others_coef)
    taken_rest = lax.ppermute(given_rest, "core", SWAP)
    image_ways = run(kept_kernel, ways, 0.5, 3, 0)(texts, own_coef, taken)
    text_rest = run(text_kernel, rest, 8, 4, 1)(*sides)
    image_rest = run(kept_kernel, rest, 4, 3, 1)(texts, own_coef, taken_rest)
    text_sums = ring_scatter(
        *text_ways, *text_rest, "y", lambda a: lax.ppermute(a, ("xl", "xh"), FLIP)
    )
    image_sums = ring_scatter(
        *image_ways, *image_rest, "z", lambda a: lax.ppermute(a, "xl", SWAP), text_sums[1],
    )

    def tower_pieces(*inputs):
        own, other_core, other_xl, other_both = call(
            back_kernel, [shape(QUARTER, SLICE, dtype=BF16)] * 4, 0, 3 << 20,
            in_specs=[SMEM] + [VMEM] * 7, out_specs=[VMEM] * 4,
            scratch_shapes=[pltpu.VMEM((4, QUARTER, SLICE), BF16)],
        )(where, *inputs)
        return (
            own,
            lax.ppermute(other_core, "core", SWAP),
            lax.ppermute(other_xl, "xl", SWAP),
            lax.ppermute(other_both, TOWER, [(i, 3 - i) for i in range(4)]),
        )

    text_backs = tower_pieces(*text_sums, own_texts, text_inverse)
    image_backs = tower_pieces(*image_sums, load, image_inverse)

    coded = call(
        terms_kernel, shape(128, GROUP, SLICE, dtype=jnp.int16),
        4 * 128 * GROUP * ROWS * SLICE, 6 << 20, 24,
        in_specs=[VMEM] * 10, out_specs=VMEM,
        scratch_shapes=[pltpu.VMEM((2, ROWS, SLICE), BF16)],
    )(image_groups, text_groups, *image_backs, *text_backs)
    coded = lax.all_to_all(coded, AXES, split_axis=0, concat_axis=0, tiled=True)
    return call(total_kernel, shape(OWN, E), 0, 2 << 20, in_specs=[VMEM], out_specs=VMEM)(coded)


def solution(mesh):
    fine = Mesh(mesh.devices.reshape([SIZES[a] for a in AXES]), AXES)
    placed = (P(DP, None), P(DP, None), P(), P(), P(DP), P(), P())
    return jax.shard_map(
        body, mesh=fine, in_specs=placed, out_specs=P(TOWER + DP, None), check_vma=False
    )
```

```python
import math

import jax
import jax.numpy as jnp
from jax import lax
from jax.experimental import pallas as pl
from jax.experimental.pallas import tpu as pltpu
from jax.sharding import Mesh, PartitionSpec as P

AXES = ("xl", "core", "z", "xh", "y")
SIZES = {"xl": 2, "core": 2, "z": 4, "xh": 2, "y": 4}
DP = ("z", "xh", "y")
TOWER = ("xl", "core")
SWAP = [(0, 1), (1, 0)]
FLIP = [(0, 3), (1, 2), (2, 1), (3, 0)]
ROWS = 384
HALF, QUARTER = 192, 96
EXTRA = 16
E = 1024
TILE = 4 * HALF
OWN = 21
GROUP = 24
SLICE = E // 4
STEP = 8
NT = (((1,), (1,)), ((), ()))
TN = (((0,), (0,)), ((), ()))
OCTAVE = math.log(2.0) / 16.0
F32, BF16 = jnp.float32, jnp.bfloat16


def shifted(array, axis, by):
    return lax.ppermute(array, axis, [(i, (i + by) % 4) for i in range(4)])


def call(kernel, outs, flops, moved, limit=16, **options):
    return pl.pallas_call(
        kernel,
        out_shape=outs,
        cost_estimate=pl.CostEstimate(flops=flops, bytes_accessed=moved, transcendentals=0),
        compiler_params=pltpu.CompilerParams(vmem_limit_bytes=limit << 20),
        **options,
    )


def shape(*dims, dtype=F32):
    return jax.ShapeDtypeStruct(dims, dtype)


VMEM = pl.BlockSpec(memory_space=pltpu.VMEM)
SMEM = pl.BlockSpec(memory_space=pltpu.SMEM)
ANY = pl.BlockSpec(memory_space=pl.ANY)


def position(where_ref):
    index = where_ref[0]
    xl, core, z, xh, y = index // 64, index // 32 % 2, index // 8 % 4, index // 4 % 2, index % 4
    return xl, core, z, xh, y, (xl + xh) % 2 * 2 + core


def normalised(pre_ref, inverse_ref):
    pre = pre_ref[...]
    total = jnp.sum(pre * pre, axis=1, keepdims=True)
    inverse = lax.rsqrt(total + 1e-06).astype(BF16).astype(F32)
    inverse_ref[...] = jnp.broadcast_to(inverse[:QUARTER], (QUARTER, 128))
    return (pre * inverse).astype(BF16)


def embed_kernel(
    where_ref, partner_ref, text_feats, image_feats, text_weight, image_weight,
    text_ref, text_inverse, load_ref, image_inverse,
    text_rows, image_rows, text_held, image_held, text_pre, image_pre, sems,
):
    count = 0

    def begin(source, target):
        nonlocal count
        copy = pltpu.make_async_copy(source, target, sems.at[count])
        copy.start()
        count += 1
        return copy

    xl, core, _, _, _, text_quarter = position(where_ref)
    places = core * 2 + xl, core * 2 + 1 - xl

    def rows(place):
        return pl.ds(pl.multiple_of(place * QUARTER, QUARTER), QUARTER)

    def begin_weight(weight, held, ends):
        spans = [slice(a, b) for a, b in zip((0,) + ends, ends)]
        return [(span, begin(weight.at[span], held.at[span])) for span in spans]

    def project(rows_ref, held, waits, pre_ref):
        for i, (span, copy) in enumerate(waits):
            copy.wait()
            got = jnp.dot(rows_ref[:, span], held[span, :], preferred_element_type=F32)
            pre_ref[...] = got if i == 0 else pre_ref[...] + got

    text_copy = begin(text_feats.at[rows(text_quarter)], text_rows)
    text_waits = begin_weight(text_weight, text_held, (256, 512, 768, 1024))
    image_copies = [
        begin(image_feats.at[rows(place)], image_rows.at[i * QUARTER : (i + 1) * QUARTER])
        for i, place in enumerate(places)
    ]
    image_waits = begin_weight(image_weight, image_held, (384, 768, 1152, 1664))

    text_copy.wait()
    project(text_rows, text_held, text_waits, text_pre)
    text_ref[...] = normalised(text_pre, text_inverse)
    for copy in image_copies:
        copy.wait()
    project(image_rows, image_held, image_waits, image_pre)
    load_ref[:HALF, :] = normalised(image_pre, image_inverse)

    partner = jnp.concatenate([partner_ref[i : i + 1, :] for i in range(3)], 1).astype(F32)
    partner = jnp.broadcast_to(partner, (EXTRA, ROWS))
    lane = lax.broadcasted_iota(jnp.int32, (EXTRA, ROWS), 1)
    row = lax.broadcasted_iota(jnp.int32, (EXTRA, ROWS), 0)
    chosen = jnp.zeros((EXTRA, ROWS), F32)
    for i, place in enumerate(places):
        moved = pltpu.roll(partner, (i + 4 - place) % 4 * QUARTER, 1)
        chosen = jnp.where(lane // QUARTER == i, moved, chosen)
    high = jnp.floor(chosen * (1.0 / 128.0))
    parts = jnp.where(row == 0, high, jnp.where(row == 1, chosen - 128.0 * high, 0.0))
    load_ref[HALF:, :] = jnp.zeros((EXTRA, E), BF16)
    load_ref[HALF:, :ROWS] = parts.astype(BF16)


CODED = E + E // 4 + 128
TOP = 2.0**19 - 1.0


def encode(value, out_ref):
    largest = jnp.max(jnp.abs(value), axis=1, keepdims=True)
    exponent = jnp.ceil(jnp.log(jnp.maximum(largest, 1e-30)) * (1.0 / OCTAVE) + 0.01)
    whole = jnp.round(value * (TOP * jnp.exp(exponent * -OCTAVE))).astype(jnp.int32)
    out_ref[:, :E] = (whole >> 4).astype(jnp.int16)
    low = whole & 15
    packed = low[:, :SLICE]
    for i in range(1, 4):
        packed = packed | (low[:, i * SLICE : (i + 1) * SLICE] << (4 * i))
    out_ref[:, E : E + SLICE] = (packed - 32768).astype(jnp.int16)
    lanes = jnp.broadcast_to(exponent, (value.shape[0], 128))
    out_ref[:, E + SLICE :] = lanes.astype(jnp.int32).astype(jnp.int16)


def decode(ref, rows=slice(None)):
    exponent = ref[rows, E + SLICE : E + SLICE + 1].astype(jnp.int32).astype(F32)
    packed = ref[rows, E : E + SLICE].astype(jnp.int32) + 32768
    low = jnp.concatenate([(packed >> (4 * i)) & 15 for i in range(4)], 1)
    whole = (ref[rows, :E].astype(jnp.int32) << 4) + low
    return whole.astype(F32) * (jnp.exp(exponent * OCTAVE) * (1.0 / TOP))


def ring_gather(block, axis):
    before, after = shifted(block, axis, 1), shifted(block, axis, -1)
    far_low = shifted(before[:QUARTER], axis, 1)
    far_high = shifted(after[QUARTER:], axis, -1)
    return block, after, before, far_low, far_high


def far_kernel(low_ref, high_ref, early_ref, out_ref):
    encode(low_ref[...] + decode(high_ref), out_ref)


def add_kernel(low_ref, high_ref, out_ref):
    encode(low_ref[...] + decode(high_ref), out_ref)


def behind_kernel(far_ref, early_ref, out_ref):
    out_ref[...] = far_ref[...]


def high_kernel(mine, right, left, out_ref):
    rows = slice(QUARTER, HALF)
    encode(mine[rows, :] + decode(right, rows) + decode(left, rows), out_ref)


def ring_scatter(far_low, far_high, after, before, mine, axis, crossed, marker=None):
    got_right, got_left = shifted(after, axis, 1), shifted(before, axis, -1)
    far = crossed(far_high)
    coded = shape(QUARTER, CODED, dtype=jnp.int16)
    if axis == "z":
        far = call(
            far_kernel, coded, 0, 1 << 20, in_specs=[VMEM, VMEM, ANY], out_specs=VMEM
        )(far_low, far, marker)
    else:
        far = call(
            add_kernel, coded, 4 << 30, 1 << 20, in_specs=[VMEM] * 2, out_specs=VMEM
        )(far_low, far)
        far = call(
            behind_kernel, coded, 0, 1 << 20, in_specs=[VMEM, ANY], out_specs=VMEM
        )(far, got_left)
    high = call(high_kernel, coded, 0, 1 << 20, in_specs=[VMEM] * 3, out_specs=VMEM)(
        mine, got_right, got_left
    )
    return mine, got_right, got_left, shifted(far, axis, 2), crossed(high)


ORDER = ((2, 0), (2, 1), (1, 0), (1, 1), (3, 0), (3, 1), (0, 0), (0, 1))


def in_order(refs, out_ref):
    me, after, before, far_low, far_high = refs
    for place, (step, half) in enumerate(ORDER):
        ref = (me, after, far_high if half else far_low, before)[step]
        start = 0 if step == 2 else half * QUARTER
        out_ref[place * QUARTER : (place + 1) * QUARTER, :] = ref[start : start + QUARTER, :]


def images_kernel(me, after, before, far_low, far_high, out_ref):
    in_order((me, after, before, far_low, far_high), out_ref)
    lane = lax.broadcasted_iota(jnp.int32, (EXTRA, E), 1)
    carried = [ref[start:, :].astype(F32) for ref, start in (
        (me, HALF), (after, HALF), (far_high, QUARTER), (before, HALF)
    )]
    total = jnp.zeros((EXTRA, E), F32)
    for place, (step, half) in enumerate(ORDER):
        inside = (lane >= half * QUARTER) & (lane < (half + 1) * QUARTER)
        piece = jnp.where(inside, carried[step], 0.0)
        total += pltpu.roll(piece, (place - half) * QUARTER % E, 1)
    out_ref[TILE:, :] = total.astype(BF16)


def coefficients(where_ref, scale_ref, shift_ref, images_ref, texts_ref, coef_ref):
    _, _, z, xh, y, text_quarter = position(where_ref)
    parts = images_ref[TILE:, :TILE].astype(F32)
    partner = (parts[0:1] * 128.0 + parts[1:2]).astype(jnp.int32)
    scale, shift = jnp.exp(jnp.full((1, 1), scale_ref[0], F32)), shift_ref[0]
    row = lax.broadcasted_iota(jnp.int32, (TILE, 1), 0)
    index = row
    for place, (step, half) in enumerate(ORDER):
        block = (z * 2 + (1 - xh if half else xh)) * 4 + lax.rem(y + step, 4)
        start = block * ROWS + text_quarter * QUARTER
        index = jnp.where(row // QUARTER == place, row + (start - place * QUARTER), index)
    logits = scale * lax.dot_general(
        texts_ref[...], images_ref[:TILE, :], NT, preferred_element_type=F32
    ) + shift
    own = index == partner
    slopes = jnp.where(own, -scale, scale) / (1.0 + jnp.exp(jnp.where(own, logits, -logits)))
    coef_ref[...] = slopes.astype(BF16)


def image_terms(coef_ref, texts_ref, part):
    return lax.dot_general(
        coef_ref[:, part * ROWS : (part + 1) * ROWS], texts_ref[...], TN,
        preferred_element_type=F32,
    )


def share_out(got, outs):
    start = 0
    for out in outs:
        part = got[start : start + out.shape[0]]
        start += out.shape[0]
        if out.dtype == jnp.int16:
            encode(part, out)
        else:
            out[...] = part


def own_kernel(
    where_ref, scale_ref, shift_ref, me, after, before, far_low, far_high, images_ref, early_a, early_b,
    texts_ref, coef_ref,
):
    in_order((me, after, before, far_low, far_high), texts_ref)
    coefficients(where_ref, scale_ref, shift_ref, images_ref, texts_ref, coef_ref)


def given_kernel(where_ref, scale_ref, shift_ref, texts_ref, images_ref, coef_ref, given_ref):
    coefficients(where_ref, scale_ref, shift_ref, images_ref, texts_ref, coef_ref)
    given_ref[...] = image_terms(coef_ref, texts_ref, 0)


def given_rest_kernel(texts_ref, coef_ref, given_ref):
    given_ref[...] = image_terms(coef_ref, texts_ref, 1)


def text_kernel(part, own_coef, images_ref, others_coef, others_ref, *outs):
    rows = slice(part * ROWS, (part + 1) * ROWS)
    got = jnp.dot(own_coef[rows, :], images_ref[:TILE, :], preferred_element_type=F32)
    got += jnp.dot(others_coef[rows, :], others_ref[:TILE, :], preferred_element_type=F32)
    share_out(got, outs)


def kept_kernel(part, texts_ref, coef_ref, taken_ref, *outs):
    share_out(image_terms(coef_ref, texts_ref, part) + taken_ref[...], outs)


def kept_rest_kernel(texts_ref, coef_ref, taken_ref, early_ref, *outs):
    kept_kernel(1, texts_ref, coef_ref, taken_ref, *outs)


def back_kernel(
    where_ref, mine, right, left, far, got, emb, inverse, own_ref, core_ref, xl_ref, both_ref, held_ref
):
    rows = slice(0, QUARTER)
    gradients = mine[rows, :] + decode(right, rows) + decode(left, rows)
    gradients += decode(far) + decode(got)
    widened = emb[:QUARTER, :].astype(F32)
    inner_sum = jnp.sum(widened * gradients, axis=1, keepdims=True)
    value = (inverse[:, :1] * (gradients - widened * inner_sum)).astype(BF16)
    for i in range(4):
        held_ref[i] = value[:, i * SLICE : (i + 1) * SLICE]
    xl, core, _, _, _, _ = position(where_ref)
    own_ref[...] = held_ref[xl * 2 + core]
    core_ref[...] = held_ref[xl * 2 + 1 - core]
    xl_ref[...] = held_ref[2 - xl * 2 + core]
    both_ref[...] = held_ref[3 - xl * 2 - core]


def terms_kernel(images_ref, texts_ref, *refs):
    *backs, out_ref, both_ref = refs
    for i, ref in enumerate(backs):
        both_ref[i // 4, i % 4 * QUARTER : (i % 4 + 1) * QUARTER, :] = ref[...]
    rows = STEP * GROUP
    steps = 128 // STEP
    last = images_ref.shape[0] // rows - 1
    first = steps - texts_ref.shape[0] // rows
    for step in range(steps):
        terms = jnp.zeros((rows, SLICE), F32)
        if step <= last:
            terms += jnp.dot(
                images_ref[step * rows : (step + 1) * rows, :], both_ref[0],
                preferred_element_type=F32,
            )
        if step >= first:
            terms += jnp.dot(
                texts_ref[(step - first) * rows : (step - first + 1) * rows, :], both_ref[1],
                preferred_element_type=F32,
            )
        terms = terms.reshape(STEP, GROUP, SLICE)
        largest = jnp.max(jnp.max(jnp.abs(terms), axis=1), axis=1, keepdims=True)
        exponent = jnp.ceil(jnp.log(jnp.maximum(largest, 1e-30)) * (1.0 / OCTAVE) + 0.01)
        factor = 32767.0 * jnp.exp(exponent * -OCTAVE)
        row = lax.broadcasted_iota(jnp.int32, terms.shape, 1)
        coded = jnp.where(row == OWN, exponent[:, :, None], jnp.round(terms * factor[:, :, None]))
        out_ref[step * STEP : (step + 1) * STEP] = coded.astype(jnp.int32).astype(jnp.int16)


def total_kernel(coded_ref, out_ref):
    for part in range(4):
        total = jnp.zeros((GROUP, SLICE), F32)
        for i in range(32):
            terms = coded_ref[part * 32 + i].astype(jnp.int32).astype(F32)
            total += terms * (jnp.exp(terms[OWN : OWN + 1, :] * OCTAVE) * (1.0 / 32767.0))
        out_ref[:, part * SLICE : (part + 1) * SLICE] = total[:OWN]


def groups_kernel(where_ref, image_feats, text_feats, early, image_out, text_out, held_ref):
    def fill(feats_ref, out_ref, starts, start, first):
        depth = feats_ref.shape[1]
        for i, at in enumerate(starts):
            held_ref[i * QUARTER : (i + 1) * QUARTER, :depth] = feats_ref[at, :]
        for i in range(out_ref.shape[0] // (STEP * GROUP)):
            begin = (first + i) * STEP * OWN - start
            low = min(max(begin // 128 * 128, 0), depth - ROWS)
            row = lax.broadcasted_iota(jnp.int32, (STEP * GROUP, ROWS), 0)
            lane = lax.broadcasted_iota(jnp.int32, (STEP * GROUP, ROWS), 1)
            inside = lax.rem(row, GROUP)
            wanted = lax.div(row, GROUP) * OWN + inside + (begin - low)
            select = jnp.where((inside < OWN) & (wanted == lane), 1.0, 0.0).astype(BF16)
            out_ref[i * STEP * GROUP : (i + 1) * STEP * GROUP, :] = lax.dot_general(
                select, held_ref[:, low : low + ROWS], NT, preferred_element_type=F32
            ).astype(BF16)

    def quarters(places):
        return [pl.ds(pl.multiple_of(place * QUARTER, QUARTER), QUARTER) for place in places]

    width = image_feats.shape[1]
    xl, core, _, _, _, text_quarter = position(where_ref)
    half = text_quarter // 2
    fill(
        image_feats, image_out,
        quarters([c * 2 + x for x in (xl, 1 - xl) for c in (core, 1 - core)]), 0, 0,
    )
    fill(
        text_feats, text_out,
        quarters([h * 2 + c for h in (half, 1 - half) for c in (core, 1 - core)]),
        width, width // OWN // STEP,
    )


def body(image_feats, text_feats, image_weight, text_weight, partner, log_scale, logit_bias):
    where = lax.axis_index(AXES).astype(jnp.int32).reshape(1)
    depth = image_feats.shape[1]
    own_texts, text_inverse, load, image_inverse = call(
        embed_kernel,
        [
            shape(QUARTER, E, dtype=BF16), shape(QUARTER, 128),
            shape(HALF + EXTRA, E, dtype=BF16), shape(QUARTER, 128),
        ],
        2 * (QUARTER * E + HALF * depth) * E, 8 << 20, 60,
        in_specs=[SMEM, VMEM] + [ANY] * 4, out_specs=[VMEM] * 4,
        scratch_shapes=[
            pltpu.VMEM((QUARTER, E), BF16), pltpu.VMEM((HALF, depth), BF16),
            pltpu.VMEM((E, E), BF16), pltpu.VMEM((depth, E), BF16),
            pltpu.VMEM((QUARTER, E), F32), pltpu.VMEM((HALF, E), F32),
            pltpu.SemaphoreType.DMA((11,)),
        ],
    )(where, partner.reshape(3, 128), text_feats, image_feats, text_weight, image_weight)
    other_texts = lax.ppermute(own_texts, ("xl", "xh"), FLIP)
    pair = jnp.concatenate([own_texts, other_texts], 0)
    image_pieces, text_pieces = ring_gather(load, "z"), ring_gather(pair, "y")
    images = call(
        images_kernel, shape(TILE + EXTRA, E, dtype=BF16), 0, 4 << 20,
        in_specs=[VMEM] * 5, out_specs=VMEM,
    )(*image_pieces)
    others = lax.ppermute(images, "core", SWAP)

    last, first = (depth - 1) // OWN // STEP, depth // OWN // STEP
    image_groups, text_groups = call(
        groups_kernel,
        [
            shape((last + 1) * STEP * GROUP, ROWS, dtype=BF16),
            shape((128 // STEP - first) * STEP * GROUP, ROWS, dtype=BF16),
        ],
        2 * 17 * STEP * GROUP * ROWS * ROWS, 5 << 20,
        in_specs=[SMEM, VMEM, VMEM, ANY], out_specs=[VMEM] * 2,
        scratch_shapes=[pltpu.VMEM((ROWS, depth), BF16)],
    )(where, image_feats, text_feats, image_pieces[2])

    flops = 2 * TILE * TILE * E
    coef, texts = shape(TILE, TILE, dtype=BF16), shape(TILE, E, dtype=BF16)
    coded_quarter = shape(QUARTER, CODED, dtype=jnp.int16)
    coded_half = shape(HALF, CODED, dtype=jnp.int16)
    ways = [shape(QUARTER, E), coded_quarter, coded_half]
    rest = [coded_half, shape(HALF, E)]

    def run(kernel, outs, share, count, *options):
        return call(
            lambda *refs: kernel(*options, *refs), outs, int(share * flops), 6 << 20, 24,
            in_specs=[VMEM] * count, out_specs=[VMEM] * len(outs),
        )

    texts, own_coef = call(
        own_kernel, [texts, coef], 16 * flops, 6 << 20, 24,
        in_specs=[SMEM] * 3 + [VMEM] * 6 + [ANY] * 2, out_specs=[VMEM] * 2,
    )(where, log_scale, logit_bias, *text_pieces, images, image_groups, text_groups)
    others_coef, given = call(
        given_kernel, [coef, shape(ROWS, E)], 2 * flops, 8 << 20, 24,
        in_specs=[SMEM] * 3 + [VMEM] * 2, out_specs=[VMEM] * 2,
    )(where, log_scale, logit_bias, texts, others)
    taken = lax.ppermute(given, "core", SWAP)
    sides = own_coef, images, others_coef, others
    text_ways = run(text_kernel, ways, 1, 4, 0)(*sides)
    given_rest, = run(given_rest_kernel, [shape(ROWS, E)], 0.5, 2)(texts, others_coef)
    taken_rest = lax.ppermute(given_rest, "core", SWAP)
    image_ways = run(kept_kernel, ways, 0.5, 3, 0)(texts, own_coef, taken)
    text_rest = run(text_kernel, rest, 8, 4, 1)(*sides)
    image_rest = call(
        kept_rest_kernel, rest, 4 * flops, 6 << 20, 24,
        in_specs=[VMEM] * 3 + [ANY], out_specs=[VMEM] * 2,
    )(texts, own_coef, taken_rest, image_ways[0])
    text_sums = ring_scatter(
        *text_ways, *text_rest, "y", lambda a: lax.ppermute(a, ("xl", "xh"), FLIP)
    )
    image_sums = ring_scatter(
        *image_ways, *image_rest, "z", lambda a: lax.ppermute(a, "xl", SWAP), text_sums[1],
    )

    def tower_pieces(*inputs):
        own, other_core, other_xl, other_both = call(
            back_kernel, [shape(QUARTER, SLICE, dtype=BF16)] * 4, 0, 3 << 20,
            in_specs=[SMEM] + [VMEM] * 7, out_specs=[VMEM] * 4,
            scratch_shapes=[pltpu.VMEM((4, QUARTER, SLICE), BF16)],
        )(where, *inputs)
        return (
            own,
            lax.ppermute(other_core, "core", SWAP),
            lax.ppermute(other_xl, "xl", SWAP),
            lax.ppermute(other_both, TOWER, [(i, 3 - i) for i in range(4)]),
        )

    text_backs = tower_pieces(*text_sums, own_texts, text_inverse)
    image_backs = tower_pieces(*image_sums, load, image_inverse)

    coded = call(
        terms_kernel, shape(128, GROUP, SLICE, dtype=jnp.int16),
        4 * 128 * GROUP * ROWS * SLICE, 6 << 20, 24,
        in_specs=[VMEM] * 10, out_specs=VMEM,
        scratch_shapes=[pltpu.VMEM((2, ROWS, SLICE), BF16)],
    )(image_groups, text_groups, *image_backs, *text_backs)
    coded = lax.all_to_all(coded, AXES, split_axis=0, concat_axis=0, tiled=True)
    return call(total_kernel, shape(OWN, E), 0, 2 << 20, in_specs=[VMEM], out_specs=VMEM)(coded)


def solution(mesh):
    fine = Mesh(mesh.devices.reshape([SIZES[a] for a in AXES]), AXES)
    placed = (P(DP, None), P(DP, None), P(), P(), P(DP), P(), P())
    return jax.shard_map(
        body, mesh=fine, in_specs=placed, out_specs=P(TOWER + DP, None), check_vma=False
    )
```

```python
import math

import jax
import jax.numpy as jnp
from jax import lax
from jax.experimental import pallas as pl
from jax.experimental.pallas import tpu as pltpu
from jax.sharding import Mesh, PartitionSpec as P

AXES = ("xl", "core", "z", "xh", "y")
SIZES = {"xl": 2, "core": 2, "z": 4, "xh": 2, "y": 4}
DP = ("z", "xh", "y")
TOWER = ("xl", "core")
SWAP = [(0, 1), (1, 0)]
FLIP = [(0, 3), (1, 2), (2, 1), (3, 0)]
ROWS = 384
HALF, QUARTER = 192, 96
EXTRA = 16
E = 1024
TILE = 4 * HALF
OWN = 21
GROUP = 24
SLICE = E // 4
STEP = 8
NT = (((1,), (1,)), ((), ()))
TN = (((0,), (0,)), ((), ()))
OCTAVE = math.log(2.0) / 16.0
F32, BF16 = jnp.float32, jnp.bfloat16


def shifted(array, axis, by):
    return lax.ppermute(array, axis, [(i, (i + by) % 4) for i in range(4)])


def call(kernel, outs, flops, moved, limit=16, **options):
    return pl.pallas_call(
        kernel,
        out_shape=outs,
        cost_estimate=pl.CostEstimate(flops=flops, bytes_accessed=moved, transcendentals=0),
        compiler_params=pltpu.CompilerParams(vmem_limit_bytes=limit << 20),
        **options,
    )


def shape(*dims, dtype=F32):
    return jax.ShapeDtypeStruct(dims, dtype)


VMEM = pl.BlockSpec(memory_space=pltpu.VMEM)
SMEM = pl.BlockSpec(memory_space=pltpu.SMEM)
ANY = pl.BlockSpec(memory_space=pl.ANY)


def position(where_ref):
    index = where_ref[0]
    xl, core, z, xh, y = index // 64, index // 32 % 2, index // 8 % 4, index // 4 % 2, index % 4
    return xl, core, z, xh, y, (xl + xh) % 2 * 2 + core


def normalised(pre_ref, inverse_ref):
    pre = pre_ref[...]
    total = jnp.sum(pre * pre, axis=1, keepdims=True)
    inverse = lax.rsqrt(total + 1e-06).astype(BF16).astype(F32)
    inverse_ref[...] = jnp.broadcast_to(inverse[:QUARTER], (QUARTER, 128))
    return (pre * inverse).astype(BF16)


def embed_kernel(
    where_ref, partner_ref, text_feats, image_feats, text_weight, image_weight,
    text_ref, text_inverse, load_ref, image_inverse,
    text_rows, image_rows, text_held, image_held, text_pre, image_pre, sems,
):
    count = 0

    def begin(source, target):
        nonlocal count
        copy = pltpu.make_async_copy(source, target, sems.at[count])
        copy.start()
        count += 1
        return copy

    xl, core, _, _, _, text_quarter = position(where_ref)
    places = core * 2 + xl, core * 2 + 1 - xl

    def rows(place):
        return pl.ds(pl.multiple_of(place * QUARTER, QUARTER), QUARTER)

    def begin_weight(weight, held, ends):
        spans = [slice(a, b) for a, b in zip((0,) + ends, ends)]
        return [(span, begin(weight.at[span], held.at[span])) for span in spans]

    def project(rows_ref, held, waits, pre_ref):
        for i, (span, copy) in enumerate(waits):
            copy.wait()
            got = jnp.dot(rows_ref[:, span], held[span, :], preferred_element_type=F32)
            pre_ref[...] = got if i == 0 else pre_ref[...] + got

    text_copy = begin(text_feats.at[rows(text_quarter)], text_rows)
    text_waits = begin_weight(text_weight, text_held, (256, 512, 768, 1024))
    image_copies = [
        begin(image_feats.at[rows(place)], image_rows.at[i * QUARTER : (i + 1) * QUARTER])
        for i, place in enumerate(places)
    ]
    image_waits = begin_weight(image_weight, image_held, (384, 768, 1152, 1664))

    text_copy.wait()
    project(text_rows, text_held, text_waits, text_pre)
    text_ref[...] = normalised(text_pre, text_inverse)
    for copy in image_copies:
        copy.wait()
    project(image_rows, image_held, image_waits, image_pre)
    load_ref[:HALF, :] = normalised(image_pre, image_inverse)

    partner = jnp.concatenate([partner_ref[i : i + 1, :] for i in range(3)], 1).astype(F32)
    partner = jnp.broadcast_to(partner, (EXTRA, ROWS))
    lane = lax.broadcasted_iota(jnp.int32, (EXTRA, ROWS), 1)
    row = lax.broadcasted_iota(jnp.int32, (EXTRA, ROWS), 0)
    chosen = jnp.zeros((EXTRA, ROWS), F32)
    for i, place in enumerate(places):
        moved = pltpu.roll(partner, (i + 4 - place) % 4 * QUARTER, 1)
        chosen = jnp.where(lane // QUARTER == i, moved, chosen)
    high = jnp.floor(chosen * (1.0 / 128.0))
    parts = jnp.where(row == 0, high, jnp.where(row == 1, chosen - 128.0 * high, 0.0))
    load_ref[HALF:, :] = jnp.zeros((EXTRA, E), BF16)
    load_ref[HALF:, :ROWS] = parts.astype(BF16)


CODED = E + E // 4 + 128
TOP = 2.0**19 - 1.0


def encode(value, out_ref):
    largest = jnp.max(jnp.abs(value), axis=1, keepdims=True)
    exponent = jnp.ceil(jnp.log(jnp.maximum(largest, 1e-30)) * (1.0 / OCTAVE) + 0.01)
    whole = jnp.round(value * (TOP * jnp.exp(exponent * -OCTAVE))).astype(jnp.int32)
    out_ref[:, :E] = (whole >> 4).astype(jnp.int16)
    low = whole & 15
    packed = low[:, :SLICE]
    for i in range(1, 4):
        packed = packed | (low[:, i * SLICE : (i + 1) * SLICE] << (4 * i))
    out_ref[:, E : E + SLICE] = (packed - 32768).astype(jnp.int16)
    lanes = jnp.broadcast_to(exponent, (value.shape[0], 128))
    out_ref[:, E + SLICE :] = lanes.astype(jnp.int32).astype(jnp.int16)


def decode(ref, rows=slice(None)):
    exponent = ref[rows, E + SLICE : E + SLICE + 1].astype(jnp.int32).astype(F32)
    packed = ref[rows, E : E + SLICE].astype(jnp.int32) + 32768
    low = jnp.concatenate([(packed >> (4 * i)) & 15 for i in range(4)], 1)
    whole = (ref[rows, :E].astype(jnp.int32) << 4) + low
    return whole.astype(F32) * (jnp.exp(exponent * OCTAVE) * (1.0 / TOP))


def ring_gather(block, axis):
    before, after = shifted(block, axis, 1), shifted(block, axis, -1)
    far_low = shifted(before[:QUARTER], axis, 1)
    far_high = shifted(after[QUARTER:], axis, -1)
    return block, after, before, far_low, far_high


def far_kernel(low_ref, high_ref, early_ref, out_ref):
    encode(low_ref[...] + decode(high_ref), out_ref)


def add_kernel(low_ref, high_ref, out_ref):
    encode(low_ref[...] + decode(high_ref), out_ref)


def behind_kernel(far_ref, early_ref, out_ref):
    out_ref[...] = far_ref[...]


def high_kernel(mine, right, left, out_ref):
    rows = slice(QUARTER, HALF)
    encode(mine[rows, :] + decode(right, rows) + decode(left, rows), out_ref)


def ring_scatter(far_low, far_high, after, before, mine, axis, crossed, marker=None):
    got_right, got_left = shifted(after, axis, 1), shifted(before, axis, -1)
    far = crossed(far_high)
    coded = shape(QUARTER, CODED, dtype=jnp.int16)
    if axis == "z":
        far = call(
            far_kernel, coded, 0, 1 << 20, in_specs=[VMEM, VMEM, ANY], out_specs=VMEM
        )(far_low, far, marker)
    else:
        far = call(
            add_kernel, coded, 4 << 30, 1 << 20, in_specs=[VMEM] * 2, out_specs=VMEM
        )(far_low, far)
        far = call(
            behind_kernel, coded, 0, 1 << 20, in_specs=[VMEM, ANY], out_specs=VMEM
        )(far, got_left)
    high = call(high_kernel, coded, 0, 1 << 20, in_specs=[VMEM] * 3, out_specs=VMEM)(
        mine, got_right, got_left
    )
    return mine, got_right, got_left, shifted(far, axis, 2), crossed(high)


ORDER = ((2, 0), (2, 1), (1, 0), (1, 1), (3, 0), (3, 1), (0, 0), (0, 1))


def in_order(refs, out_ref):
    me, after, before, far_low, far_high = refs
    for place, (step, half) in enumerate(ORDER):
        ref = (me, after, far_high if half else far_low, before)[step]
        start = 0 if step == 2 else half * QUARTER
        out_ref[place * QUARTER : (place + 1) * QUARTER, :] = ref[start : start + QUARTER, :]


def images_kernel(me, after, before, far_low, far_high, out_ref):
    in_order((me, after, before, far_low, far_high), out_ref)
    lane = lax.broadcasted_iota(jnp.int32, (EXTRA, E), 1)
    carried = [ref[start:, :].astype(F32) for ref, start in (
        (me, HALF), (after, HALF), (far_high, QUARTER), (before, HALF)
    )]
    total = jnp.zeros((EXTRA, E), F32)
    for place, (step, half) in enumerate(ORDER):
        inside = (lane >= half * QUARTER) & (lane < (half + 1) * QUARTER)
        piece = jnp.where(inside, carried[step], 0.0)
        total += pltpu.roll(piece, (place - half) * QUARTER % E, 1)
    out_ref[TILE:, :] = total.astype(BF16)


def coefficients(where_ref, scale_ref, shift_ref, images_ref, texts_ref, coef_ref):
    _, _, z, xh, y, text_quarter = position(where_ref)
    parts = images_ref[TILE:, :TILE].astype(F32)
    partner = (parts[0:1] * 128.0 + parts[1:2]).astype(jnp.int32)
    scale, shift = jnp.exp(jnp.full((1, 1), scale_ref[0], F32)), shift_ref[0]
    row = lax.broadcasted_iota(jnp.int32, (TILE, 1), 0)
    index = row
    for place, (step, half) in enumerate(ORDER):
        block = (z * 2 + (1 - xh if half else xh)) * 4 + lax.rem(y + step, 4)
        start = block * ROWS + text_quarter * QUARTER
        index = jnp.where(row // QUARTER == place, row + (start - place * QUARTER), index)
    logits = scale * lax.dot_general(
        texts_ref[...], images_ref[:TILE, :], NT, preferred_element_type=F32
    ) + shift
    own = index == partner
    slopes = jnp.where(own, -scale, scale) / (1.0 + jnp.exp(jnp.where(own, logits, -logits)))
    coef_ref[...] = slopes.astype(BF16)


def image_terms(coef_ref, texts_ref, part):
    return lax.dot_general(
        coef_ref[:, part * ROWS : (part + 1) * ROWS], texts_ref[...], TN,
        preferred_element_type=F32,
    )


def share_out(got, outs):
    start = 0
    for out in outs:
        part = got[start : start + out.shape[0]]
        start += out.shape[0]
        if out.dtype == jnp.int16:
            encode(part, out)
        else:
            out[...] = part


def own_kernel(
    where_ref, scale_ref, shift_ref, me, after, before, far_low, far_high, images_ref, early_a, early_b,
    texts_ref, coef_ref,
):
    in_order((me, after, before, far_low, far_high), texts_ref)
    coefficients(where_ref, scale_ref, shift_ref, images_ref, texts_ref, coef_ref)


def given_kernel(where_ref, scale_ref, shift_ref, texts_ref, images_ref, coef_ref, given_ref):
    coefficients(where_ref, scale_ref, shift_ref, images_ref, texts_ref, coef_ref)
    given_ref[...] = image_terms(coef_ref, texts_ref, 0)


def given_rest_kernel(texts_ref, coef_ref, given_ref):
    given_ref[...] = image_terms(coef_ref, texts_ref, 1)


def text_kernel(own_coef, images_ref, others_coef, others_ref, *outs):
    got = jnp.dot(own_coef[...], images_ref[:TILE, :], preferred_element_type=F32)
    got += jnp.dot(others_coef[...], others_ref[:TILE, :], preferred_element_type=F32)
    share_out(got, outs)


def kept_kernel(part, texts_ref, coef_ref, taken_ref, *outs):
    share_out(image_terms(coef_ref, texts_ref, part) + taken_ref[...], outs)


def kept_rest_kernel(texts_ref, coef_ref, taken_ref, early_ref, *outs):
    kept_kernel(1, texts_ref, coef_ref, taken_ref, *outs)


def back_kernel(
    where_ref, mine, right, left, far, got, emb, inverse, own_ref, core_ref, xl_ref, both_ref, held_ref
):
    rows = slice(0, QUARTER)
    gradients = mine[rows, :] + decode(right, rows) + decode(left, rows)
    gradients += decode(far) + decode(got)
    widened = emb[:QUARTER, :].astype(F32)
    inner_sum = jnp.sum(widened * gradients, axis=1, keepdims=True)
    value = (inverse[:, :1] * (gradients - widened * inner_sum)).astype(BF16)
    for i in range(4):
        held_ref[i] = value[:, i * SLICE : (i + 1) * SLICE]
    xl, core, _, _, _, _ = position(where_ref)
    own_ref[...] = held_ref[xl * 2 + core]
    core_ref[...] = held_ref[xl * 2 + 1 - core]
    xl_ref[...] = held_ref[2 - xl * 2 + core]
    both_ref[...] = held_ref[3 - xl * 2 - core]


def terms_kernel(images_ref, texts_ref, *refs):
    *backs, out_ref, both_ref = refs
    for i, ref in enumerate(backs):
        both_ref[i // 4, i % 4 * QUARTER : (i % 4 + 1) * QUARTER, :] = ref[...]
    rows = STEP * GROUP
    steps = 128 // STEP
    last = images_ref.shape[0] // rows - 1
    first = steps - texts_ref.shape[0] // rows
    for step in range(steps):
        terms = jnp.zeros((rows, SLICE), F32)
        if step <= last:
            terms += jnp.dot(
                images_ref[step * rows : (step + 1) * rows, :], both_ref[0],
                preferred_element_type=F32,
            )
        if step >= first:
            terms += jnp.dot(
                texts_ref[(step - first) * rows : (step - first + 1) * rows, :], both_ref[1],
                preferred_element_type=F32,
            )
        terms = terms.reshape(STEP, GROUP, SLICE)
        largest = jnp.max(jnp.max(jnp.abs(terms), axis=1), axis=1, keepdims=True)
        exponent = jnp.ceil(jnp.log(jnp.maximum(largest, 1e-30)) * (1.0 / OCTAVE) + 0.01)
        factor = 32767.0 * jnp.exp(exponent * -OCTAVE)
        row = lax.broadcasted_iota(jnp.int32, terms.shape, 1)
        coded = jnp.where(row == OWN, exponent[:, :, None], jnp.round(terms * factor[:, :, None]))
        out_ref[step * STEP : (step + 1) * STEP] = coded.astype(jnp.int32).astype(jnp.int16)


def total_kernel(coded_ref, out_ref):
    for part in range(4):
        total = jnp.zeros((GROUP, SLICE), F32)
        for i in range(32):
            terms = coded_ref[part * 32 + i].astype(jnp.int32).astype(F32)
            total += terms * (jnp.exp(terms[OWN : OWN + 1, :] * OCTAVE) * (1.0 / 32767.0))
        out_ref[:, part * SLICE : (part + 1) * SLICE] = total[:OWN]


def groups_kernel(where_ref, image_feats, text_feats, early, image_out, text_out, held_ref):
    def fill(feats_ref, out_ref, starts, start, first):
        depth = feats_ref.shape[1]
        for i, at in enumerate(starts):
            held_ref[i * QUARTER : (i + 1) * QUARTER, :depth] = feats_ref[at, :]
        for i in range(out_ref.shape[0] // (STEP * GROUP)):
            begin = (first + i) * STEP * OWN - start
            low = min(max(begin // 128 * 128, 0), depth - ROWS)
            row = lax.broadcasted_iota(jnp.int32, (STEP * GROUP, ROWS), 0)
            lane = lax.broadcasted_iota(jnp.int32, (STEP * GROUP, ROWS), 1)
            inside = lax.rem(row, GROUP)
            wanted = lax.div(row, GROUP) * OWN + inside + (begin - low)
            select = jnp.where((inside < OWN) & (wanted == lane), 1.0, 0.0).astype(BF16)
            out_ref[i * STEP * GROUP : (i + 1) * STEP * GROUP, :] = lax.dot_general(
                select, held_ref[:, low : low + ROWS], NT, preferred_element_type=F32
            ).astype(BF16)

    def quarters(places):
        return [pl.ds(pl.multiple_of(place * QUARTER, QUARTER), QUARTER) for place in places]

    width = image_feats.shape[1]
    xl, core, _, _, _, text_quarter = position(where_ref)
    half = text_quarter // 2
    fill(
        image_feats, image_out,
        quarters([c * 2 + x for x in (xl, 1 - xl) for c in (core, 1 - core)]), 0, 0,
    )
    fill(
        text_feats, text_out,
        quarters([h * 2 + c for h in (half, 1 - half) for c in (core, 1 - core)]),
        width, width // OWN // STEP,
    )


def body(image_feats, text_feats, image_weight, text_weight, partner, log_scale, logit_bias):
    where = lax.axis_index(AXES).astype(jnp.int32).reshape(1)
    depth = image_feats.shape[1]
    own_texts, text_inverse, load, image_inverse = call(
        embed_kernel,
        [
            shape(QUARTER, E, dtype=BF16), shape(QUARTER, 128),
            shape(HALF + EXTRA, E, dtype=BF16), shape(QUARTER, 128),
        ],
        2 * (QUARTER * E + HALF * depth) * E, 8 << 20, 60,
        in_specs=[SMEM, VMEM] + [ANY] * 4, out_specs=[VMEM] * 4,
        scratch_shapes=[
            pltpu.VMEM((QUARTER, E), BF16), pltpu.VMEM((HALF, depth), BF16),
            pltpu.VMEM((E, E), BF16), pltpu.VMEM((depth, E), BF16),
            pltpu.VMEM((QUARTER, E), F32), pltpu.VMEM((HALF, E), F32),
            pltpu.SemaphoreType.DMA((11,)),
        ],
    )(where, partner.reshape(3, 128), text_feats, image_feats, text_weight, image_weight)
    other_texts = lax.ppermute(own_texts, ("xl", "xh"), FLIP)
    pair = jnp.concatenate([own_texts, other_texts], 0)
    image_pieces, text_pieces = ring_gather(load, "z"), ring_gather(pair, "y")
    images = call(
        images_kernel, shape(TILE + EXTRA, E, dtype=BF16), 0, 4 << 20,
        in_specs=[VMEM] * 5, out_specs=VMEM,
    )(*image_pieces)
    others = lax.ppermute(images, "core", SWAP)

    last, first = (depth - 1) // OWN // STEP, depth // OWN // STEP
    image_groups, text_groups = call(
        groups_kernel,
        [
            shape((last + 1) * STEP * GROUP, ROWS, dtype=BF16),
            shape((128 // STEP - first) * STEP * GROUP, ROWS, dtype=BF16),
        ],
        2 * 17 * STEP * GROUP * ROWS * ROWS, 5 << 20,
        in_specs=[SMEM, VMEM, VMEM, ANY], out_specs=[VMEM] * 2,
        scratch_shapes=[pltpu.VMEM((ROWS, depth), BF16)],
    )(where, image_feats, text_feats, image_pieces[2])

    flops = 2 * TILE * TILE * E
    coef, texts = shape(TILE, TILE, dtype=BF16), shape(TILE, E, dtype=BF16)
    coded_quarter = shape(QUARTER, CODED, dtype=jnp.int16)
    coded_half = shape(HALF, CODED, dtype=jnp.int16)
    ways = [shape(QUARTER, E), coded_quarter, coded_half]
    rest = [coded_half, shape(HALF, E)]

    def run(kernel, outs, share, count, *options):
        return call(
            lambda *refs: kernel(*options, *refs), outs, int(share * flops), 6 << 20, 24,
            in_specs=[VMEM] * count, out_specs=[VMEM] * len(outs),
        )

    texts, own_coef = call(
        own_kernel, [texts, coef], 16 * flops, 6 << 20, 24,
        in_specs=[SMEM] * 3 + [VMEM] * 6 + [ANY] * 2, out_specs=[VMEM] * 2,
    )(where, log_scale, logit_bias, *text_pieces, images, image_groups, text_groups)
    others_coef, given = call(
        given_kernel, [coef, shape(ROWS, E)], 2 * flops, 8 << 20, 24,
        in_specs=[SMEM] * 3 + [VMEM] * 2, out_specs=[VMEM] * 2,
    )(where, log_scale, logit_bias, texts, others)
    taken = lax.ppermute(given, "core", SWAP)
    sides = own_coef, images, others_coef, others
    text_parts = run(text_kernel, ways + rest, 2, 4)(*sides)
    text_ways, text_rest = text_parts[:3], text_parts[3:]
    given_rest, = run(given_rest_kernel, [shape(ROWS, E)], 0.5, 2)(texts, others_coef)
    taken_rest = lax.ppermute(given_rest, "core", SWAP)
    image_ways = run(kept_kernel, ways, 0.5, 3, 0)(texts, own_coef, taken)
    image_rest = call(
        kept_rest_kernel, rest, 4 * flops, 6 << 20, 24,
        in_specs=[VMEM] * 3 + [ANY], out_specs=[VMEM] * 2,
    )(texts, own_coef, taken_rest, image_ways[0])
    text_sums = ring_scatter(
        *text_ways, *text_rest, "y", lambda a: lax.ppermute(a, ("xl", "xh"), FLIP)
    )
    image_sums = ring_scatter(
        *image_ways, *image_rest, "z", lambda a: lax.ppermute(a, "xl", SWAP), text_sums[1],
    )

    def tower_pieces(*inputs):
        own, other_core, other_xl, other_both = call(
            back_kernel, [shape(QUARTER, SLICE, dtype=BF16)] * 4, 0, 3 << 20,
            in_specs=[SMEM] + [VMEM] * 7, out_specs=[VMEM] * 4,
            scratch_shapes=[pltpu.VMEM((4, QUARTER, SLICE), BF16)],
        )(where, *inputs)
        return (
            own,
            lax.ppermute(other_core, "core", SWAP),
            lax.ppermute(other_xl, "xl", SWAP),
            lax.ppermute(other_both, TOWER, [(i, 3 - i) for i in range(4)]),
        )

    text_backs = tower_pieces(*text_sums, own_texts, text_inverse)
    image_backs = tower_pieces(*image_sums, load, image_inverse)

    coded = call(
        terms_kernel, shape(128, GROUP, SLICE, dtype=jnp.int16),
        4 * 128 * GROUP * ROWS * SLICE, 6 << 20, 24,
        in_specs=[VMEM] * 10, out_specs=VMEM,
        scratch_shapes=[pltpu.VMEM((2, ROWS, SLICE), BF16)],
    )(image_groups, text_groups, *image_backs, *text_backs)
    coded = lax.all_to_all(coded, AXES, split_axis=0, concat_axis=0, tiled=True)
    return call(total_kernel, shape(OWN, E), 0, 2 << 20, in_specs=[VMEM], out_specs=VMEM)(coded)


def solution(mesh):
    fine = Mesh(mesh.devices.reshape([SIZES[a] for a in AXES]), AXES)
    placed = (P(DP, None), P(DP, None), P(), P(), P(DP), P(), P())
    return jax.shard_map(
        body, mesh=fine, in_specs=placed, out_specs=P(TOWER + DP, None), check_vma=False
    )
```

```python
import math

import jax
import jax.numpy as jnp
from jax import lax
from jax.experimental import pallas as pl
from jax.experimental.pallas import tpu as pltpu
from jax.sharding import Mesh, PartitionSpec as P

AXES = ("xl", "core", "z", "xh", "y")
SIZES = {"xl": 2, "core": 2, "z": 4, "xh": 2, "y": 4}
DP = ("z", "xh", "y")
TOWER = ("xl", "core")
SWAP = [(0, 1), (1, 0)]
FLIP = [(0, 3), (1, 2), (2, 1), (3, 0)]
ROWS = 384
HALF, QUARTER = 192, 96
EXTRA = 16
E = 1024
TILE = 4 * HALF
OWN = 21
GROUP = 24
SLICE = E // 4
STEP = 8
NT = (((1,), (1,)), ((), ()))
TN = (((0,), (0,)), ((), ()))
OCTAVE = math.log(2.0) / 16.0
F32, BF16 = jnp.float32, jnp.bfloat16


def shifted(array, axis, by):
    return lax.ppermute(array, axis, [(i, (i + by) % 4) for i in range(4)])


def call(kernel, outs, flops, moved, limit=16, **options):
    return pl.pallas_call(
        kernel,
        out_shape=outs,
        cost_estimate=pl.CostEstimate(flops=flops, bytes_accessed=moved, transcendentals=0),
        compiler_params=pltpu.CompilerParams(vmem_limit_bytes=limit << 20),
        **options,
    )


def shape(*dims, dtype=F32):
    return jax.ShapeDtypeStruct(dims, dtype)


VMEM = pl.BlockSpec(memory_space=pltpu.VMEM)
SMEM = pl.BlockSpec(memory_space=pltpu.SMEM)
ANY = pl.BlockSpec(memory_space=pl.ANY)


def position(where_ref):
    index = where_ref[0]
    xl, core, z, xh, y = index // 64, index // 32 % 2, index // 8 % 4, index // 4 % 2, index % 4
    return xl, core, z, xh, y, (xl + xh) % 2 * 2 + core


def normalised(pre_ref, inverse_ref):
    pre = pre_ref[...]
    total = jnp.sum(pre * pre, axis=1, keepdims=True)
    inverse = lax.rsqrt(total + 1e-06).astype(BF16).astype(F32)
    inverse_ref[...] = jnp.broadcast_to(inverse[:QUARTER], (QUARTER, 128))
    return (pre * inverse).astype(BF16)


def embed_kernel(
    where_ref, partner_ref, text_feats, image_feats, text_weight, image_weight,
    text_ref, text_inverse, load_ref, image_inverse,
    text_rows, image_rows, text_held, image_held, text_pre, image_pre, sems,
):
    count = 0

    def begin(source, target):
        nonlocal count
        copy = pltpu.make_async_copy(source, target, sems.at[count])
        copy.start()
        count += 1
        return copy

    xl, core, _, _, _, text_quarter = position(where_ref)
    places = core * 2 + xl, core * 2 + 1 - xl

    def rows(place):
        return pl.ds(pl.multiple_of(place * QUARTER, QUARTER), QUARTER)

    def begin_weight(weight, held, ends):
        spans = [slice(a, b) for a, b in zip((0,) + ends, ends)]
        return [(span, begin(weight.at[span], held.at[span])) for span in spans]

    def project(rows_ref, held, waits, pre_ref):
        for i, (span, copy) in enumerate(waits):
            copy.wait()
            got = jnp.dot(rows_ref[:, span], held[span, :], preferred_element_type=F32)
            pre_ref[...] = got if i == 0 else pre_ref[...] + got

    text_copy = begin(text_feats.at[rows(text_quarter)], text_rows)
    text_waits = begin_weight(text_weight, text_held, (256, 512, 768, 1024))
    image_copies = [
        begin(image_feats.at[rows(place)], image_rows.at[i * QUARTER : (i + 1) * QUARTER])
        for i, place in enumerate(places)
    ]
    image_waits = begin_weight(image_weight, image_held, (384, 768, 1152, 1664))

    text_copy.wait()
    project(text_rows, text_held, text_waits, text_pre)
    text_ref[...] = normalised(text_pre, text_inverse)
    for copy in image_copies:
        copy.wait()
    project(image_rows, image_held, image_waits, image_pre)
    load_ref[:HALF, :] = normalised(image_pre, image_inverse)

    partner = jnp.concatenate([partner_ref[i : i + 1, :] for i in range(3)], 1).astype(F32)
    partner = jnp.broadcast_to(partner, (EXTRA, ROWS))
    lane = lax.broadcasted_iota(jnp.int32, (EXTRA, ROWS), 1)
    row = lax.broadcasted_iota(jnp.int32, (EXTRA, ROWS), 0)
    chosen = jnp.zeros((EXTRA, ROWS), F32)
    for i, place in enumerate(places):
        moved = pltpu.roll(partner, (i + 4 - place) % 4 * QUARTER, 1)
        chosen = jnp.where(lane // QUARTER == i, moved, chosen)
    high = jnp.floor(chosen * (1.0 / 128.0))
    parts = jnp.where(row == 0, high, jnp.where(row == 1, chosen - 128.0 * high, 0.0))
    load_ref[HALF:, :] = jnp.zeros((EXTRA, E), BF16)
    load_ref[HALF:, :ROWS] = parts.astype(BF16)


CODED = E + E // 4 + 128
TOP = 2.0**19 - 1.0


def encode(value, out_ref):
    largest = jnp.max(jnp.abs(value), axis=1, keepdims=True)
    exponent = jnp.ceil(jnp.log(jnp.maximum(largest, 1e-30)) * (1.0 / OCTAVE) + 0.01)
    whole = jnp.round(value * (TOP * jnp.exp(exponent * -OCTAVE))).astype(jnp.int32)
    out_ref[:, :E] = (whole >> 4).astype(jnp.int16)
    low = whole & 15
    packed = low[:, :SLICE]
    for i in range(1, 4):
        packed = packed | (low[:, i * SLICE : (i + 1) * SLICE] << (4 * i))
    out_ref[:, E : E + SLICE] = (packed - 32768).astype(jnp.int16)
    lanes = jnp.broadcast_to(exponent, (value.shape[0], 128))
    out_ref[:, E + SLICE :] = lanes.astype(jnp.int32).astype(jnp.int16)


def decode(ref, rows=slice(None)):
    exponent = ref[rows, E + SLICE : E + SLICE + 1].astype(jnp.int32).astype(F32)
    packed = ref[rows, E : E + SLICE].astype(jnp.int32) + 32768
    low = jnp.concatenate([(packed >> (4 * i)) & 15 for i in range(4)], 1)
    whole = (ref[rows, :E].astype(jnp.int32) << 4) + low
    return whole.astype(F32) * (jnp.exp(exponent * OCTAVE) * (1.0 / TOP))


def ring_gather(block, axis):
    before, after = shifted(block, axis, 1), shifted(block, axis, -1)
    far_low = shifted(before[:QUARTER], axis, 1)
    far_high = shifted(after[QUARTER:], axis, -1)
    return block, after, before, far_low, far_high


def far_kernel(low_ref, high_ref, early_ref, out_ref):
    encode(low_ref[...] + decode(high_ref), out_ref)


def add_kernel(low_ref, high_ref, out_ref):
    encode(low_ref[...] + decode(high_ref), out_ref)


def behind_kernel(far_ref, early_ref, out_ref):
    out_ref[...] = far_ref[...]


def high_kernel(mine, right, left, out_ref):
    rows = slice(QUARTER, HALF)
    encode(mine[rows, :] + decode(right, rows) + decode(left, rows), out_ref)


def ring_scatter(far_low, far_high, after, before, mine, axis, crossed, marker=None):
    got_right, got_left = shifted(after, axis, 1), shifted(before, axis, -1)
    far = crossed(far_high)
    coded = shape(QUARTER, CODED, dtype=jnp.int16)
    if axis == "z":
        far = call(
            far_kernel, coded, 0, 1 << 20, in_specs=[VMEM, VMEM, ANY], out_specs=VMEM
        )(far_low, far, marker)
    else:
        far = call(
            add_kernel, coded, 4 << 30, 1 << 20, in_specs=[VMEM] * 2, out_specs=VMEM
        )(far_low, far)
        far = call(
            behind_kernel, coded, 0, 1 << 20, in_specs=[VMEM, ANY], out_specs=VMEM
        )(far, got_left)
    high = call(high_kernel, coded, 0, 1 << 20, in_specs=[VMEM] * 3, out_specs=VMEM)(
        mine, got_right, got_left
    )
    return mine, got_right, got_left, shifted(far, axis, 2), crossed(high)


ORDER = ((2, 0), (2, 1), (1, 0), (1, 1), (3, 0), (3, 1), (0, 0), (0, 1))


def in_order(refs, out_ref):
    me, after, before, far_low, far_high = refs
    for place, (step, half) in enumerate(ORDER):
        ref = (me, after, far_high if half else far_low, before)[step]
        start = 0 if step == 2 else half * QUARTER
        out_ref[place * QUARTER : (place + 1) * QUARTER, :] = ref[start : start + QUARTER, :]


def images_kernel(me, after, before, far_low, far_high, out_ref):
    in_order((me, after, before, far_low, far_high), out_ref)
    lane = lax.broadcasted_iota(jnp.int32, (EXTRA, E), 1)
    carried = [ref[start:, :].astype(F32) for ref, start in (
        (me, HALF), (after, HALF), (far_high, QUARTER), (before, HALF)
    )]
    total = jnp.zeros((EXTRA, E), F32)
    for place, (step, half) in enumerate(ORDER):
        inside = (lane >= half * QUARTER) & (lane < (half + 1) * QUARTER)
        piece = jnp.where(inside, carried[step], 0.0)
        total += pltpu.roll(piece, (place - half) * QUARTER % E, 1)
    out_ref[TILE:, :] = total.astype(BF16)


def coefficients(where_ref, scale_ref, shift_ref, images_ref, texts_ref, coef_ref):
    _, _, z, xh, y, text_quarter = position(where_ref)
    parts = images_ref[TILE:, :TILE].astype(F32)
    partner = (parts[0:1] * 128.0 + parts[1:2]).astype(jnp.int32)
    scale, shift = jnp.exp(jnp.full((1, 1), scale_ref[0], F32)), shift_ref[0]
    row = lax.broadcasted_iota(jnp.int32, (TILE, 1), 0)
    index = row
    for place, (step, half) in enumerate(ORDER):
        block = (z * 2 + (1 - xh if half else xh)) * 4 + lax.rem(y + step, 4)
        start = block * ROWS + text_quarter * QUARTER
        index = jnp.where(row // QUARTER == place, row + (start - place * QUARTER), index)
    logits = scale * lax.dot_general(
        texts_ref[...], images_ref[:TILE, :], NT, preferred_element_type=F32
    ) + shift
    own = index == partner
    slopes = jnp.where(own, -scale, scale) / (1.0 + jnp.exp(jnp.where(own, logits, -logits)))
    coef_ref[...] = slopes.astype(BF16)


def image_terms(coef_ref, texts_ref, part):
    return lax.dot_general(
        coef_ref[:, part * ROWS : (part + 1) * ROWS], texts_ref[...], TN,
        preferred_element_type=F32,
    )


def share_out(got, outs):
    start = 0
    for out in outs:
        part = got[start : start + out.shape[0]]
        start += out.shape[0]
        if out.dtype == jnp.int16:
            encode(part, out)
        else:
            out[...] = part


def own_kernel(
    where_ref, scale_ref, shift_ref, me, after, before, far_low, far_high, images_ref, early_a, early_b,
    texts_ref, coef_ref,
):
    in_order((me, after, before, far_low, far_high), texts_ref)
    coefficients(where_ref, scale_ref, shift_ref, images_ref, texts_ref, coef_ref)


def given_kernel(where_ref, scale_ref, shift_ref, texts_ref, images_ref, coef_ref, given_ref):
    coefficients(where_ref, scale_ref, shift_ref, images_ref, texts_ref, coef_ref)
    for part in range(2):
        given_ref[part * ROWS : (part + 1) * ROWS, :] = image_terms(coef_ref, texts_ref, part)


def text_kernel(own_coef, images_ref, others_coef, others_ref, *outs):
    got = jnp.dot(own_coef[...], images_ref[:TILE, :], preferred_element_type=F32)
    got += jnp.dot(others_coef[...], others_ref[:TILE, :], preferred_element_type=F32)
    share_out(got, outs)


def kept_kernel(texts_ref, coef_ref, taken_ref, *outs):
    for part, some in enumerate((outs[:3], outs[3:])):
        rows = slice(part * ROWS, (part + 1) * ROWS)
        share_out(image_terms(coef_ref, texts_ref, part) + taken_ref[rows, :], some)


def back_kernel(
    where_ref, mine, right, left, far, got, emb, inverse, own_ref, core_ref, xl_ref, both_ref, held_ref
):
    rows = slice(0, QUARTER)
    gradients = mine[rows, :] + decode(right, rows) + decode(left, rows)
    gradients += decode(far) + decode(got)
    widened = emb[:QUARTER, :].astype(F32)
    inner_sum = jnp.sum(widened * gradients, axis=1, keepdims=True)
    value = (inverse[:, :1] * (gradients - widened * inner_sum)).astype(BF16)
    for i in range(4):
        held_ref[i] = value[:, i * SLICE : (i + 1) * SLICE]
    xl, core, _, _, _, _ = position(where_ref)
    own_ref[...] = held_ref[xl * 2 + core]
    core_ref[...] = held_ref[xl * 2 + 1 - core]
    xl_ref[...] = held_ref[2 - xl * 2 + core]
    both_ref[...] = held_ref[3 - xl * 2 - core]


def terms_kernel(images_ref, texts_ref, *refs):
    *backs, out_ref, both_ref = refs
    for i, ref in enumerate(backs):
        both_ref[i // 4, i % 4 * QUARTER : (i % 4 + 1) * QUARTER, :] = ref[...]
    rows = STEP * GROUP
    steps = 128 // STEP
    last = images_ref.shape[0] // rows - 1
    first = steps - texts_ref.shape[0] // rows
    for step in range(steps):
        terms = jnp.zeros((rows, SLICE), F32)
        if step <= last:
            terms += jnp.dot(
                images_ref[step * rows : (step + 1) * rows, :], both_ref[0],
                preferred_element_type=F32,
            )
        if step >= first:
            terms += jnp.dot(
                texts_ref[(step - first) * rows : (step - first + 1) * rows, :], both_ref[1],
                preferred_element_type=F32,
            )
        terms = terms.reshape(STEP, GROUP, SLICE)
        largest = jnp.max(jnp.max(jnp.abs(terms), axis=1), axis=1, keepdims=True)
        exponent = jnp.ceil(jnp.log(jnp.maximum(largest, 1e-30)) * (1.0 / OCTAVE) + 0.01)
        factor = 32767.0 * jnp.exp(exponent * -OCTAVE)
        row = lax.broadcasted_iota(jnp.int32, terms.shape, 1)
        coded = jnp.where(row == OWN, exponent[:, :, None], jnp.round(terms * factor[:, :, None]))
        out_ref[step * STEP : (step + 1) * STEP] = coded.astype(jnp.int32).astype(jnp.int16)


def total_kernel(coded_ref, out_ref):
    for part in range(4):
        total = jnp.zeros((GROUP, SLICE), F32)
        for i in range(32):
            terms = coded_ref[part * 32 + i].astype(jnp.int32).astype(F32)
            total += terms * (jnp.exp(terms[OWN : OWN + 1, :] * OCTAVE) * (1.0 / 32767.0))
        out_ref[:, part * SLICE : (part + 1) * SLICE] = total[:OWN]


def groups_kernel(where_ref, image_feats, text_feats, early, image_out, text_out, held_ref):
    def fill(feats_ref, out_ref, starts, start, first):
        depth = feats_ref.shape[1]
        for i, at in enumerate(starts):
            held_ref[i * QUARTER : (i + 1) * QUARTER, :depth] = feats_ref[at, :]
        for i in range(out_ref.shape[0] // (STEP * GROUP)):
            begin = (first + i) * STEP * OWN - start
            low = min(max(begin // 128 * 128, 0), depth - ROWS)
            row = lax.broadcasted_iota(jnp.int32, (STEP * GROUP, ROWS), 0)
            lane = lax.broadcasted_iota(jnp.int32, (STEP * GROUP, ROWS), 1)
            inside = lax.rem(row, GROUP)
            wanted = lax.div(row, GROUP) * OWN + inside + (begin - low)
            select = jnp.where((inside < OWN) & (wanted == lane), 1.0, 0.0).astype(BF16)
            out_ref[i * STEP * GROUP : (i + 1) * STEP * GROUP, :] = lax.dot_general(
                select, held_ref[:, low : low + ROWS], NT, preferred_element_type=F32
            ).astype(BF16)

    def quarters(places):
        return [pl.ds(pl.multiple_of(place * QUARTER, QUARTER), QUARTER) for place in places]

    width = image_feats.shape[1]
    xl, core, _, _, _, text_quarter = position(where_ref)
    half = text_quarter // 2
    fill(
        image_feats, image_out,
        quarters([c * 2 + x for x in (xl, 1 - xl) for c in (core, 1 - core)]), 0, 0,
    )
    fill(
        text_feats, text_out,
        quarters([h * 2 + c for h in (half, 1 - half) for c in (core, 1 - core)]),
        width, width // OWN // STEP,
    )


def body(image_feats, text_feats, image_weight, text_weight, partner, log_scale, logit_bias):
    where = lax.axis_index(AXES).astype(jnp.int32).reshape(1)
    depth = image_feats.shape[1]
    own_texts, text_inverse, load, image_inverse = call(
        embed_kernel,
        [
            shape(QUARTER, E, dtype=BF16), shape(QUARTER, 128),
            shape(HALF + EXTRA, E, dtype=BF16), shape(QUARTER, 128),
        ],
        2 * (QUARTER * E + HALF * depth) * E, 8 << 20, 60,
        in_specs=[SMEM, VMEM] + [ANY] * 4, out_specs=[VMEM] * 4,
        scratch_shapes=[
            pltpu.VMEM((QUARTER, E), BF16), pltpu.VMEM((HALF, depth), BF16),
            pltpu.VMEM((E, E), BF16), pltpu.VMEM((depth, E), BF16),
            pltpu.VMEM((QUARTER, E), F32), pltpu.VMEM((HALF, E), F32),
            pltpu.SemaphoreType.DMA((11,)),
        ],
    )(where, partner.reshape(3, 128), text_feats, image_feats, text_weight, image_weight)
    other_texts = lax.ppermute(own_texts, ("xl", "xh"), FLIP)
    pair = jnp.concatenate([own_texts, other_texts], 0)
    image_pieces, text_pieces = ring_gather(load, "z"), ring_gather(pair, "y")
    images = call(
        images_kernel, shape(TILE + EXTRA, E, dtype=BF16), 0, 4 << 20,
        in_specs=[VMEM] * 5, out_specs=VMEM,
    )(*image_pieces)
    others = lax.ppermute(images, "core", SWAP)

    last, first = (depth - 1) // OWN // STEP, depth // OWN // STEP
    image_groups, text_groups = call(
        groups_kernel,
        [
            shape((last + 1) * STEP * GROUP, ROWS, dtype=BF16),
            shape((128 // STEP - first) * STEP * GROUP, ROWS, dtype=BF16),
        ],
        2 * 17 * STEP * GROUP * ROWS * ROWS, 5 << 20,
        in_specs=[SMEM, VMEM, VMEM, ANY], out_specs=[VMEM] * 2,
        scratch_shapes=[pltpu.VMEM((ROWS, depth), BF16)],
    )(where, image_feats, text_feats, image_pieces[2])

    flops = 2 * TILE * TILE * E
    coef, texts = shape(TILE, TILE, dtype=BF16), shape(TILE, E, dtype=BF16)
    coded_quarter = shape(QUARTER, CODED, dtype=jnp.int16)
    coded_half = shape(HALF, CODED, dtype=jnp.int16)
    ways = [shape(QUARTER, E), coded_quarter, coded_half]
    rest = [coded_half, shape(HALF, E)]

    def run(kernel, outs, share, count, *options):
        return call(
            lambda *refs: kernel(*options, *refs), outs, int(share * flops), 6 << 20, 24,
            in_specs=[VMEM] * count, out_specs=[VMEM] * len(outs),
        )

    texts, own_coef = call(
        own_kernel, [texts, coef], 16 * flops, 6 << 20, 24,
        in_specs=[SMEM] * 3 + [VMEM] * 6 + [ANY] * 2, out_specs=[VMEM] * 2,
    )(where, log_scale, logit_bias, *text_pieces, images, image_groups, text_groups)
    others_coef, given = call(
        given_kernel, [coef, shape(TILE, E)], 2 * flops, 8 << 20, 24,
        in_specs=[SMEM] * 3 + [VMEM] * 2, out_specs=[VMEM] * 2,
    )(where, log_scale, logit_bias, texts, others)
    taken = lax.ppermute(given, "core", SWAP)
    sides = own_coef, images, others_coef, others
    text_parts = run(text_kernel, ways + rest, 2, 4)(*sides)
    text_ways, text_rest = text_parts[:3], text_parts[3:]
    image_parts = run(kept_kernel, ways + rest, 1, 3)(texts, own_coef, taken)
    image_ways, image_rest = image_parts[:3], image_parts[3:]
    text_sums = ring_scatter(
        *text_ways, *text_rest, "y", lambda a: lax.ppermute(a, ("xl", "xh"), FLIP)
    )
    image_sums = ring_scatter(
        *image_ways, *image_rest, "z", lambda a: lax.ppermute(a, "xl", SWAP), text_sums[1],
    )

    def tower_pieces(*inputs):
        own, other_core, other_xl, other_both = call(
            back_kernel, [shape(QUARTER, SLICE, dtype=BF16)] * 4, 0, 3 << 20,
            in_specs=[SMEM] + [VMEM] * 7, out_specs=[VMEM] * 4,
            scratch_shapes=[pltpu.VMEM((4, QUARTER, SLICE), BF16)],
        )(where, *inputs)
        return (
            own,
            lax.ppermute(other_core, "core", SWAP),
            lax.ppermute(other_xl, "xl", SWAP),
            lax.ppermute(other_both, TOWER, [(i, 3 - i) for i in range(4)]),
        )

    text_backs = tower_pieces(*text_sums, own_texts, text_inverse)
    image_backs = tower_pieces(*image_sums, load, image_inverse)

    coded = call(
        terms_kernel, shape(128, GROUP, SLICE, dtype=jnp.int16),
        4 * 128 * GROUP * ROWS * SLICE, 6 << 20, 24,
        in_specs=[VMEM] * 10, out_specs=VMEM,
        scratch_shapes=[pltpu.VMEM((2, ROWS, SLICE), BF16)],
    )(image_groups, text_groups, *image_backs, *text_backs)
    coded = lax.all_to_all(coded, AXES, split_axis=0, concat_axis=0, tiled=True)
    return call(total_kernel, shape(OWN, E), 0, 2 << 20, in_specs=[VMEM], out_specs=VMEM)(coded)


def solution(mesh):
    fine = Mesh(mesh.devices.reshape([SIZES[a] for a in AXES]), AXES)
    placed = (P(DP, None), P(DP, None), P(), P(), P(DP), P(), P())
    return jax.shard_map(
        body, mesh=fine, in_specs=placed, out_specs=P(TOWER + DP, None), check_vma=False
    )
```

```python
import math

import jax
import jax.numpy as jnp
from jax import lax
from jax.experimental import pallas as pl
from jax.experimental.pallas import tpu as pltpu
from jax.sharding import Mesh, PartitionSpec as P

AXES = ("xl", "core", "z", "xh", "y")
SIZES = {"xl": 2, "core": 2, "z": 4, "xh": 2, "y": 4}
DP = ("z", "xh", "y")
TOWER = ("xl", "core")
SWAP = [(0, 1), (1, 0)]
FLIP = [(0, 3), (1, 2), (2, 1), (3, 0)]
ROWS = 384
HALF, QUARTER = 192, 96
EXTRA = 16
E = 1024
TILE = 4 * HALF
OWN = 21
GROUP = 24
SLICE = E // 4
STEP = 8
NT = (((1,), (1,)), ((), ()))
TN = (((0,), (0,)), ((), ()))
OCTAVE = math.log(2.0) / 16.0
F32, BF16 = jnp.float32, jnp.bfloat16


def shifted(array, axis, by):
    return lax.ppermute(array, axis, [(i, (i + by) % 4) for i in range(4)])


def call(kernel, outs, flops, moved, limit=16, **options):
    return pl.pallas_call(
        kernel,
        out_shape=outs,
        cost_estimate=pl.CostEstimate(flops=flops, bytes_accessed=moved, transcendentals=0),
        compiler_params=pltpu.CompilerParams(vmem_limit_bytes=limit << 20),
        **options,
    )


def shape(*dims, dtype=F32):
    return jax.ShapeDtypeStruct(dims, dtype)


VMEM = pl.BlockSpec(memory_space=pltpu.VMEM)
SMEM = pl.BlockSpec(memory_space=pltpu.SMEM)
ANY = pl.BlockSpec(memory_space=pl.ANY)


def position(where_ref):
    index = where_ref[0]
    xl, core, z, xh, y = index // 64, index // 32 % 2, index // 8 % 4, index // 4 % 2, index % 4
    return xl, core, z, xh, y, (xl + xh) % 2 * 2 + core


def normalised(pre_ref, inverse_ref):
    pre = pre_ref[...]
    total = jnp.sum(pre * pre, axis=1, keepdims=True)
    inverse = lax.rsqrt(total + 1e-06).astype(BF16).astype(F32)
    inverse_ref[...] = jnp.broadcast_to(inverse[:QUARTER], (QUARTER, 128))
    return (pre * inverse).astype(BF16)


def embed_kernel(
    where_ref, partner_ref, text_feats, image_feats, text_weight, image_weight,
    text_ref, text_inverse, load_ref, image_inverse,
    text_rows, image_rows, text_held, image_held, text_pre, image_pre, sems,
):
    count = 0

    def begin(source, target):
        nonlocal count
        copy = pltpu.make_async_copy(source, target, sems.at[count])
        copy.start()
        count += 1
        return copy

    xl, core, _, _, _, text_quarter = position(where_ref)
    places = core * 2 + xl, core * 2 + 1 - xl

    def rows(place):
        return pl.ds(pl.multiple_of(place * QUARTER, QUARTER), QUARTER)

    def begin_weight(weight, held, ends):
        spans = [slice(a, b) for a, b in zip((0,) + ends, ends)]
        return [(span, begin(weight.at[span], held.at[span])) for span in spans]

    def project(rows_ref, held, waits, pre_ref):
        for i, (span, copy) in enumerate(waits):
            copy.wait()
            got = jnp.dot(rows_ref[:, span], held[span, :], preferred_element_type=F32)
            pre_ref[...] = got if i == 0 else pre_ref[...] + got

    text_copy = begin(text_feats.at[rows(text_quarter)], text_rows)
    text_waits = begin_weight(text_weight, text_held, (256, 512, 768, 1024))
    image_copies = [
        begin(image_feats.at[rows(place)], image_rows.at[i * QUARTER : (i + 1) * QUARTER])
        for i, place in enumerate(places)
    ]
    image_waits = begin_weight(image_weight, image_held, (384, 768, 1152, 1664))

    text_copy.wait()
    project(text_rows, text_held, text_waits, text_pre)
    text_ref[...] = normalised(text_pre, text_inverse)
    for copy in image_copies:
        copy.wait()
    project(image_rows, image_held, image_waits, image_pre)
    load_ref[:HALF, :] = normalised(image_pre, image_inverse)

    partner = jnp.concatenate([partner_ref[i : i + 1, :] for i in range(3)], 1).astype(F32)
    partner = jnp.broadcast_to(partner, (EXTRA, ROWS))
    lane = lax.broadcasted_iota(jnp.int32, (EXTRA, ROWS), 1)
    row = lax.broadcasted_iota(jnp.int32, (EXTRA, ROWS), 0)
    chosen = jnp.zeros((EXTRA, ROWS), F32)
    for i, place in enumerate(places):
        moved = pltpu.roll(partner, (i + 4 - place) % 4 * QUARTER, 1)
        chosen = jnp.where(lane // QUARTER == i, moved, chosen)
    high = jnp.floor(chosen * (1.0 / 128.0))
    parts = jnp.where(row == 0, high, jnp.where(row == 1, chosen - 128.0 * high, 0.0))
    load_ref[HALF:, :] = jnp.zeros((EXTRA, E), BF16)
    load_ref[HALF:, :ROWS] = parts.astype(BF16)


CODED = E + E // 4 + 128
TOP = 2.0**19 - 1.0


def encode(value, out_ref):
    largest = jnp.max(jnp.abs(value), axis=1, keepdims=True)
    exponent = jnp.ceil(jnp.log(jnp.maximum(largest, 1e-30)) * (1.0 / OCTAVE) + 0.01)
    whole = jnp.round(value * (TOP * jnp.exp(exponent * -OCTAVE))).astype(jnp.int32)
    out_ref[:, :E] = (whole >> 4).astype(jnp.int16)
    low = whole & 15
    packed = low[:, :SLICE]
    for i in range(1, 4):
        packed = packed | (low[:, i * SLICE : (i + 1) * SLICE] << (4 * i))
    out_ref[:, E : E + SLICE] = (packed - 32768).astype(jnp.int16)
    lanes = jnp.broadcast_to(exponent, (value.shape[0], 128))
    out_ref[:, E + SLICE :] = lanes.astype(jnp.int32).astype(jnp.int16)


def decode(ref, rows=slice(None)):
    exponent = ref[rows, E + SLICE : E + SLICE + 1].astype(jnp.int32).astype(F32)
    packed = ref[rows, E : E + SLICE].astype(jnp.int32) + 32768
    low = jnp.concatenate([(packed >> (4 * i)) & 15 for i in range(4)], 1)
    whole = (ref[rows, :E].astype(jnp.int32) << 4) + low
    return whole.astype(F32) * (jnp.exp(exponent * OCTAVE) * (1.0 / TOP))


def ring_gather(block, axis):
    before, after = shifted(block, axis, 1), shifted(block, axis, -1)
    far_low = shifted(before[:QUARTER], axis, 1)
    far_high = shifted(after[QUARTER:], axis, -1)
    return block, after, before, far_low, far_high


def far_kernel(low_ref, high_ref, early_ref, out_ref):
    encode(low_ref[...] + decode(high_ref), out_ref)


def add_kernel(low_ref, high_ref, out_ref):
    encode(low_ref[...] + decode(high_ref), out_ref)


def behind_kernel(far_ref, early_ref, out_ref):
    out_ref[...] = far_ref[...]


def high_kernel(mine, right, left, out_ref):
    rows = slice(QUARTER, HALF)
    encode(mine[rows, :] + decode(right, rows) + decode(left, rows), out_ref)


def ring_scatter(far_low, far_high, after, before, mine, axis, crossed, marker=None):
    got_right, got_left = shifted(after, axis, 1), shifted(before, axis, -1)
    far = crossed(far_high)
    coded = shape(QUARTER, CODED, dtype=jnp.int16)
    if axis == "z":
        far = call(
            far_kernel, coded, 0, 1 << 20, in_specs=[VMEM, VMEM, ANY], out_specs=VMEM
        )(far_low, far, marker)
    else:
        far = call(
            add_kernel, coded, 4 << 30, 1 << 20, in_specs=[VMEM] * 2, out_specs=VMEM
        )(far_low, far)
        far = call(
            behind_kernel, coded, 0, 1 << 20, in_specs=[VMEM, ANY], out_specs=VMEM
        )(far, got_left)
    high = call(high_kernel, coded, 0, 1 << 20, in_specs=[VMEM] * 3, out_specs=VMEM)(
        mine, got_right, got_left
    )
    return mine, got_right, got_left, shifted(far, axis, 2), crossed(high)


ORDER = ((2, 0), (2, 1), (1, 0), (1, 1), (3, 0), (3, 1), (0, 0), (0, 1))


def in_order(refs, out_ref):
    me, after, before, far_low, far_high = refs
    for place, (step, half) in enumerate(ORDER):
        ref = (me, after, far_high if half else far_low, before)[step]
        start = 0 if step == 2 else half * QUARTER
        out_ref[place * QUARTER : (place + 1) * QUARTER, :] = ref[start : start + QUARTER, :]


def images_kernel(me, after, before, far_low, far_high, out_ref):
    in_order((me, after, before, far_low, far_high), out_ref)
    lane = lax.broadcasted_iota(jnp.int32, (EXTRA, E), 1)
    carried = [ref[start:, :].astype(F32) for ref, start in (
        (me, HALF), (after, HALF), (far_high, QUARTER), (before, HALF)
    )]
    total = jnp.zeros((EXTRA, E), F32)
    for place, (step, half) in enumerate(ORDER):
        inside = (lane >= half * QUARTER) & (lane < (half + 1) * QUARTER)
        piece = jnp.where(inside, carried[step], 0.0)
        total += pltpu.roll(piece, (place - half) * QUARTER % E, 1)
    out_ref[TILE:, :] = total.astype(BF16)


def coefficients(where_ref, scale_ref, shift_ref, images_ref, texts_ref, coef_ref):
    _, _, z, xh, y, text_quarter = position(where_ref)
    parts = images_ref[TILE:, :TILE].astype(F32)
    partner = (parts[0:1] * 128.0 + parts[1:2]).astype(jnp.int32)
    scale, shift = jnp.exp(jnp.full((1, 1), scale_ref[0], F32)), shift_ref[0]
    row = lax.broadcasted_iota(jnp.int32, (TILE, 1), 0)
    index = row
    for place, (step, half) in enumerate(ORDER):
        block = (z * 2 + (1 - xh if half else xh)) * 4 + lax.rem(y + step, 4)
        start = block * ROWS + text_quarter * QUARTER
        index = jnp.where(row // QUARTER == place, row + (start - place * QUARTER), index)
    logits = scale * lax.dot_general(
        texts_ref[...], images_ref[:TILE, :], NT, preferred_element_type=F32
    ) + shift
    own = index == partner
    slopes = jnp.where(own, -scale, scale) / (1.0 + jnp.exp(jnp.where(own, logits, -logits)))
    coef_ref[...] = slopes.astype(BF16)


def image_terms(coef_ref, texts_ref, part):
    return lax.dot_general(
        coef_ref[:, part * ROWS : (part + 1) * ROWS], texts_ref[...], TN,
        preferred_element_type=F32,
    )


def share_out(got, outs):
    start = 0
    for out in outs:
        part = got[start : start + out.shape[0]]
        start += out.shape[0]
        if out.dtype == jnp.int16:
            encode(part, out)
        else:
            out[...] = part


def own_kernel(
    where_ref, scale_ref, shift_ref, me, after, before, far_low, far_high, images_ref, early_a, early_b,
    texts_ref, coef_ref,
):
    in_order((me, after, before, far_low, far_high), texts_ref)
    coefficients(where_ref, scale_ref, shift_ref, images_ref, texts_ref, coef_ref)


def given_kernel(where_ref, scale_ref, shift_ref, texts_ref, images_ref, coef_ref, given_ref):
    coefficients(where_ref, scale_ref, shift_ref, images_ref, texts_ref, coef_ref)
    for part in range(2):
        given_ref[part * ROWS : (part + 1) * ROWS, :] = image_terms(coef_ref, texts_ref, part)


def text_kernel(own_coef, images_ref, others_coef, others_ref, *outs):
    got = jnp.dot(own_coef[...], images_ref[:TILE, :], preferred_element_type=F32)
    got += jnp.dot(others_coef[...], others_ref[:TILE, :], preferred_element_type=F32)
    share_out(got, outs)


def kept_kernel(part, texts_ref, coef_ref, taken_ref, *outs):
    taken = taken_ref[part * ROWS : (part + 1) * ROWS, :]
    share_out(image_terms(coef_ref, texts_ref, part) + taken, outs)


def kept_rest_kernel(texts_ref, coef_ref, taken_ref, early_ref, *outs):
    kept_kernel(1, texts_ref, coef_ref, taken_ref, *outs)


def back_kernel(
    where_ref, mine, right, left, far, got, emb, inverse, own_ref, core_ref, xl_ref, both_ref, held_ref
):
    rows = slice(0, QUARTER)
    gradients = mine[rows, :] + decode(right, rows) + decode(left, rows)
    gradients += decode(far) + decode(got)
    widened = emb[:QUARTER, :].astype(F32)
    inner_sum = jnp.sum(widened * gradients, axis=1, keepdims=True)
    value = (inverse[:, :1] * (gradients - widened * inner_sum)).astype(BF16)
    for i in range(4):
        held_ref[i] = value[:, i * SLICE : (i + 1) * SLICE]
    xl, core, _, _, _, _ = position(where_ref)
    own_ref[...] = held_ref[xl * 2 + core]
    core_ref[...] = held_ref[xl * 2 + 1 - core]
    xl_ref[...] = held_ref[2 - xl * 2 + core]
    both_ref[...] = held_ref[3 - xl * 2 - core]


def terms_kernel(images_ref, texts_ref, *refs):
    *backs, out_ref, both_ref = refs
    for i, ref in enumerate(backs):
        both_ref[i // 4, i % 4 * QUARTER : (i % 4 + 1) * QUARTER, :] = ref[...]
    rows = STEP * GROUP
    steps = 128 // STEP
    last = images_ref.shape[0] // rows - 1
    first = steps - texts_ref.shape[0] // rows
    for step in range(steps):
        terms = jnp.zeros((rows, SLICE), F32)
        if step <= last:
            terms += jnp.dot(
                images_ref[step * rows : (step + 1) * rows, :], both_ref[0],
                preferred_element_type=F32,
            )
        if step >= first:
            terms += jnp.dot(
                texts_ref[(step - first) * rows : (step - first + 1) * rows, :], both_ref[1],
                preferred_element_type=F32,
            )
        terms = terms.reshape(STEP, GROUP, SLICE)
        largest = jnp.max(jnp.max(jnp.abs(terms), axis=1), axis=1, keepdims=True)
        exponent = jnp.ceil(jnp.log(jnp.maximum(largest, 1e-30)) * (1.0 / OCTAVE) + 0.01)
        factor = 32767.0 * jnp.exp(exponent * -OCTAVE)
        row = lax.broadcasted_iota(jnp.int32, terms.shape, 1)
        coded = jnp.where(row == OWN, exponent[:, :, None], jnp.round(terms * factor[:, :, None]))
        out_ref[step * STEP : (step + 1) * STEP] = coded.astype(jnp.int32).astype(jnp.int16)


def total_kernel(coded_ref, out_ref):
    for part in range(4):
        total = jnp.zeros((GROUP, SLICE), F32)
        for i in range(32):
            terms = coded_ref[part * 32 + i].astype(jnp.int32).astype(F32)
            total += terms * (jnp.exp(terms[OWN : OWN + 1, :] * OCTAVE) * (1.0 / 32767.0))
        out_ref[:, part * SLICE : (part + 1) * SLICE] = total[:OWN]


def groups_kernel(where_ref, image_feats, text_feats, early, image_out, text_out, held_ref):
    def fill(feats_ref, out_ref, starts, start, first):
        depth = feats_ref.shape[1]
        for i, at in enumerate(starts):
            held_ref[i * QUARTER : (i + 1) * QUARTER, :depth] = feats_ref[at, :]
        for i in range(out_ref.shape[0] // (STEP * GROUP)):
            begin = (first + i) * STEP * OWN - start
            low = min(max(begin // 128 * 128, 0), depth - ROWS)
            row = lax.broadcasted_iota(jnp.int32, (STEP * GROUP, ROWS), 0)
            lane = lax.broadcasted_iota(jnp.int32, (STEP * GROUP, ROWS), 1)
            inside = lax.rem(row, GROUP)
            wanted = lax.div(row, GROUP) * OWN + inside + (begin - low)
            select = jnp.where((inside < OWN) & (wanted == lane), 1.0, 0.0).astype(BF16)
            out_ref[i * STEP * GROUP : (i + 1) * STEP * GROUP, :] = lax.dot_general(
                select, held_ref[:, low : low + ROWS], NT, preferred_element_type=F32
            ).astype(BF16)

    def quarters(places):
        return [pl.ds(pl.multiple_of(place * QUARTER, QUARTER), QUARTER) for place in places]

    width = image_feats.shape[1]
    xl, core, _, _, _, text_quarter = position(where_ref)
    half = text_quarter // 2
    fill(
        image_feats, image_out,
        quarters([c * 2 + x for x in (xl, 1 - xl) for c in (core, 1 - core)]), 0, 0,
    )
    fill(
        text_feats, text_out,
        quarters([h * 2 + c for h in (half, 1 - half) for c in (core, 1 - core)]),
        width, width // OWN // STEP,
    )


def body(image_feats, text_feats, image_weight, text_weight, partner, log_scale, logit_bias):
    where = lax.axis_index(AXES).astype(jnp.int32).reshape(1)
    depth = image_feats.shape[1]
    own_texts, text_inverse, load, image_inverse = call(
        embed_kernel,
        [
            shape(QUARTER, E, dtype=BF16), shape(QUARTER, 128),
            shape(HALF + EXTRA, E, dtype=BF16), shape(QUARTER, 128),
        ],
        2 * (QUARTER * E + HALF * depth) * E, 8 << 20, 60,
        in_specs=[SMEM, VMEM] + [ANY] * 4, out_specs=[VMEM] * 4,
        scratch_shapes=[
            pltpu.VMEM((QUARTER, E), BF16), pltpu.VMEM((HALF, depth), BF16),
            pltpu.VMEM((E, E), BF16), pltpu.VMEM((depth, E), BF16),
            pltpu.VMEM((QUARTER, E), F32), pltpu.VMEM((HALF, E), F32),
            pltpu.SemaphoreType.DMA((11,)),
        ],
    )(where, partner.reshape(3, 128), text_feats, image_feats, text_weight, image_weight)
    other_texts = lax.ppermute(own_texts, ("xl", "xh"), FLIP)
    pair = jnp.concatenate([own_texts, other_texts], 0)
    image_pieces, text_pieces = ring_gather(load, "z"), ring_gather(pair, "y")
    images = call(
        images_kernel, shape(TILE + EXTRA, E, dtype=BF16), 0, 4 << 20,
        in_specs=[VMEM] * 5, out_specs=VMEM,
    )(*image_pieces)
    others = lax.ppermute(images, "core", SWAP)

    last, first = (depth - 1) // OWN // STEP, depth // OWN // STEP
    image_groups, text_groups = call(
        groups_kernel,
        [
            shape((last + 1) * STEP * GROUP, ROWS, dtype=BF16),
            shape((128 // STEP - first) * STEP * GROUP, ROWS, dtype=BF16),
        ],
        2 * 17 * STEP * GROUP * ROWS * ROWS, 5 << 20,
        in_specs=[SMEM, VMEM, VMEM, ANY], out_specs=[VMEM] * 2,
        scratch_shapes=[pltpu.VMEM((ROWS, depth), BF16)],
    )(where, image_feats, text_feats, image_pieces[2])

    flops = 2 * TILE * TILE * E
    coef, texts = shape(TILE, TILE, dtype=BF16), shape(TILE, E, dtype=BF16)
    coded_quarter = shape(QUARTER, CODED, dtype=jnp.int16)
    coded_half = shape(HALF, CODED, dtype=jnp.int16)
    ways = [shape(QUARTER, E), coded_quarter, coded_half]
    rest = [coded_half, shape(HALF, E)]

    def run(kernel, outs, share, count, *options):
        return call(
            lambda *refs: kernel(*options, *refs), outs, int(share * flops), 6 << 20, 24,
            in_specs=[VMEM] * count, out_specs=[VMEM] * len(outs),
        )

    texts, own_coef = call(
        own_kernel, [texts, coef], 16 * flops, 6 << 20, 24,
        in_specs=[SMEM] * 3 + [VMEM] * 6 + [ANY] * 2, out_specs=[VMEM] * 2,
    )(where, log_scale, logit_bias, *text_pieces, images, image_groups, text_groups)
    others_coef, given = call(
        given_kernel, [coef, shape(TILE, E)], 2 * flops, 8 << 20, 24,
        in_specs=[SMEM] * 3 + [VMEM] * 2, out_specs=[VMEM] * 2,
    )(where, log_scale, logit_bias, texts, others)
    taken = lax.ppermute(given, "core", SWAP)
    sides = own_coef, images, others_coef, others
    text_parts = run(text_kernel, ways + rest, 2, 4)(*sides)
    text_ways, text_rest = text_parts[:3], text_parts[3:]
    image_ways = run(kept_kernel, ways, 0.5, 3, 0)(texts, own_coef, taken)
    image_rest = call(
        kept_rest_kernel, rest, 4 * flops, 6 << 20, 24,
        in_specs=[VMEM] * 3 + [ANY], out_specs=[VMEM] * 2,
    )(texts, own_coef, taken, image_ways[0])
    text_sums = ring_scatter(
        *text_ways, *text_rest, "y", lambda a: lax.ppermute(a, ("xl", "xh"), FLIP)
    )
    image_sums = ring_scatter(
        *image_ways, *image_rest, "z", lambda a: lax.ppermute(a, "xl", SWAP), text_sums[1],
    )

    def tower_pieces(*inputs):
        own, other_core, other_xl, other_both = call(
            back_kernel, [shape(QUARTER, SLICE, dtype=BF16)] * 4, 0, 3 << 20,
            in_specs=[SMEM] + [VMEM] * 7, out_specs=[VMEM] * 4,
            scratch_shapes=[pltpu.VMEM((4, QUARTER, SLICE), BF16)],
        )(where, *inputs)
        return (
            own,
            lax.ppermute(other_core, "core", SWAP),
            lax.ppermute(other_xl, "xl", SWAP),
            lax.ppermute(other_both, TOWER, [(i, 3 - i) for i in range(4)]),
        )

    text_backs = tower_pieces(*text_sums, own_texts, text_inverse)
    image_backs = tower_pieces(*image_sums, load, image_inverse)

    coded = call(
        terms_kernel, shape(128, GROUP, SLICE, dtype=jnp.int16),
        4 * 128 * GROUP * ROWS * SLICE, 6 << 20, 24,
        in_specs=[VMEM] * 10, out_specs=VMEM,
        scratch_shapes=[pltpu.VMEM((2, ROWS, SLICE), BF16)],
    )(image_groups, text_groups, *image_backs, *text_backs)
    coded = lax.all_to_all(coded, AXES, split_axis=0, concat_axis=0, tiled=True)
    return call(total_kernel, shape(OWN, E), 0, 2 << 20, in_specs=[VMEM], out_specs=VMEM)(coded)


def solution(mesh):
    fine = Mesh(mesh.devices.reshape([SIZES[a] for a in AXES]), AXES)
    placed = (P(DP, None), P(DP, None), P(), P(), P(DP), P(), P())
    return jax.shard_map(
        body, mesh=fine, in_specs=placed, out_specs=P(TOWER + DP, None), check_vma=False
    )
```
